256 devices in a mesh: blocks: 64 (over z, y, core), group: 4 (over x).
Axes of the slice: x: 4, y: 4, z: 8, core: 2. Of those that a mesh axis runs over, the one named last changes fastest.
Arguments:
- populations: float32 [4, 27, 524288], P('group', None, 'blocks'), may hold values from 0.5 to 1.5
- solid_mask: int32 [4, 524288], P('group', 'blocks'), may hold values 0 or 1
- relax_rates: float32 [27], replicated, may hold values from 0.5 to 1.9
- coarse_pops: bfloat16 [4, 128, 3456], P('group', 'blocks'), may hold values from 0.5 to 1.5
- interface_pairs: int32 [4, 128], P('group'), may hold values from 0 to 127, as said below
Outputs:
- populations_next: float32 [4, 27, 524288], P('group', None, 'blocks')
- coarse_update: float32 [4, 128, 3456], P('group', 'blocks')
The draws below stay inside these ranges and needn't reach their ends.
Inputs may be any that keep to these rules, and one draw needn't show every extreme that they name: `interface_pairs`: each row q is a permutation of the fine columns. In each aligned block of 2 records (the records of one index of blocks), the owners (column // 2) are each named either 0 times or exactly 2 times.
All inputs are finite; a program needn't handle non-finite values. No bound on the sum of `solid_mask` on one device may be relied on, other than what follows from the above.
Results may differ from the reference program's by a relative error of at most 0.0015.
Values may be sent and summed in bfloat16 or wider, within the bound.
No kernel may reach another device: no remote copies, remote signals or barrier semaphores. Data moves between devices by JAX's collectives and lax.ppermute only.
A program may use at most 64 MiB of HBM per device.

```python
import jax
import jax.numpy as jnp
import numpy as np
from jax import lax

Q = 27
B = 16
QUAD = 4
COLS = 2
REC = 3456
NCOL = 128
NX = 2048
N_BLOCKS = 64


def draw_interface_pairs(key, part):
    key = jax.random.fold_in(key, 11)

    def one_position(subkey):
        cycle_key, shift_key, order_key, slot_key = jax.random.split(subkey, 4)
        cycle = jax.random.permutation(cycle_key, N_BLOCKS).astype(jnp.int32)
        position_of = jnp.argsort(cycle).astype(jnp.int32)
        pair_count = COLS // 2
        if pair_count <= N_BLOCKS:
            shifts = jax.random.permutation(shift_key, N_BLOCKS)[:pair_count].astype(jnp.int32)
        else:
            shifts = (jnp.arange(pair_count, dtype=jnp.int32) % N_BLOCKS).astype(jnp.int32)
        record_order = jax.vmap(lambda inner_key: jax.random.permutation(inner_key, COLS))(jax.random.split(order_key, N_BLOCKS)).astype(jnp.int32)
        pair_index = record_order // 2
        half_bit = record_order % 2
        devices = jnp.arange(N_BLOCKS, dtype=jnp.int32)[:, None]
        destination = cycle[(position_of[devices] + shifts[pair_index]) % N_BLOCKS]
        arrival = 2 * pair_index + half_bit
        slot_order = jax.vmap(lambda inner_key: jax.random.permutation(inner_key, COLS))(jax.random.split(slot_key, N_BLOCKS)).astype(jnp.int32)
        slot_ids = slot_order[destination, arrival]
        return (destination * COLS + slot_ids).reshape(-1).astype(jnp.int32)
    return jax.vmap(one_position)(jax.random.split(key, QUAD))


def plant(entries, stream_key, low, largest):
    dims = entries.shape
    index_at = [jax.random.randint(jax.random.fold_in(stream_key, axis), (), 0, dims[axis]) for axis in range(len(dims))]
    entries = entries.at[tuple(index_at)].set(low)
    longest = dims.index(max(dims))
    index_at[longest] = (index_at[longest] + 1) % dims[longest]
    return entries.at[tuple(index_at)].set(largest)


def shard_levels(stream_key, dims, cuts, low, high):
    factor_of, own = 1.0, jax.random.fold_in(stream_key, 6)
    for dim, shards_of in cuts:
        steps = jnp.exp(jax.random.uniform(jax.random.fold_in(own, dim), (shards_of,), jnp.float32, low / len(cuts), high / len(cuts)))
        factor_of = factor_of * jnp.repeat(steps, dims[dim] // shards_of).reshape([-1 if axis == dim else 1 for axis in range(len(dims))])
    return factor_of


def setup_inputs(seed: int = 0) -> dict:
    arg_keys = jax.random.split(jax.random.key(seed), 6)
    populations = jnp.clip(0.5 + 1.0 * jax.random.uniform(arg_keys[0], (QUAD, Q, NX * B * B), jnp.float32) ** shard_levels(arg_keys[0], (QUAD, Q, NX * B * B), ((0, 4), (2, 64)), -0.2, 0.2), 0.5, 1.5)
    solid_mask = plant((jax.random.randint(arg_keys[1], (QUAD, NX * B * B), 0, 8) < 1).astype(jnp.int32), jax.random.fold_in(arg_keys[1], 1), 0, 1)
    relax_rates = jnp.clip(jax.random.uniform(arg_keys[2], (Q,), jnp.float32, 0.5, 1.9), 0.5, 1.9)
    coarse_pops = jnp.clip(0.5 + 1.0 * jax.random.uniform(arg_keys[3], (QUAD, NCOL, REC), jnp.float32) ** shard_levels(arg_keys[3], (QUAD, NCOL, REC), ((0, 4), (1, 64)), -0.2, 0.2), 0.5, 1.5).astype(jnp.bfloat16)
    interface_pairs = draw_interface_pairs(jax.random.fold_in(arg_keys[5], 71), 0)
    return {"populations": populations, "solid_mask": solid_mask, "relax_rates": relax_rates, "coarse_pops": coarse_pops, "interface_pairs": interface_pairs}


VELOCITIES = np.array([[a - 1, b - 1, c - 1] for a in range(3) for b in range(3) for c in range(3)])
LINE_WEIGHTS = np.array([1.0 / 6.0, 2.0 / 3.0, 1.0 / 6.0])
WEIGHTS = np.array([LINE_WEIGHTS[a] * LINE_WEIGHTS[b] * LINE_WEIGHTS[c] for a in range(3) for b in range(3) for c in range(3)])
LINE_MOMENTS = np.array([[1.0, 1.0, 1.0], [-1.0, 0.0, 1.0], [1.0, 0.0, 1.0]])
LINE_INVERSE = np.array([[0.0, -0.5, 0.5], [1.0, 0.0, -1.0], [0.0, 0.5, 0.5]])
FORWARD = np.kron(np.kron(LINE_MOMENTS, LINE_MOMENTS), LINE_MOMENTS) * WEIGHTS[None, :]
BACKWARD = np.kron(np.kron(LINE_INVERSE, LINE_INVERSE), LINE_INVERSE) / WEIGHTS[:, None]
HIGHEST = lax.Precision.HIGHEST


def interp_table(block_edge):
    fine_cells = np.arange(block_edge)[:, None]
    coarse_cells = np.arange(block_edge // 2)[None, :]
    raw_weights = np.maximum(0.0, 1.0 - np.abs((fine_cells - 0.5) / 2.0 - coarse_cells))
    return raw_weights / raw_weights.sum(axis=1, keepdims=True)


def collide(current, solid_cells, relax_rates):
    weights = jnp.asarray(WEIGHTS, jnp.float32)
    velocity_table = jnp.asarray(VELOCITIES, jnp.float32)
    density = jnp.dot(weights[None, :], current, precision=HIGHEST)[0]
    momentum = jnp.dot((velocity_table * weights[:, None]).T, current, precision=HIGHEST)
    velocity = momentum / density[None, :]
    projected = jnp.dot(velocity_table, velocity, precision=HIGHEST)
    square = jnp.sum(velocity * velocity, axis=0)
    balance = density[None, :] * (1.0 + 3.0 * projected + 4.5 * projected * projected - 1.5 * square[None, :])
    moments = jnp.dot(jnp.asarray(FORWARD, jnp.float32), current - balance, precision=HIGHEST)
    collided = current - jnp.dot(jnp.asarray(BACKWARD, jnp.float32), relax_rates[:, None] * moments, precision=HIGHEST)
    return jnp.where(solid_cells[None, :] == 1, current[::-1], collided)


def reference(populations, solid_mask, relax_rates, coarse_pops, interface_pairs):
    half_edge = B // 2
    span = 2 * B
    field = populations.reshape(2, 2, Q, NX, B, B)
    solid_field = solid_mask.reshape(2, 2, NX, B, B)
    inverse = jax.vmap(lambda row_pairs: jnp.zeros((NCOL,), jnp.int32).at[row_pairs].set(jnp.arange(NCOL, dtype=jnp.int32)))(interface_pairs)
    interp = jnp.asarray(interp_table(B), jnp.float32)
    cross_index = np.arange(span)
    source_y = cross_index[None, :] - VELOCITIES[:, 1][:, None]
    source_z = cross_index[None, :] - VELOCITIES[:, 2][:, None]
    low_y = jnp.asarray(source_y < 0)[:, None, :, None]
    high_y = jnp.asarray(source_y > span - 1)[:, None, :, None]
    low_z = jnp.asarray(source_z < 0)[:, None, None, :]
    high_z = jnp.asarray(source_z > span - 1)[:, None, None, :]

    def one_column(column):
        x_index = (column * B - 1 + jnp.arange(B + 2, dtype=jnp.int32)) % NX
        window = jnp.take(field, x_index, axis=3).transpose(2, 3, 1, 4, 0, 5).reshape(Q, B + 2, span, span)
        solid_window = jnp.take(solid_field, x_index, axis=2).transpose(2, 1, 3, 0, 4).reshape(-1)
        collided = collide(window.reshape(Q, -1), solid_window, relax_rates).reshape(Q, B + 2, span, span)
        padded = jnp.pad(collided, ((0, 0), (0, 0), (1, 1), (1, 1)))
        pieces = []
        for index in range(Q):
            move_x = int(VELOCITIES[index, 0])
            move_y = int(VELOCITIES[index, 1])
            move_z = int(VELOCITIES[index, 2])
            pieces.append(padded[index, 1 - move_x:1 - move_x + B, 1 - move_y:1 - move_y + span, 1 - move_z:1 - move_z + span])
        passed = jnp.stack(pieces)
        column_records = coarse_pops[jnp.arange(4), inverse[:, column]].astype(jnp.float32).reshape(4, Q, 2, half_edge, half_edge)
        ghost_y = jnp.einsum("qiab,xa,zb->qixz", column_records[:, :, 0], interp, interp, precision=HIGHEST)
        ghost_z = jnp.einsum("qiab,xa,yb->qixy", column_records[:, :, 1], interp, interp, precision=HIGHEST)
        low_face_y = jnp.concatenate([ghost_y[0], ghost_y[2]], axis=2)
        high_face_y = jnp.concatenate([ghost_y[1], ghost_y[3]], axis=2)
        low_face_z = jnp.concatenate([ghost_z[0], ghost_z[1]], axis=2)
        high_face_z = jnp.concatenate([ghost_z[2], ghost_z[3]], axis=2)
        value_y = jnp.where(low_y, low_face_y[:, :, None, :], high_face_y[:, :, None, :])
        value_z = jnp.where(low_z, low_face_z[:, :, :, None], high_face_z[:, :, :, None])
        result = jnp.where(low_y | high_y, value_y, jnp.where(low_z | high_z, value_z, passed))
        faces = []
        for position in range(4):
            side_y = position % 2
            side_z = position // 2
            rows_y = slice(0, 2) if side_y == 0 else slice(span - 2, span)
            rows_z = slice(0, 2) if side_z == 0 else slice(span - 2, span)
            part_y = result[:, :, rows_y, side_z * B:(side_z + 1) * B].reshape(Q, half_edge, 2, 2, half_edge, 2).mean(axis=(2, 3, 5))
            part_z = result[:, :, side_y * B:(side_y + 1) * B, rows_z].reshape(Q, half_edge, 2, half_edge, 2, 2).mean(axis=(2, 4, 5))
            faces.append(jnp.stack([part_y, part_z], axis=1).reshape(-1))
        return result, jnp.stack(faces)

    results, restricted = lax.map(one_column, jnp.arange(NCOL, dtype=jnp.int32))
    populations_next = results.reshape(NCOL, Q, B, 2, B, 2, B).transpose(5, 3, 1, 0, 2, 4, 6).reshape(4, Q, NX * B * B)
    coarse_update = restricted[interface_pairs, jnp.arange(4, dtype=jnp.int32)[:, None]]
    return populations_next, coarse_update
```

```python
import jax
import jax.numpy as jnp
import numpy as np
from jax import lax
from jax.experimental import pallas as pl
from jax.experimental.pallas import tpu as pltpu
from jax.sharding import PartitionSpec as P

Q = 27
EDGE = 16
HALF = 8
NX = 32
LANES = 128
PITCH = 48
FIRST = 8
PLANE = 8
BLOCKS = PLANE * PLANE
ROWS = 64
PAIRS = [(i // 9, i // 3 % 3, i % 3) for i in range(Q)]
F32 = jnp.float32
BF16 = jnp.bfloat16


def interp_table():
    fine = np.arange(EDGE)[:, None]
    coarse = np.arange(HALF)[None, :]
    raw = np.maximum(0.0, 1.0 - np.abs((fine - 0.5) / 2.0 - coarse))
    return raw / raw.sum(axis=1, keepdims=True)


def side_tables():
    interp = interp_table()
    pair = interp[0::2] + interp[1::2]
    pools, ghosts, coarse, cell_masks, pop_masks = [], [], [], [], []
    for q in range(4):
        side_y, side_z = q % 2, q // 2
        out_y, out_z = 15 * side_y, 15 * side_z
        next_y = 1 if side_y == 0 else 14
        next_z = 1 if side_z == 0 else 14
        pool = np.zeros((16, 16, 2, 8, 8))
        for s in range(16):
            pool[out_y, s, 0, :, s // 2] = 0.125
            pool[next_y, s, 0, :, s // 2] = 0.125
            pool[s, out_z, 1, :, s // 2] = 0.125
            pool[s, next_z, 1, :, s // 2] = 0.125
        pools.append(pool.reshape(256, 128))
        ghost = np.zeros((2, 8, 8, 2, 16, 16))
        for s in range(16):
            ghost[0, :, :, 0, out_y, s] = interp[s][None, :]
            ghost[1, :, :, 1, s, out_z] = interp[s][None, :]
        ghost = ghost.reshape(128, 512)
        ghosts.append(np.concatenate([ghost, ghost], 0))
        part = np.zeros((2, 8, 8, 3, 2, 8, 8))
        pair_y, pair_z = out_y // 2, out_z // 2
        for a in range(8):
            for b in range(8):
                part[0, :, :, 0, 0, a, b] = np.outer(pair[a], pair[b])
                part[1, :, :, 1, 1, a, b] = np.outer(pair[a], pair[b])
            part[0, :, :, 0, 1, a, pair_y] = np.outer(pair[a], interp[out_z] + interp[next_z])
            part[1, :, :, 1, 0, a, pair_z] = np.outer(pair[a], interp[out_y] + interp[next_y])
            part[1, :, :, 2, 0, a, pair_z] = np.outer(pair[a], interp[out_y])
            part[1, :, :, 2, 1, a, pair_y] = np.outer(pair[a], interp[out_y])
        coarse.append(0.125 * part.reshape(128, 384))
        in_y, in_z = 2 * (1 - side_y), 2 * (1 - side_z)
        cells = np.zeros((2, 32, 16, 16))
        pops = np.zeros((2, 32, 128))
        for i, (a, b, c) in enumerate(PAIRS):
            if b == in_y:
                cells[0, i, out_y, :] = 1.0
                pops[0, i] = 1.0
            if c == in_z:
                cells[1, i, :, out_z] = 1.0
                pops[1, i] = 1.0
            if b == in_y:
                cells[1, i, out_y, :] = 0.0
        cell_masks.append(cells.reshape(64, 256))
        pop_masks.append(pops.reshape(64, 128))
    return (
        np.stack(pools),
        np.stack(ghosts),
        np.stack(coarse),
        np.stack(cell_masks),
        np.stack(pop_masks),
    )


def sides():
    position = lax.axis_index("group")
    return position % 2, position // 2


def lane_ids(rows=8):
    return lax.broadcasted_iota(jnp.int32, (rows, LANES), 1)


def rolled(value, shift):
    return pltpu.roll(value, shift, 1)


def split_bf16(value):
    high = value.astype(BF16)
    return high, (value - high.astype(F32)).astype(BF16)


def dot(left, right):
    return jnp.dot(left, right, preferred_element_type=F32)


def along(table, axis, line):
    out = {}
    for first in range(3):
        for second in range(3):
            keys = []
            for third in range(3):
                key = [first, second]
                key.insert(axis, third)
                keys.append(tuple(key))
            values = line(*[table[key] for key in keys])
            for key, value in zip(keys, values):
                out[key] = value
    return out


def line_moments(low, mid, high):
    both = low + high
    return both + 4.0 * mid, high - low, both


def line_inverse(zeroth, first, second):
    return second - first, zeroth - 0.5 * second, first + second


def collide_cells(current, rates):
    table = {PAIRS[i]: current[i] for i in range(Q)}
    moments = table
    for axis in range(3):
        moments = along(moments, axis, line_moments)
    density = moments[0, 0, 0]
    inverse = 1.0 / density
    flow = [moments[1, 0, 0], moments[0, 1, 0], moments[0, 0, 1]]
    speed = [part * inverse for part in flow]
    carried = [density * part for part in speed]
    square = [carried[axis] * speed[axis] for axis in range(3)]
    third = density * (1.0 / 3.0)
    relaxed = {}
    for index, key in enumerate(PAIRS):
        ones = [axis for axis in range(3) if key[axis] == 1]
        twos = [axis for axis in range(3) if key[axis] == 2]
        scale = (1.0 / 3.0) ** len(twos)
        if len(ones) == 0:
            if len(twos) == 0:
                balance = density
            elif len(twos) == 1:
                balance = third + square[twos[0]]
            elif len(twos) == 2:
                balance = (third + square[twos[0]] + square[twos[1]]) * (1.0 / 3.0)
            else:
                balance = (third + square[0] + square[1] + square[2]) * (1.0 / 9.0)
        elif len(ones) == 1:
            balance = carried[ones[0]] * scale if twos else carried[ones[0]]
        elif len(ones) == 2:
            balance = carried[ones[0]] * speed[ones[1]]
            balance = balance * scale if twos else balance
        else:
            balance = None
        rest = moments[key] if balance is None else moments[key] - balance
        relaxed[key] = rates[index] * rest
    change = relaxed
    for axis in range(3):
        change = along(change, axis, line_inverse)
    return [current[i] - change[PAIRS[i]] for i in range(Q)]


def collide_kernel(g_ref, solid_ref, rates_ref, w_ref, y_ref, z_ref, e_ref):
    side_y, side_z = sides()
    for group in range(4):
        count = min(8, Q - 8 * group)
        for x in range(NX):
            for h in range(2):
                start = 256 * x + LANES * h
                w_ref[h, pl.ds(8 * group * NX + x, count, stride=NX), :] = g_ref[
                    0, 8 * group : 8 * group + count, start : start + LANES
                ]
    rates = []
    for i in range(Q):
        scale = 1.0 / 216.0
        for part in PAIRS[i]:
            scale *= 1.5 if part == 0 else 3.0
        rates.append(rates_ref[i] * scale)

    for h in range(2):

        def chunk(index, carry, h=h):
            x = pl.multiple_of(8 * index, 8)
            current = [w_ref[h, pl.ds(NX * i + x, 8), :] for i in range(Q)]
            solid = solid_ref[pl.ds(2 * x + h, 8, stride=2), :] == 1
            collided = collide_cells(current, rates)
            for i in range(Q):
                w_ref[h, pl.ds(NX * i + x, 8), :] = jnp.where(
                    solid, current[Q - 1 - i], collided[i]
                )
            return carry

        lax.fori_loop(0, NX // 8, chunk, 0)

    send_y, send_z = 2 * (1 - side_y), 2 * (1 - side_z)
    base, inner = 112 * (1 - side_y), 15 * (1 - side_z)
    lanes = lane_ids(NX)
    tile = 1 - side_y

    def population(index, h):
        return w_ref[h, pl.ds(pl.multiple_of(index * NX, NX), NX), :]

    packed = [jnp.zeros((NX, LANES), F32), jnp.zeros((NX, LANES), F32)]
    for k in range(9):
        value = population(9 * (k // 3) + 3 * send_y + k % 3, tile)
        value = rolled(value, (16 * (k % 8) - base) & 127)
        packed[k // 8] = jnp.where(lanes >> 4 == k % 8, value, packed[k // 8])
    y_ref[0] = packed[0]
    y_ref[1] = packed[1]
    for h in range(2):
        packed_z = jnp.zeros((NX, LANES), F32)
        for k in range(9):
            value = population(9 * (k // 3) + 3 * (k % 3) + send_z, h)
            value = rolled(value, (k - inner) & 127)
            packed_z = jnp.where(lanes & 15 == k, value, packed_z)
        z_ref[h] = packed_z
    packed_e = jnp.zeros((NX, LANES), F32)
    for a in range(3):
        value = population(9 * a + 3 * send_y + send_z, tile)
        value = rolled(value, (a - base - inner) & 127)
        packed_e = jnp.where(lanes == a, value, packed_e)
    e_ref[...] = packed_e


def stream_kernel(
    q_ref, w_ref, y_ref, z_ref, e_ref, rec_ref, pool_ref, base_ref, right_ref, left_ref, pay_ref, t_ref
):
    del q_ref
    side_y, side_z = sides()
    lanes = lane_ids()
    cells_z = lanes & 15
    zeros = jnp.zeros((8, LANES), F32)
    for h in range(2):
        for i in range(Q):
            for row in (0, 8, 32, 40):
                t_ref[h, pl.ds(PITCH * i + row, 8), :] = zeros
        for row in range(PITCH * Q, PITCH * 32, 8):
            t_ref[h, pl.ds(row, 8), :] = zeros
    z_valid = [cells_z <= 14, None, cells_z >= 1]

    def shifted(first, second, b, shift):
        first, second = rolled(first, shift), rolled(second, shift)
        if b == 2:
            return jnp.where(lanes >= 16, first, 0.0), jnp.where(lanes < 16, first, second)
        if b == 0:
            return jnp.where(lanes >= 112, second, first), jnp.where(lanes < 112, second, 0.0)
        return first, second

    for i, (a, b, c) in enumerate(PAIRS):
        shift = (16 * (b - 1) + c - 1) % 128
        for x in range(0, NX, 8):
            both = [w_ref[h, pl.ds(NX * i + x, 8), :] for h in range(2)]
            if shift:
                both = shifted(both[0], both[1], b, shift)
            for h in range(2):
                value = both[h]
                if z_valid[c] is not None:
                    value = jnp.where(z_valid[c], value, 0.0)
                t_ref[h, pl.ds(PITCH * i + FIRST + x + a - 1, 8), :] = value

    halo_y, halo_z = 2 * side_y, 2 * side_z
    base, inner = 112 * (1 - side_y), 15 * (1 - side_z)
    tile = 1 - side_y

    def add(h, index, a, x, value):
        rows = pl.ds(PITCH * index + FIRST + x + a - 1, 8)
        t_ref[h, rows, :] = t_ref[h, rows, :] + value

    row_mask = lanes >> 4 == base >> 4
    column_mask = cells_z == inner
    for x in range(0, NX, 8):
        for k in range(9):
            a, c = k // 3, k % 3
            value = rolled(y_ref[k // 8, pl.ds(x, 8), :], (base - 16 * (k % 8) + c - 1) & 127)
            mask = row_mask if z_valid[c] is None else row_mask & z_valid[c]
            add(tile, 9 * a + 3 * halo_y + c, a, x, jnp.where(mask, value, 0.0))
        for k in range(9):
            a, b = k // 3, k % 3
            shift = (inner - k + 16 * (b - 1)) & 127
            both = shifted(z_ref[0, pl.ds(x, 8), :], z_ref[1, pl.ds(x, 8), :], b, shift)
            for h in range(2):
                add(h, 9 * a + 3 * b + halo_z, a, x, jnp.where(column_mask, both[h], 0.0))
        for a in range(3):
            value = rolled(e_ref[pl.ds(x, 8), :], (base + inner - a) & 127)
            value = jnp.where(lanes == base + inner, value, 0.0)
            add(tile, 9 * a + 3 * halo_y + halo_z, a, x, value)

    for group in range(4):
        count = min(8, Q - 8 * group)
        start = PITCH * 8 * group
        for h in range(2):
            for x in range(NX):
                base_ref[
                    8 * group : 8 * group + count, 256 * x + LANES * h : 256 * x + LANES * (h + 1)
                ] = t_ref[h, pl.ds(start + FIRST + x, count, stride=PITCH), :]
            right_ref[8 * group : 8 * group + 8, LANES * h : LANES * (h + 1)] = t_ref[
                h, pl.ds(start + FIRST + NX, 8, stride=PITCH), :
            ]
            left_ref[8 * group : 8 * group + 8, LANES * h : LANES * (h + 1)] = t_ref[
                h, pl.ds(start + FIRST - 1, 8, stride=PITCH), :
            ]

    sums = []
    for h in range(2):
        parts = []
        for i in range(Q):
            for s in range(2):
                row = PITCH * i + FIRST + EDGE * s
                parts.append(
                    t_ref[h, pl.ds(row, 8, stride=2), :] + t_ref[h, pl.ds(row + 1, 8, stride=2), :]
                )
        high, low = FIRST + NX, FIRST - 1
        parts.append(t_ref[h, pl.ds(PITCH * 18 + high, 8, stride=PITCH), :])
        last = t_ref[h, pl.ds(PITCH * 24 + high, 8, stride=PITCH), :]
        rows = lax.broadcasted_iota(jnp.int32, (8, LANES), 0)
        parts.append(jnp.where(rows == 2, last, 0.0))
        parts.append(t_ref[h, pl.ds(low, 8, stride=PITCH), :])
        parts.append(t_ref[h, pl.ds(PITCH * 8 + low, 8, stride=PITCH), :])
        sums.append(jnp.concatenate(parts, 0))
    total = len(parts) * 8
    pooled = jnp.zeros((total, LANES), F32)
    for h in range(2):
        for part in split_bf16(sums[h]):
            pooled = pooled + dot(part, pool_ref[0, LANES * h : LANES * (h + 1), :])
    row_a = lax.broadcasted_iota(jnp.int32, (total, LANES), 0) & 7
    lane_a = lax.broadcasted_iota(jnp.int32, (total, LANES), 1) >> 3 & 7
    pooled = jnp.where(row_a == lane_a, pooled, 0.0)
    target = lax.broadcasted_iota(jnp.int32, (ROWS, total), 0)
    block = lax.broadcasted_iota(jnp.int32, (ROWS, total), 1) >> 3
    column, index = target >> 5, target & 31
    wanted = jnp.where(
        index < Q, 2 * index + column, jnp.where(index < Q + 2, 2 * Q + 2 * column + index - Q, -1)
    )
    chosen = (wanted == block).astype(F32).astype(BF16)
    routed = jnp.zeros((ROWS, LANES), F32)
    for part in split_bf16(pooled):
        routed = routed + dot(chosen, part)
    records = rec_ref[...]
    for slot in range(PLANE):
        pay_ref[slot, 0:ROWS, :] = routed.astype(pay_ref.dtype)
        pay_ref[slot, ROWS : 2 * ROWS, :] = records.astype(pay_ref.dtype)


def owner_of(pairs_ref, device):
    return pairs_ref[2 * device] >> 1


def route_kernel(pairs_ref, inverse_ref, in_ref, out_ref):
    place = lax.axis_index("blocks") & (PLANE - 1)
    for plane in range(PLANE):
        device = PLANE * plane + place
        owner = owner_of(pairs_ref, device)
        source = owner & (PLANE - 1)
        before = (owner - 1) & (PLANE - 1)
        after = (owner + 1) & (PLANE - 1)
        holder = owner_of(inverse_ref, device) & (PLANE - 1)
        main = in_ref[source, 0:ROWS, :]
        rows = lax.broadcasted_iota(jnp.int32, (ROWS, LANES), 0)
        from_before = (rows == 27) | (rows == 28)
        from_after = (rows == 59) | (rows == 60)
        main = jnp.where(from_before, in_ref[before, 0:ROWS, :], main)
        main = jnp.where(from_after, in_ref[after, 0:ROWS, :], main)
        out_ref[plane, 0:ROWS, :] = main
        out_ref[plane, ROWS : 2 * ROWS, :] = in_ref[holder, ROWS : 2 * ROWS, :]


def finish_kernel(
    q_ref,
    pairs_ref,
    inverse_ref,
    base_ref,
    right_ref,
    left_ref,
    in_ref,
    rec_ref,
    line_ref,
    ghost_ref,
    coarse_ref,
    cell_ref,
    pop_ref,
    next_ref,
    update_ref,
):
    del q_ref
    me = lax.axis_index("blocks")
    owner = owner_of(pairs_ref, me)
    before = (owner + BLOCKS - 1) & (BLOCKS - 1)
    after = (owner + 1) & (BLOCKS - 1)
    holder = owner_of(inverse_ref, me)

    records = in_ref[holder >> 3, ROWS : 2 * ROWS, :].astype(F32)
    swap = (inverse_ref[2 * me] & 1) == 1
    first = jnp.where(swap, records[32:64], records[0:32])
    second = jnp.where(swap, records[0:32], records[32:64])
    columns = jnp.concatenate([first, second], 0)
    cell_y = cell_ref[0, 0:Q, :]
    cell_z = cell_ref[0, 32 : 32 + Q, :]
    for x in range(EDGE):
        scaled = columns * line_ref[x : x + 1, :]
        ghost = dot(jnp.concatenate(split_bf16(scaled), 1), ghost_ref[0])
        for s in range(2):
            place = EDGE * s + x
            rows = ghost[32 * s : 32 * s + Q]
            value = base_ref[:, 256 * place : 256 * (place + 1)]
            value = value + rows[:, 0:256] * cell_y + rows[:, 256:512] * cell_z
            if place == 0:
                value = value + right_ref[0:Q, :]
            if place == NX - 1:
                value = value + left_ref[0:Q, :]
            next_ref[0, :, 256 * place : 256 * (place + 1)] = value

    main = in_ref[owner >> 3, 0:ROWS, :].astype(F32)
    lower = in_ref[before >> 3, 16:32, :].astype(F32)
    upper = in_ref[after >> 3, 48:64, :].astype(F32)
    rows = lax.broadcasted_iota(jnp.int32, (32, LANES), 0)
    lane_a = lax.broadcasted_iota(jnp.int32, (32, LANES), 1) >> 3 & 7
    from_low = jnp.where(
        rows == 26, jnp.where(lane_a == 2, lower[12:13], 0.0), jnp.where(rows - 18 == lane_a, lower[11:12], 0.0)
    )
    from_high = jnp.where(
        rows == 8, jnp.where(lane_a == 0, upper[12:13], 0.0), jnp.where(rows == lane_a, upper[11:12], 0.0)
    )
    lane_in = lax.broadcasted_iota(jnp.int32, (LANES, LANES), 0)
    lane_out = lax.broadcasted_iota(jnp.int32, (LANES, LANES), 1)
    alike = ((lane_in >> 6 == lane_out >> 6) & (lane_in & 7 == lane_out & 7)).astype(F32).astype(BF16)
    edges = jnp.zeros((2 * 32, LANES), F32)
    for part in split_bf16(jnp.concatenate([from_low, from_high], 0)):
        edges = edges + dot(part, alike)
    column_0 = main[0:32] + jnp.where(lane_a == 0, edges[0:32], 0.0)
    column_1 = main[32:64] + jnp.where(lane_a == HALF - 1, edges[32:64], 0.0)
    own = dot(rec_ref[...].astype(BF16), coarse_ref[0])
    in_y, in_z = pop_ref[0, 0:32, :], pop_ref[0, 32:64, :]
    for t in range(2):
        share = own[32 * t : 32 * t + 32]
        value = jnp.where((pairs_ref[2 * me + t] & 1) == 1, column_1, column_0)
        value = (
            value
            + in_y * share[:, 0:128]
            + in_z * share[:, 128:256]
            - in_y * in_z * share[:, 256:384]
        )
        for i in range(Q):
            update_ref[0, t : t + 1, LANES * i : LANES * (i + 1)] = value[i : i + 1]


VMEM = pl.BlockSpec(memory_space=pltpu.VMEM)
SMEM = pl.BlockSpec(memory_space=pltpu.SMEM)


def whole(*shape):
    return pl.BlockSpec(shape, lambda i, *scalars: (0,) * len(shape))


def by_side(*shape):
    return pl.BlockSpec((1, *shape), lambda i, side, *rest: (side[0],) + (0,) * len(shape))


def params():
    return pltpu.CompilerParams(vmem_limit_bytes=48 * 1024 * 1024)


def swapped(block, bits):
    return lax.ppermute(block, "group", [(i, i ^ bits) for i in range(4)])


def body(populations, solid_mask, relax_rates, coarse_pops, interface_pairs):
    pools, ghosts, coarse, cell_masks, pop_masks = side_tables()
    position = lax.axis_index("group").astype(jnp.int32).reshape(1)
    pairs = interface_pairs[0]
    columns = jnp.arange(2 * BLOCKS, dtype=jnp.int32)
    inverse = jnp.sum(
        jnp.where(pairs[None, :] == columns[:, None], columns[None, :], 0), axis=1, dtype=jnp.int32
    )
    records = jnp.pad(
        coarse_pops.astype(F32).reshape(2, Q, LANES), ((0, 0), (0, 32 - Q), (0, 0))
    ).reshape(ROWS, LANES)

    shape = jax.ShapeDtypeStruct
    collided, edge_y, edge_z, edge_yz = pl.pallas_call(
        collide_kernel,
        out_shape=(
            shape((2, Q * NX, LANES), F32),
            shape((2, NX, LANES), F32),
            shape((2, NX, LANES), F32),
            shape((NX, LANES), F32),
        ),
        in_specs=[VMEM, VMEM, SMEM],
        out_specs=(VMEM,) * 4,
        compiler_params=params(),
        name="collide",
    )(populations, solid_mask.reshape(2 * NX, LANES), relax_rates)

    edge_y = swapped(edge_y, 1)
    edge_z = swapped(edge_z, 2)
    edge_yz = swapped(edge_yz, 3)

    base, right, left, payload = pl.pallas_call(
        stream_kernel,
        out_shape=(
            shape((Q, NX * 256), F32),
            shape((32, 256), F32),
            shape((32, 256), F32),
            shape((PLANE, 2 * ROWS, LANES), F32),
        ),
        grid_spec=pltpu.PrefetchScalarGridSpec(
            num_scalar_prefetch=1,
            grid=(1,),
            in_specs=[
                whole(2, Q * NX, LANES),
                whole(2, NX, LANES),
                whole(2, NX, LANES),
                whole(NX, LANES),
                whole(ROWS, LANES),
                by_side(256, 128),
            ],
            out_specs=(
                whole(Q, NX * 256),
                whole(32, 256),
                whole(32, 256),
                whole(PLANE, 2 * ROWS, LANES),
            ),
            scratch_shapes=[pltpu.VMEM((2, PITCH * 32, LANES), F32)],
        ),
        compiler_params=params(),
        name="stream",
    )(position, collided, edge_y, edge_z, edge_yz, records, jnp.asarray(pools, BF16))

    ring = [(i, (i + 1) % BLOCKS) for i in range(BLOCKS)]
    right = lax.ppermute(right, "blocks", ring)
    left = lax.ppermute(left, "blocks", [(b, a) for a, b in ring])

    near = [[PLANE * i + j for j in range(PLANE)] for i in range(PLANE)]
    far = [[PLANE * j + i for j in range(PLANE)] for i in range(PLANE)]
    payload = lax.all_to_all(payload, "blocks", 0, 0, axis_index_groups=near, tiled=True)
    payload = pl.pallas_call(
        route_kernel,
        out_shape=shape((PLANE, 2 * ROWS, LANES), F32),
        in_specs=[SMEM, SMEM, VMEM],
        out_specs=VMEM,
        compiler_params=params(),
        name="route",
    )(pairs, inverse, payload)
    payload = lax.all_to_all(payload, "blocks", 0, 0, axis_index_groups=far, tiled=True)

    lines = np.tile(np.repeat(interp_table(), HALF, axis=1), (1, 2))
    return pl.pallas_call(
        finish_kernel,
        out_shape=(shape((1, Q, NX * 256), F32), shape((1, 2, Q * LANES), F32)),
        grid_spec=pltpu.PrefetchScalarGridSpec(
            num_scalar_prefetch=3,
            grid=(1,),
            in_specs=[
                whole(Q, NX * 256),
                whole(32, 256),
                whole(32, 256),
                whole(PLANE, 2 * ROWS, LANES),
                whole(ROWS, LANES),
                whole(EDGE, LANES),
                by_side(256, 512),
                by_side(128, 384),
                by_side(64, 256),
                by_side(64, 128),
            ],
            out_specs=(whole(1, Q, NX * 256), whole(1, 2, Q * LANES)),
        ),
        compiler_params=params(),
        name="finish",
    )(
        position,
        pairs,
        inverse,
        base,
        right,
        left,
        payload,
        records,
        jnp.asarray(lines, F32),
        jnp.asarray(ghosts, BF16),
        jnp.asarray(coarse, BF16),
        jnp.asarray(cell_masks, F32),
        jnp.asarray(pop_masks, F32),
    )


def solution(mesh):
    placed = (
        P("group", None, "blocks"),
        P("group", "blocks"),
        P(),
        P("group", "blocks", None),
        P("group", None),
    )
    return jax.shard_map(
        body,
        mesh=mesh,
        in_specs=placed,
        out_specs=(P("group", None, "blocks"), P("group", "blocks", None)),
        check_vma=False,
    )
```

```python
import jax
import jax.numpy as jnp
import numpy as np
from jax import lax
from jax.experimental import pallas as pl
from jax.experimental.pallas import tpu as pltpu
from jax.sharding import PartitionSpec as P

Q = 27
EDGE = 16
HALF = 8
NX = 32
SPAN = 2 * NX
PITCH = SPAN + 16
FIRST = 8
LANES = 128
PLANE = 8
BLOCKS = PLANE * PLANE
LOW, HIGH, SHARED, CENTRE, RECORDS, ROWS = 54, 55, 56, 57, 58, 112
PAIRS = [(i // 9, i // 3 % 3, i % 3) for i in range(Q)]
F32 = jnp.float32
BF16 = jnp.bfloat16


def interp_table():
    fine = np.arange(EDGE)[:, None]
    coarse = np.arange(HALF)[None, :]
    raw = np.maximum(0.0, 1.0 - np.abs((fine - 0.5) / 2.0 - coarse))
    return raw / raw.sum(axis=1, keepdims=True)


def share_table(pool, in_y, in_z, out_y, out_z):
    layer = np.zeros((Q, 2, 8, 8))
    for i, (a, b, c) in enumerate(PAIRS):
        valid = np.ones((16, 16))
        if b == in_y:
            valid[out_y, :] = 0.0
        if c == in_z:
            valid[:, out_z] = 0.0
        layer[i] = (valid.reshape(256) @ pool).reshape(2, 8, 8)
    share = np.zeros((64, 2, 8, 8))
    for i, (a, b, c) in enumerate(PAIRS):
        for column in range(2):
            share[27 * column + i] = 2.0 * layer[i]
        if a == 2:
            share[i, :, 0, :] = layer[i, :, 0, :]
            row, at = (LOW, i - 18) if i < 26 else (SHARED, 7)
            share[row, :, at, :] = layer[i, :, 0, :]
        if a == 0:
            share[27 + i, :, 7, :] = layer[i, :, 0, :]
            row, at = (HIGH, i) if i < 8 else (SHARED, 0)
            share[row, :, at, :] = layer[i, :, 0, :]
    return share.reshape(64, 128)


def side_tables():
    interp = interp_table()
    pair = interp[0::2] + interp[1::2]
    pools, shares, ghosts, coarse, pop_masks = [], [], [], [], []
    for q in range(4):
        side_y, side_z = q % 2, q // 2
        out_y, out_z = 15 * side_y, 15 * side_z
        next_y = 1 if side_y == 0 else 14
        next_z = 1 if side_z == 0 else 14
        in_y, in_z = 2 * (1 - side_y), 2 * (1 - side_z)
        pool = np.zeros((16, 16, 2, 8, 8))
        for s in range(16):
            pool[out_y, s, 0, :, s // 2] = 0.125
            pool[next_y, s, 0, :, s // 2] = 0.125
            pool[s, out_z, 1, :, s // 2] = 0.125
            pool[s, next_z, 1, :, s // 2] = 0.125
        pool = pool.reshape(256, 128)
        pools.append(pool)
        shares.append(share_table(pool, in_y, in_z, out_y, out_z))
        ghost = np.zeros((2, 8, 8, 2, 16, 16))
        for s in range(16):
            ghost[0, :, :, 0, out_y, s] = interp[s][None, :]
            ghost[1, :, :, 1, s, out_z] = interp[s][None, :]
        ghost = ghost.reshape(128, 512)
        ghosts.append(np.concatenate([ghost, ghost], 0))
        part = np.zeros((2, 8, 8, 3, 2, 8, 8))
        pair_y, pair_z = out_y // 2, out_z // 2
        for a in range(8):
            for b in range(8):
                part[0, :, :, 0, 0, a, b] = np.outer(pair[a], pair[b])
                part[1, :, :, 1, 1, a, b] = np.outer(pair[a], pair[b])
            part[0, :, :, 0, 1, a, pair_y] = np.outer(pair[a], interp[out_z] + interp[next_z])
            part[1, :, :, 1, 0, a, pair_z] = np.outer(pair[a], interp[out_y] + interp[next_y])
            part[1, :, :, 2, 0, a, pair_z] = np.outer(pair[a], interp[out_y])
            part[1, :, :, 2, 1, a, pair_y] = np.outer(pair[a], interp[out_y])
        coarse.append(0.125 * part.reshape(128, 384))
        pops = np.zeros((2, 32, 128))
        for i, (a, b, c) in enumerate(PAIRS):
            pops[0, i] = float(b == in_y)
            pops[1, i] = float(c == in_z)
        pop_masks.append(pops.reshape(64, 128))
    return [np.stack(table) for table in (pools, shares, ghosts, coarse, pop_masks)]


def sides():
    position = lax.axis_index("group")
    return position & 1, position >> 1


def geometry():
    side_y, side_z = sides()
    return 1 - side_y, 112 * (1 - side_y), 15 * (1 - side_z)


def ids(shape, dim):
    return lax.broadcasted_iota(jnp.int32, shape, dim)


def rolled(value, shift):
    return pltpu.roll(value, shift, 1)


def split_bf16(value):
    high = value.astype(BF16)
    return high, (value - high.astype(F32)).astype(BF16)


def dot(left, right):
    return jnp.dot(left, right, preferred_element_type=F32)


def along(table, axis, line):
    out = {}
    for first in range(3):
        for second in range(3):
            keys = []
            for third in range(3):
                key = [first, second]
                key.insert(axis, third)
                keys.append(tuple(key))
            values = line(*[table[key] for key in keys])
            for key, value in zip(keys, values):
                out[key] = value
    return out


def line_moments(low, mid, high):
    both = low + high
    return both + 4.0 * mid, high - low, both


def line_inverse(zeroth, first, second):
    return second - first, zeroth - 0.5 * second, first + second


def collide_cells(current, rates):
    table = {PAIRS[i]: current[i] for i in range(Q)}
    moments = table
    for axis in range(3):
        moments = along(moments, axis, line_moments)
    density = moments[0, 0, 0]
    inverse = 1.0 / density
    flow = [moments[1, 0, 0], moments[0, 1, 0], moments[0, 0, 1]]
    speed = [part * inverse for part in flow]
    carried = [density * part for part in speed]
    square = [carried[axis] * speed[axis] for axis in range(3)]
    third = density * (1.0 / 3.0)
    relaxed = {}
    for index, key in enumerate(PAIRS):
        ones = [axis for axis in range(3) if key[axis] == 1]
        twos = [axis for axis in range(3) if key[axis] == 2]
        scale = (1.0 / 3.0) ** len(twos)
        if len(ones) == 0:
            if len(twos) == 0:
                balance = density
            elif len(twos) == 1:
                balance = third + square[twos[0]]
            elif len(twos) == 2:
                balance = (third + square[twos[0]] + square[twos[1]]) * (1.0 / 3.0)
            else:
                balance = (third + square[0] + square[1] + square[2]) * (1.0 / 9.0)
        elif len(ones) == 1:
            balance = carried[ones[0]] * scale if twos else carried[ones[0]]
        elif len(ones) == 2:
            balance = carried[ones[0]] * speed[ones[1]]
            balance = balance * scale if twos else balance
        else:
            balance = None
        rest = moments[key] if balance is None else moments[key] - balance
        relaxed[key] = rates[index] * rest
    change = relaxed
    for axis in range(3):
        change = along(change, axis, line_inverse)
    return [current[i] - change[PAIRS[i]] for i in range(Q)]


def collide_kernel(g_ref, solid_ref, rates_ref, w_ref, y_ref, z_ref):
    side_y, side_z = sides()
    rates = []
    for i in range(Q):
        scale = 1.0 / 216.0
        for part in PAIRS[i]:
            scale *= 1.5 if part == 0 else 3.0
        rates.append(rates_ref[i] * scale)

    def chunk(index, carry):
        row = pl.multiple_of(8 * index, 8)
        current = [g_ref[pl.ds(SPAN * i + row, 8), :] for i in range(Q)]
        solid = solid_ref[pl.ds(row, 8), :] == 1
        collided = collide_cells(current, rates)
        for i in range(Q):
            w_ref[pl.ds(SPAN * i + row, 8), :] = jnp.where(solid, current[Q - 1 - i], collided[i])
        return carry

    lax.fori_loop(0, SPAN // 8, chunk, 0)

    send_y, send_z = 2 * (1 - side_y), 2 * (1 - side_z)
    tile, base, inner = geometry()
    lanes = ids((NX, LANES), 1)
    packed = [jnp.zeros((NX, LANES), F32), jnp.zeros((NX, LANES), F32)]
    for k in range(9):
        index = 9 * (k // 3) + 3 * send_y + k % 3
        value = w_ref[pl.ds(index * SPAN + tile, NX, stride=2), :]
        value = rolled(value, (16 * (k % 8) - base) & 127)
        packed[k // 8] = jnp.where(lanes >> 4 == k % 8, value, packed[k // 8])
    y_ref[0] = packed[0]
    y_ref[1] = packed[1]
    lanes = ids((SPAN, LANES), 1)
    packed_z = jnp.zeros((SPAN, LANES), F32)
    for k in range(9):
        index = 9 * (k // 3) + 3 * (k % 3) + send_z
        value = w_ref[pl.ds(pl.multiple_of(index * SPAN, SPAN), SPAN), :]
        packed_z = jnp.where(lanes & 15 == k, rolled(value, (k - inner) & 127), packed_z)
    z_ref[...] = packed_z


def moved(value, b, shift):
    value = rolled(value, shift)
    if b == 1:
        return value
    rows, lanes = ids(value.shape, 0), ids(value.shape, 1)
    if b == 2:
        other = pltpu.roll(value, 1, 0)
        return jnp.where(lanes >= 16, value, jnp.where(rows & 1 == 1, other, 0.0))
    other = pltpu.roll(value, value.shape[0] - 1, 0)
    return jnp.where(lanes < 112, value, jnp.where(rows & 1 == 0, other, 0.0))


def z_inside(lanes, c):
    return lanes & 15 <= 14 if c == 0 else lanes & 15 >= 1


def stream_kernel(w_ref, t_ref, e_ref):
    lanes = ids((8, LANES), 1)
    zeros = jnp.zeros((8, LANES), F32)
    for i, (a, b, c) in enumerate(PAIRS):
        for row in (0, 8, SPAN, SPAN + 8):
            t_ref[pl.ds(PITCH * i + row, 8), :] = zeros
        shift = (16 * (b - 1) + c - 1) % 128
        for row in range(0, SPAN, 8):
            value = w_ref[pl.ds(SPAN * i + row, 8), :]
            if shift:
                value = moved(value, b, shift)
            if c != 1:
                value = jnp.where(z_inside(lanes, c), value, 0.0)
            t_ref[pl.ds(PITCH * i + FIRST + row + 2 * (a - 1), 8), :] = value

    side_y, side_z = sides()
    tile, base, inner = geometry()
    lanes = ids((NX, LANES), 1)
    packed = jnp.zeros((NX, LANES), F32)
    for a in range(3):
        index = 9 * a + 6 * (1 - side_y) + 2 * (1 - side_z)
        value = w_ref[pl.ds(index * SPAN + tile, NX, stride=2), :]
        packed = jnp.where(lanes == a, rolled(value, (a - base - inner) & 127), packed)
    e_ref[...] = packed


def halo_kernel(
    q_ref, t_ref, y_ref, z_ref, e_ref, rec_ref, pool_ref, share_ref,
    out_ref, right_ref, left_ref, pay_ref, edge_ref,
):
    del q_ref, t_ref
    side_y, side_z = sides()
    halo_y, halo_z = 2 * side_y, 2 * side_z
    tile, base, inner = geometry()
    edge_ref[...] = e_ref[...]

    lanes = ids((NX, LANES), 1)
    row_mask = lanes >> 4 == base >> 4
    for k in range(9):
        a, c = k // 3, k % 3
        value = rolled(y_ref[k // 8], (base - 16 * (k % 8) + c - 1) & 127)
        mask = row_mask if c == 1 else row_mask & z_inside(lanes, c)
        index = 9 * a + 3 * halo_y + c
        rows = pl.ds(PITCH * index + FIRST + 2 * (a - 1) + tile, NX, stride=2)
        out_ref[rows, :] = out_ref[rows, :] + jnp.where(mask, value, 0.0)
    lanes = ids((8, LANES), 1)
    for k in range(9):
        a, b = k // 3, k % 3
        shift = (inner - k + 16 * (b - 1)) & 127
        index = 9 * a + 3 * b + halo_z
        for row in range(0, SPAN, 8):
            value = moved(z_ref[pl.ds(row, 8), :], b, shift)
            rows = pl.ds(PITCH * index + FIRST + row + 2 * (a - 1), 8)
            out_ref[rows, :] = out_ref[rows, :] + jnp.where(lanes & 15 == inner, value, 0.0)

    for k in range(9):
        right_ref[8 * k : 8 * k + 8, :] = out_ref[pl.ds(PITCH * (18 + k) + FIRST + SPAN, 8), :]
        left_ref[8 * k : 8 * k + 8, :] = out_ref[pl.ds(PITCH * k, 8), :]

    row_8 = ids((8, LANES), 0)
    total = 8 * (2 * Q + 4)
    pooled = jnp.zeros((total, LANES), F32)
    for h in range(2):
        parts = []
        for i in range(Q):
            for s in range(2):
                row = PITCH * i + FIRST + NX * s + h
                parts.append(
                    out_ref[pl.ds(row, 8, stride=4), :] + out_ref[pl.ds(row + 2, 8, stride=4), :]
                )
        over, under = FIRST + SPAN + h, FIRST - 2 + h
        parts.append(out_ref[pl.ds(PITCH * 18 + over, 8, stride=PITCH), :])
        last = out_ref[pl.ds(PITCH * 19 + over, 8, stride=PITCH), :]
        parts.append(jnp.where(row_8 == 7, last, 0.0))
        parts.append(out_ref[pl.ds(under, 8, stride=PITCH), :])
        parts.append(out_ref[pl.ds(PITCH * 8 + under, 8, stride=PITCH), :])
        for part in split_bf16(jnp.concatenate(parts, 0)):
            pooled = pooled + dot(part, pool_ref[0, LANES * h : LANES * (h + 1), :])
    pooled = jnp.where(ids((total, LANES), 0) & 7 == ids((total, LANES), 1) >> 3 & 7, pooled, 0.0)
    target, block = ids((64, total), 0), ids((64, total), 1) >> 3
    second = (target >= Q).astype(jnp.int32)
    wanted = jnp.where(target < LOW, 2 * (target - Q * second) + second, -1)
    wanted = jnp.where(target == LOW, 54, jnp.where(target == HIGH, 56, wanted))
    chosen = (wanted == block) | ((target == SHARED) & ((block == 55) | (block == 57)))
    chosen = chosen.astype(F32).astype(BF16)
    routed = jnp.zeros((64, LANES), F32)
    for part in split_bf16(pooled):
        routed = routed + dot(chosen, part)

    share = share_ref[0]
    rows, lane_a = ids((64, LANES), 0), ids((64, LANES), 1) >> 3 & 7
    inside = rows < LOW
    held = jnp.sum(jnp.where(inside, routed, 0.0), axis=0, keepdims=True)
    held = jnp.sum(held, axis=1, keepdims=True)
    parts = jnp.sum(jnp.where(inside, share, 0.0), axis=0, keepdims=True)
    parts = jnp.sum(parts, axis=1, keepdims=True)
    centre = (held / parts).astype(BF16).astype(F32)
    routed = routed - centre * share
    is_centre = (rows == CENTRE) | ((rows == SHARED) & ((lane_a == 1) | (lane_a == 6)))
    routed = jnp.where(is_centre, centre, routed)
    payload = jnp.concatenate([routed[0:RECORDS], rec_ref[...]], 0).astype(BF16)
    for slot in range(PLANE):
        pay_ref[slot] = payload


def owner_of(pairs_ref, device):
    return pairs_ref[2 * device] >> 1


def route_kernel(
    pairs_ref, inverse_ref, in_ref, e_ref, right_in, left_in, out_ref, right_ref, left_ref
):
    place = lax.axis_index("blocks") & (PLANE - 1)
    rows, lane_a = ids((16, LANES), 0) + 48, ids((16, LANES), 1) >> 3 & 7
    from_low = (rows == LOW) | ((rows == SHARED) & (lane_a >= 4))
    from_high = (rows == HIGH) | ((rows == SHARED) & (lane_a < 4))
    for plane in range(PLANE):
        device = PLANE * plane + place
        owner = owner_of(pairs_ref, device)
        source = owner & (PLANE - 1)
        before = (owner - 1) & (PLANE - 1)
        after = (owner + 1) & (PLANE - 1)
        holder = owner_of(inverse_ref, device) & (PLANE - 1)
        out_ref[plane, 0:48] = in_ref[source, 0:48]
        mixed = in_ref[source, 48:64].astype(F32)
        mixed = jnp.where(rows >= RECORDS, in_ref[holder, 48:64].astype(F32), mixed)
        mixed = jnp.where(from_low, in_ref[before, 48:64].astype(F32), mixed)
        mixed = jnp.where(from_high, in_ref[after, 48:64].astype(F32), mixed)
        out_ref[plane, 48:64] = mixed.astype(BF16)
        out_ref[plane, 64:ROWS] = in_ref[holder, 64:ROWS]

    side_y, side_z = sides()
    tile, base, inner = geometry()
    right_ref[...] = right_in[...]
    left_ref[...] = left_in[...]
    corner = 8 * (6 * side_y + 2 * side_z)
    lanes = ids((1, LANES), 1)
    for ref, layer, a, row in ((right_ref, NX - 1, 2, 0), (left_ref, 0, 0, 6)):
        value = rolled(e_ref[layer : layer + 1, :], (base + inner - a) & 127)
        at = pl.ds(corner + row + tile, 1)
        ref[at, :] = ref[at, :] + jnp.where(lanes == base + inner, value, 0.0)


def finish_kernel(
    q_ref, pairs_ref, inverse_ref,
    t_ref, e_ref, right_ref, left_ref, in_ref, rec_ref, line_ref, share_ref, ghost_ref, coarse_ref, pop_ref,
    next_ref, update_ref,
    p_ref,
):
    del q_ref
    me = lax.axis_index("blocks")
    owner = owner_of(pairs_ref, me)
    before = (owner + BLOCKS - 1) & (BLOCKS - 1)
    after = (owner + 1) & (BLOCKS - 1)
    holder = owner_of(inverse_ref, me)
    side_y, side_z = sides()
    tile, base, inner = geometry()

    records = in_ref[holder >> 3].astype(F32)[RECORDS:ROWS]
    swap = (inverse_ref[2 * me] & 1) == 1
    p_ref[0:Q] = jnp.where(swap, records[Q:], records[:Q])
    p_ref[32 : 32 + Q] = jnp.where(swap, records[:Q], records[Q:])
    lines = line_ref[...]
    lanes = ids((NX, LANES), 1)
    for a in range(3):
        for b in range(3):
            scaled = []
            for c in range(3):
                i = 9 * a + 3 * b + c
                for s in range(2):
                    scaled.append(lines * p_ref[32 * s + i : 32 * s + i + 1, :])
            scaled = jnp.concatenate(scaled, 0)
            ghost = dot(jnp.concatenate(split_bf16(scaled), 1), ghost_ref[0])
            in_y = b == 2 * (1 - side_y)
            for c in range(3):
                i = 9 * a + 3 * b + c
                in_z = c == 2 * (1 - side_z)
                for h in range(2):
                    rows_y = ghost[NX * c : NX * (c + 1), LANES * h : LANES * (h + 1)]
                    rows_z = ghost[NX * c : NX * (c + 1), 256 + LANES * h : 256 + LANES * (h + 1)]
                    value = t_ref[pl.ds(PITCH * i + FIRST + h, NX, stride=2), :]
                    if c != 1:
                        value = value + jnp.where(in_z, rows_z, 0.0)
                    if b != 1:
                        outer = (lanes >> 4 == 7 * side_y) & (h == side_y) & in_y
                        value = jnp.where(outer, rows_y, value)
                    next_ref[pl.ds(SPAN * i + h, NX, stride=2), :] = value
    for k in range(9):
        rows = pl.ds(SPAN * (18 + k), 8)
        next_ref[rows, :] = next_ref[rows, :] + right_ref[8 * k : 8 * k + 8, :]
        rows = pl.ds(SPAN * k + SPAN - 8, 8)
        next_ref[rows, :] = next_ref[rows, :] + left_ref[8 * k : 8 * k + 8, :]
    for a in range(3):
        index = 9 * a + 6 * side_y + 2 * side_z
        low, high = (0, NX - (a - 1)) if a >= 1 else (1, NX)
        value = rolled(e_ref[low:high, :], (base + inner - a) & 127)
        value = jnp.where(lanes[low:high] == base + inner, value, 0.0)
        rows = pl.ds(SPAN * index + 2 * (low + a - 1) + tile, high - low, stride=2)
        next_ref[rows, :] = next_ref[rows, :] + value

    main = in_ref[owner >> 3].astype(F32)
    lower = in_ref[before >> 3, 48:64].astype(F32)
    upper = in_ref[after >> 3, 48:64].astype(F32)
    share = share_ref[0]
    main = main[0:LOW] + main[CENTRE : CENTRE + 1] * share[0:LOW]
    shared = SHARED - 48
    lane_1 = ids((1, LANES), 1)
    low_centre = jnp.sum(jnp.where(lane_1 == 48, lower[shared : shared + 1], 0.0), axis=1, keepdims=True)
    high_centre = jnp.sum(jnp.where(lane_1 == 8, upper[shared : shared + 1], 0.0), axis=1, keepdims=True)
    lower = lower + low_centre * share[48:64]
    upper = upper + high_centre * share[48:64]
    rows, lane_a = ids((32, LANES), 0), ids((32, LANES), 1) >> 3 & 7
    from_low = jnp.where(
        rows == 26,
        jnp.where(lane_a == 7, lower[shared : shared + 1], 0.0),
        jnp.where(rows - 18 == lane_a, lower[LOW - 48 : LOW - 47], 0.0),
    )
    from_high = jnp.where(
        rows == 8,
        jnp.where(lane_a == 0, upper[shared : shared + 1], 0.0),
        jnp.where(rows == lane_a, upper[HIGH - 48 : HIGH - 47], 0.0),
    )
    lane_in, lane_out = ids((LANES, LANES), 0), ids((LANES, LANES), 1)
    alike = (lane_in >> 6 == lane_out >> 6) & (lane_in & 7 == lane_out & 7)
    alike = alike.astype(F32).astype(BF16)
    edges = jnp.zeros((2 * 32, LANES), F32)
    for part in split_bf16(jnp.concatenate([from_low, from_high], 0)):
        edges = edges + dot(part, alike)
    column_0 = main[0:Q] + jnp.where(lane_a == 0, edges[0:32], 0.0)[0:Q]
    column_1 = main[Q : 2 * Q] + jnp.where(lane_a == HALF - 1, edges[32:64], 0.0)[0:Q]
    own = dot(rec_ref[...].astype(BF16), coarse_ref[0])
    in_y, in_z = pop_ref[0, 0:Q, :], pop_ref[0, 32 : 32 + Q, :]
    for t in range(2):
        part = own[Q * t : Q * t + Q]
        value = jnp.where((pairs_ref[2 * me + t] & 1) == 1, column_1, column_0)
        value = value + in_y * part[:, 0:128] + in_z * part[:, 128:256] - in_y * in_z * part[:, 256:384]
        for i in range(Q):
            update_ref[0, t : t + 1, LANES * i : LANES * (i + 1)] = value[i : i + 1]


VMEM = pl.BlockSpec(memory_space=pltpu.VMEM)
SMEM = pl.BlockSpec(memory_space=pltpu.SMEM)


def whole(*shape):
    return pl.BlockSpec(shape, lambda i, *scalars: (0,) * len(shape))


def by_side(*shape):
    return pl.BlockSpec((1, *shape), lambda i, side, *rest: (side[0],) + (0,) * len(shape))


def params():
    return pltpu.CompilerParams(vmem_limit_bytes=32 * 1024 * 1024)


def cost(flops, moved_bytes):
    return pl.CostEstimate(flops=flops, bytes_accessed=moved_bytes, transcendentals=0)


def swapped(block, bits):
    return lax.ppermute(block, "group", [(i, i ^ bits) for i in range(4)])


def body(populations, solid_mask, relax_rates, coarse_pops, interface_pairs):
    pools, shares, ghosts, coarse, pop_masks = side_tables()
    position = lax.axis_index("group").astype(jnp.int32).reshape(1)
    pairs = interface_pairs[0]
    columns = jnp.arange(2 * BLOCKS, dtype=jnp.int32)
    inverse = jnp.sum(
        jnp.where(pairs[None, :] == columns[:, None], columns[None, :], 0), axis=1, dtype=jnp.int32
    )
    records = coarse_pops.reshape(2 * Q, LANES).astype(F32)
    shares = jnp.asarray(shares, F32)

    shape = jax.ShapeDtypeStruct
    collided, edge_y, edge_z = pl.pallas_call(
        collide_kernel,
        out_shape=(
            shape((Q * SPAN, LANES), F32),
            shape((2, NX, LANES), F32),
            shape((SPAN, LANES), F32),
        ),
        in_specs=[VMEM, VMEM, SMEM],
        out_specs=(VMEM,) * 3,
        compiler_params=params(),
        name="collide",
    )(populations.reshape(Q * SPAN, LANES), solid_mask.reshape(SPAN, LANES), relax_rates)

    edge_y = swapped(edge_y, 1)
    edge_z = swapped(edge_z, 2)
    streamed, edge_yz = pl.pallas_call(
        stream_kernel,
        out_shape=(shape((Q * PITCH, LANES), F32), shape((NX, LANES), F32)),
        in_specs=[VMEM],
        out_specs=(VMEM,) * 2,
        compiler_params=params(),
        cost_estimate=cost(10_000_000, 8_000_000),
        name="stream",
    )(collided)

    streamed, right, left, payload, edge_yz = pl.pallas_call(
        halo_kernel,
        out_shape=(
            shape((Q * PITCH, LANES), F32),
            shape((72, LANES), F32),
            shape((72, LANES), F32),
            shape((PLANE, ROWS, LANES), BF16),
            shape((NX, LANES), F32),
        ),
        grid_spec=pltpu.PrefetchScalarGridSpec(
            num_scalar_prefetch=1,
            grid=(1,),
            in_specs=[VMEM, VMEM, VMEM, VMEM, VMEM, by_side(256, 128), by_side(64, 128)],
            out_specs=(VMEM,) * 5,
        ),
        input_output_aliases={1: 0},
        compiler_params=params(),
        name="halo",
    )(position, streamed, edge_y, edge_z, edge_yz, records, jnp.asarray(pools, BF16), shares)
    edge_yz = swapped(edge_yz, 3)

    near = [[PLANE * i + j for j in range(PLANE)] for i in range(PLANE)]
    far = [[PLANE * j + i for j in range(PLANE)] for i in range(PLANE)]
    payload = lax.all_to_all(payload, "blocks", 0, 0, axis_index_groups=near, tiled=True)
    payload, right, left = pl.pallas_call(
        route_kernel,
        out_shape=(
            shape((PLANE, ROWS, LANES), BF16),
            shape((72, LANES), F32),
            shape((72, LANES), F32),
        ),
        in_specs=[SMEM, SMEM, VMEM, VMEM, VMEM, VMEM],
        out_specs=(VMEM,) * 3,
        compiler_params=params(),
        name="route",
    )(pairs, inverse, payload, edge_yz, right, left)
    payload = lax.all_to_all(payload, "blocks", 0, 0, axis_index_groups=far, tiled=True)
    ring = [(i, (i + 1) % BLOCKS) for i in range(BLOCKS)]
    right = lax.ppermute(right, "blocks", ring)
    left = lax.ppermute(left, "blocks", [(b, a) for a, b in ring])

    lines = np.tile(np.repeat(interp_table(), HALF, axis=1), (1, 2))
    result, update = pl.pallas_call(
        finish_kernel,
        out_shape=(shape((Q * SPAN, LANES), F32), shape((1, 2, Q * LANES), F32)),
        grid_spec=pltpu.PrefetchScalarGridSpec(
            num_scalar_prefetch=3,
            grid=(1,),
            in_specs=[
                VMEM, VMEM, VMEM, VMEM, VMEM, VMEM, VMEM,
                by_side(64, 128), by_side(256, 512), by_side(128, 384), by_side(64, 128),
            ],
            out_specs=(VMEM,) * 2,
            scratch_shapes=[pltpu.VMEM((64, LANES), F32)],
        ),
        compiler_params=params(),
        name="finish",
    )(
        position, pairs, inverse,
        streamed, edge_yz, right, left, payload, records,
        jnp.asarray(lines, F32), shares, jnp.asarray(ghosts, BF16), jnp.asarray(coarse, BF16), jnp.asarray(pop_masks, F32),
    )
    return result.reshape(1, Q, SPAN * LANES), update


def solution(mesh):
    placed = (
        P("group", None, "blocks"),
        P("group", "blocks"),
        P(),
        P("group", "blocks", None),
        P("group", None),
    )
    return jax.shard_map(
        body,
        mesh=mesh,
        in_specs=placed,
        out_specs=(P("group", None, "blocks"), P("group", "blocks", None)),
        check_vma=False,
    )
```

```python
import jax
import jax.numpy as jnp
from jax import lax
from jax.experimental import pallas as pl
from jax.experimental.pallas import tpu as pltpu
from jax.sharding import PartitionSpec as P

Q = 27
EDGE = 16
HALF = 8
NX = 32
SPAN = 2 * NX
PITCH = SPAN + 16
FIRST = 8
LANES = 128
PLANE = 8
BLOCKS = PLANE * PLANE
LOW, HIGH, SHARED, CENTRE, RECORDS, ROWS = 54, 55, 56, 57, 62, 80
MIXED = 48
PAIRS = [(i // 9, i // 3 % 3, i % 3) for i in range(Q)]
F32 = jnp.float32
BF16 = jnp.bfloat16


def sides():
    position = lax.axis_index("group")
    return position & 1, position >> 1


def geometry():
    side_y, side_z = sides()
    return 1 - side_y, 112 * (1 - side_y), 15 * (1 - side_z)


def ids(shape, dim):
    return lax.broadcasted_iota(jnp.int32, shape, dim)


def rolled(value, shift):
    return pltpu.roll(value, shift, 1)


def split_bf16(value):
    high = value.astype(BF16)
    return high, (value - high.astype(F32)).astype(BF16)


def dot(left, right):
    return jnp.dot(left, right, preferred_element_type=F32)


def record_ids(shape, dim):
    value = ids(shape, dim) & 127
    return value >> 6, value >> 3 & 7, value & 7


def digits(index):
    third, ninth = index * 11 >> 5, index * 57 >> 9
    return ninth, third - 3 * ninth, index - 3 * third


def interp(fine, coarse):
    weight = 1.0 - jnp.abs(0.5 * fine.astype(F32) - 0.25 - coarse.astype(F32))
    end = (fine == 0) | (fine == EDGE - 1)
    return jnp.where(weight > 0.0, jnp.where(end, 1.0, weight), 0.0)


def pool_table():
    side_y, side_z = sides()
    shape = (256, LANES)
    cell = ids(shape, 0)
    pair_y, pair_z = cell >> 5, cell >> 1 & 7
    face, a, b = record_ids(shape, 1)
    on_y = (pair_y == 7 * side_y) & (pair_z == b)
    on_z = (pair_z == 7 * side_z) & (pair_y == b)
    return jnp.where(((face == 0) & on_y) | ((face == 1) & on_z), 0.125, 0.0).astype(BF16)


def share_table():
    side_y, side_z = sides()
    shape = (64, LANES)
    row = ids(shape, 0)
    face, a, b = record_ids(shape, 1)
    column = (row >= Q).astype(jnp.int32)
    index = jnp.where(row < LOW, row - Q * column, jnp.where(row == LOW, 18 + a, a))
    index = jnp.where(row == SHARED, jnp.where(a == 7, 26, 8), index)
    by_x, by_y, by_z = digits(index)
    in_y, in_z = by_y == 2 * (1 - side_y), by_z == 2 * (1 - side_z)
    half_y = in_y & ((face == 0) | (b == 7 * side_y))
    half_z = in_z & ((face == 1) | (b == 7 * side_z))
    low = (by_x == 2) & (column == 0) & (a == 0)
    high = (by_x == 0) & (column == 1) & (a == HALF - 1)
    half_x = (row >= LOW) | low | high
    share = jnp.where(half_y, 0.5, 1.0) * jnp.where(half_z, 0.5, 1.0) * jnp.where(half_x, 0.5, 1.0)
    held = (row <= HIGH) | ((row == SHARED) & ((a == 0) | (a == 7)))
    return jnp.where(held, share, 0.0)


def ghost_table():
    side_y, side_z = sides()
    shape = (LANES, LANES)
    face, a, b = record_ids(shape, 0)
    lanes = ids(shape, 1)
    y, z = lanes >> 4, lanes & 15
    parts = [jnp.where((face == 0) & (y == 7 * side_y), interp(z, b), 0.0)]
    for h in range(2):
        parts.append(jnp.where((face == 1) & (z == 15 * side_z), interp(y + HALF * h, b), 0.0))
    return jnp.concatenate(parts, 1).astype(BF16)


def part_table():
    side_y, side_z = sides()
    shape = (LANES, LANES)
    face, a, b = record_ids(shape, 0)
    to_face, to_a, to_b = record_ids(shape, 1)
    along_x = 0.125 * (interp(2 * to_a, a) + interp(2 * to_a + 1, a))
    across = along_x * (interp(2 * to_b, b) + interp(2 * to_b + 1, b))
    zero = jnp.zeros(shape, jnp.int32)
    out_y, out_z = zero + 15 * side_y, zero + 15 * side_z
    next_y, next_z = zero + 1 + 13 * side_y, zero + 1 + 13 * side_z
    edge_y, edge_z = to_b == 7 * side_y, to_b == 7 * side_z
    line_y = along_x * interp(out_y, b)
    both_y = line_y + along_x * interp(next_y, b)
    both_z = along_x * (interp(out_z, b) + interp(next_z, b))
    in_y = jnp.where(to_face == 0, across, jnp.where(edge_y, both_z, 0.0))
    in_z = jnp.where(to_face == 1, across, jnp.where(edge_z, both_y, 0.0))
    ends = ((to_face == 0) & edge_z) | ((to_face == 1) & edge_y)
    shared = jnp.where(ends, line_y, 0.0)
    parts = [jnp.where(face == 0, in_y, 0.0), jnp.where(face == 1, in_z, 0.0), jnp.where(face == 1, shared, 0.0)]
    return jnp.concatenate(parts, 1).astype(BF16)


def along(table, axis, line):
    out = {}
    for first in range(3):
        for second in range(3):
            keys = []
            for third in range(3):
                key = [first, second]
                key.insert(axis, third)
                keys.append(tuple(key))
            values = line(*[table[key] for key in keys])
            for key, value in zip(keys, values):
                out[key] = value
    return out


def line_moments(low, mid, high):
    both = low + high
    return both + 4.0 * mid, high - low, both


def line_inverse(zeroth, first, second):
    return second - first, zeroth - 0.5 * second, first + second


def collide_cells(current, rates):
    table = {PAIRS[i]: current[i] for i in range(Q)}
    moments = table
    for axis in range(3):
        moments = along(moments, axis, line_moments)
    density = moments[0, 0, 0]
    inverse = 1.0 / density
    flow = [moments[1, 0, 0], moments[0, 1, 0], moments[0, 0, 1]]
    speed = [part * inverse for part in flow]
    carried = [density * part for part in speed]
    square = [carried[axis] * speed[axis] for axis in range(3)]
    third = density * (1.0 / 3.0)
    relaxed = {}
    for index, key in enumerate(PAIRS):
        ones = [axis for axis in range(3) if key[axis] == 1]
        twos = [axis for axis in range(3) if key[axis] == 2]
        scale = (1.0 / 3.0) ** len(twos)
        if len(ones) == 0:
            if len(twos) == 0:
                balance = density
            elif len(twos) == 1:
                balance = third + square[twos[0]]
            elif len(twos) == 2:
                balance = (third + square[twos[0]] + square[twos[1]]) * (1.0 / 3.0)
            else:
                balance = (third + square[0] + square[1] + square[2]) * (1.0 / 9.0)
        elif len(ones) == 1:
            balance = carried[ones[0]] * scale if twos else carried[ones[0]]
        elif len(ones) == 2:
            balance = carried[ones[0]] * speed[ones[1]]
            balance = balance * scale if twos else balance
        else:
            balance = None
        rest = moments[key] if balance is None else moments[key] - balance
        relaxed[key] = rates[index] * rest
    change = relaxed
    for axis in range(3):
        change = along(change, axis, line_inverse)
    return [current[i] - change[PAIRS[i]] for i in range(Q)]


def collide_kernel(
    g_hbm, solid_hbm, rates_hbm, w_hbm, y_ref, z_ref, g_ref, w_ref, solid_ref, rates_ref, sems
):
    pieces = 4
    size = SPAN // pieces
    copies = [
        pltpu.make_async_copy(rates_hbm, rates_ref, sems.at[pieces]),
        pltpu.make_async_copy(solid_hbm, solid_ref, sems.at[pieces + 1]),
    ]
    for piece in range(pieces):
        rows = pl.ds(size * piece, size)
        copies.append(
            pltpu.make_async_copy(g_hbm.at[:, rows, :], g_ref.at[:, rows, :], sems.at[piece])
        )
    for copy in copies:
        copy.start()
    side_y, side_z = sides()
    copies[0].wait()
    rates = []
    for i in range(Q):
        scale = 1.0 / 216.0
        for part in PAIRS[i]:
            scale *= 1.5 if part == 0 else 3.0
        rates.append(rates_ref[i] * scale)
    copies[1].wait()

    def chunk(index, carry):
        row = pl.multiple_of(8 * index, 8)
        current = [g_ref[i, pl.ds(row, 8), :] for i in range(Q)]
        solid = solid_ref[pl.ds(row, 8), :] == 1
        collided = collide_cells(current, rates)
        for i in range(Q):
            w_ref[i, pl.ds(row, 8), :] = jnp.where(solid, current[Q - 1 - i], collided[i])
        return carry

    for piece in range(pieces):
        copies[2 + piece].wait()
        lax.fori_loop(size // 8 * piece, size // 8 * (piece + 1), chunk, 0)
        rows = pl.ds(size * piece, size)
        copy = pltpu.make_async_copy(
            w_ref.at[:, rows, :], w_hbm.at[:, rows, :], sems.at[pieces + 2 + piece]
        )
        copy.start()
        copies.append(copy)

    send_y, send_z = 2 * (1 - side_y), 2 * (1 - side_z)
    tile, base, inner = geometry()
    lanes = ids((NX, LANES), 1)
    packed = [jnp.zeros((NX, LANES), F32), jnp.zeros((NX, LANES), F32)]
    for k in range(9):
        index = 9 * (k // 3) + 3 * send_y + k % 3
        value = w_ref[index, pl.ds(tile, NX, stride=2), :]
        value = rolled(value, (16 * (k % 8) - base) & 127)
        packed[k // 8] = jnp.where(lanes >> 4 == k % 8, value, packed[k // 8])
    y_ref[0] = packed[0]
    y_ref[1] = packed[1]
    lanes = ids((SPAN, LANES), 1)
    packed_z = jnp.zeros((SPAN, LANES), F32)
    for k in range(9):
        index = 9 * (k // 3) + 3 * (k % 3) + send_z
        value = w_ref[index]
        packed_z = jnp.where(lanes & 15 == k, rolled(value, (k - inner) & 127), packed_z)
    z_ref[...] = packed_z
    for copy in copies[2 + pieces :]:
        copy.wait()


def moved(value, b, shift):
    value = rolled(value, shift)
    if b == 1:
        return value
    rows, lanes = ids(value.shape, 0), ids(value.shape, 1)
    if b == 2:
        other = pltpu.roll(value, 1, 0)
        return jnp.where(lanes >= 16, value, jnp.where(rows & 1 == 1, other, 0.0))
    other = pltpu.roll(value, value.shape[0] - 1, 0)
    return jnp.where(lanes < 112, value, jnp.where(rows & 1 == 0, other, 0.0))


def z_inside(lanes, c):
    return lanes & 15 <= 14 if c == 0 else lanes & 15 >= 1


def stream_kernel(w_ref, coarse_ref, t_ref, e_ref, pool_ref, share_ref, rec_ref, p_ref):
    lanes = ids((8, LANES), 1)
    zeros = jnp.zeros((8, LANES), F32)
    for i, (a, b, c) in enumerate(PAIRS):
        for row in (0, 8, SPAN, SPAN + 8):
            t_ref[pl.ds(PITCH * i + row, 8), :] = zeros
        shift = (16 * (b - 1) + c - 1) % 128
        for row in range(0, SPAN, 8):
            value = w_ref[i, pl.ds(row, 8), :]
            if shift:
                value = moved(value, b, shift)
            if c != 1:
                value = jnp.where(z_inside(lanes, c), value, 0.0)
            t_ref[pl.ds(PITCH * i + FIRST + row + 2 * (a - 1), 8), :] = value

    side_y, side_z = sides()
    tile, base, inner = geometry()
    lanes = ids((NX, LANES), 1)
    packed = jnp.zeros((NX, LANES), F32)
    for a in range(3):
        index = 9 * a + 6 * (1 - side_y) + 2 * (1 - side_z)
        value = w_ref[index, pl.ds(tile, NX, stride=2), :]
        packed = jnp.where(lanes == a, rolled(value, (a - base - inner) & 127), packed)
    e_ref[...] = packed

    p_ref[...] = jnp.zeros((64, LANES), F32)
    records = coarse_ref[0].astype(F32)
    for t in range(2):
        for i in range(Q):
            p_ref[32 * t + i : 32 * t + i + 1, :] = records[t : t + 1, LANES * i : LANES * (i + 1)]
    in_y, in_z = 2 * (1 - side_y), 2 * (1 - side_z)
    first = ids((1, LANES), 1) < 64
    rec_ref[...] = jnp.zeros((32, LANES), F32)
    for t in range(2):
        for k in range(9):
            for_y = p_ref[pl.ds(32 * t + 9 * (k // 3) + 3 * in_y + k % 3, 1), :]
            for_z = p_ref[pl.ds(32 * t + 9 * (k // 3) + 3 * (k % 3) + in_z, 1), :]
            row = RECORDS - MIXED + 9 * t + k
            rec_ref[row : row + 1, :] = jnp.where(first, for_y, for_z)

    pool_ref[...] = pool_table()
    share_ref[...] = share_table()


def halo_kernel(
    t_ref, y_ref, z_ref, e_ref, rec_ref, pool_ref, share_ref, p_ref,
    out_ref, right_ref, left_ref, pay_ref, edge_ref, kept_ref,
):
    del t_ref
    kept_ref[...] = p_ref[...]
    side_y, side_z = sides()
    halo_y, halo_z = 2 * side_y, 2 * side_z
    tile, base, inner = geometry()
    edge_ref[...] = e_ref[...]

    lanes = ids((NX, LANES), 1)
    row_mask = lanes >> 4 == base >> 4
    for k in range(9):
        a, c = k // 3, k % 3
        value = rolled(y_ref[k // 8], (base - 16 * (k % 8) + c - 1) & 127)
        mask = row_mask if c == 1 else row_mask & z_inside(lanes, c)
        index = 9 * a + 3 * halo_y + c
        rows = pl.ds(PITCH * index + FIRST + 2 * (a - 1) + tile, NX, stride=2)
        out_ref[rows, :] = out_ref[rows, :] + jnp.where(mask, value, 0.0)
    lanes = ids((8, LANES), 1)
    for k in range(9):
        a, b = k // 3, k % 3
        shift = (inner - k + 16 * (b - 1)) & 127
        index = 9 * a + 3 * b + halo_z
        for row in range(0, SPAN, 8):
            value = moved(z_ref[pl.ds(row, 8), :], b, shift)
            rows = pl.ds(PITCH * index + FIRST + row + 2 * (a - 1), 8)
            out_ref[rows, :] = out_ref[rows, :] + jnp.where(lanes & 15 == inner, value, 0.0)

    for k in range(9):
        right_ref[8 * k : 8 * k + 8, :] = out_ref[pl.ds(PITCH * (18 + k) + FIRST + SPAN, 8), :]
        left_ref[8 * k : 8 * k + 8, :] = out_ref[pl.ds(PITCH * k, 8), :]

    row_8 = ids((8, LANES), 0)
    total = 8 * (2 * Q + 4)
    pooled = jnp.zeros((total, LANES), F32)
    for h in range(2):
        parts = []
        for i in range(Q):
            for s in range(2):
                row = PITCH * i + FIRST + NX * s + h
                parts.append(
                    out_ref[pl.ds(row, 8, stride=4), :] + out_ref[pl.ds(row + 2, 8, stride=4), :]
                )
        over, under = FIRST + SPAN + h, FIRST - 2 + h
        parts.append(out_ref[pl.ds(PITCH * 18 + over, 8, stride=PITCH), :])
        last = out_ref[pl.ds(PITCH * 19 + over, 8, stride=PITCH), :]
        parts.append(jnp.where(row_8 == 7, last, 0.0))
        parts.append(out_ref[pl.ds(under, 8, stride=PITCH), :])
        parts.append(out_ref[pl.ds(PITCH * 8 + under, 8, stride=PITCH), :])
        for part in split_bf16(jnp.concatenate(parts, 0)):
            pooled = pooled + dot(part, pool_ref[LANES * h : LANES * (h + 1), :])
    pooled = jnp.where(ids((total, LANES), 0) & 7 == ids((total, LANES), 1) >> 3 & 7, pooled, 0.0)
    target, block = ids((64, total), 0), ids((64, total), 1) >> 3
    second = (target >= Q).astype(jnp.int32)
    wanted = jnp.where(target < LOW, 2 * (target - Q * second) + second, -1)
    wanted = jnp.where(target == LOW, 54, jnp.where(target == HIGH, 56, wanted))
    chosen = (wanted == block) | ((target == SHARED) & ((block == 55) | (block == 57)))
    chosen = chosen.astype(F32).astype(BF16)
    routed = jnp.zeros((64, LANES), F32)
    for part in split_bf16(pooled):
        routed = routed + dot(chosen, part)

    share = share_ref[...]
    rows, lane_a = ids((64, LANES), 0), ids((64, LANES), 1) >> 3 & 7
    inside = rows < LOW
    held = jnp.sum(jnp.where(inside, routed, 0.0), axis=0, keepdims=True)
    held = jnp.sum(held, axis=1, keepdims=True)
    parts = jnp.sum(jnp.where(inside, share, 0.0), axis=0, keepdims=True)
    parts = jnp.sum(parts, axis=1, keepdims=True)
    centre = (held / parts).astype(BF16).astype(F32)
    routed = routed - centre * share
    is_centre = (rows == CENTRE) | ((rows == SHARED) & ((lane_a == 1) | (lane_a == 6)))
    routed = jnp.where(is_centre, centre, routed)
    payload = jnp.where(rows[MIXED:64] >= RECORDS, rec_ref[0:16], routed[MIXED:64])
    payload = jnp.concatenate([routed[0:MIXED], payload, rec_ref[16:32]], 0).astype(BF16)
    for slot in range(PLANE):
        pay_ref[slot] = payload


def tables_kernel(p_ref, pairs_ref, ghost_ref, line_ref, own_ref, route_ref):
    side_y, side_z = sides()
    ghost = ghost_table()
    ghost_ref[0:LANES] = ghost
    ghost_ref[LANES : 2 * LANES] = ghost
    shape = (EDGE, LANES)
    line_ref[...] = interp(ids(shape, 0), record_ids(shape, 1)[1])

    part = dot(p_ref[...].astype(BF16), part_table())
    _, by_y, by_z = digits(ids((32, LANES), 0))
    in_y, in_z = by_y == 2 * (1 - side_y), by_z == 2 * (1 - side_z)
    for t in range(2):
        rows = part[32 * t : 32 * t + 32]
        value = jnp.where(in_y, rows[:, 0:128], 0.0) + jnp.where(in_z, rows[:, 128:256], 0.0)
        own_ref[32 * t : 32 * t + 32] = value - jnp.where(in_y & in_z, rows[:, 256:384], 0.0)

    me = lax.axis_index("blocks")
    pairs = jnp.broadcast_to(pairs_ref[...], (8, LANES))
    lanes = ids((8, LANES), 1)
    devices = PLANE * ids((8, LANES), 0) + (me & (PLANE - 1))

    def total(mask, value):
        value = jnp.where(mask, value.astype(F32), 0.0)
        return jnp.broadcast_to(jnp.sum(value, axis=1, keepdims=True), (8, LANES)).astype(jnp.int32)

    route_ref[0:8] = total(lanes == 2 * devices, pairs >> 1)
    route_ref[8:16] = total(pairs == 2 * devices, lanes >> 1)
    rows = ids((8, LANES), 0)
    mine = total(lanes == 2 * me, pairs)
    held = total(pairs == 2 * me, lanes)
    route_ref[16:24] = jnp.where(
        rows == 0, mine >> 1, jnp.where(rows == 1, held >> 1, jnp.where(rows == 2, held & 1, mine & 1))
    )


def pick(route, mask, in_ref, rows):
    chosen = None
    for member in range(PLANE):
        value = in_ref[member, rows].astype(F32)
        chosen = value if chosen is None else jnp.where((route & mask) == member, value, chosen)
    return chosen


def route_kernel(route_ref, in_ref, e_ref, right_in, left_in, out_ref, right_ref, left_ref):
    rows, lane_a = ids((16, LANES), 0) + MIXED, ids((16, LANES), 1) >> 3 & 7
    from_low = (rows == LOW) | ((rows == SHARED) & (lane_a >= 4))
    from_high = (rows == HIGH) | ((rows == SHARED) & (lane_a < 4))
    from_holder = rows >= RECORDS
    for plane in range(PLANE):
        owner = route_ref[plane : plane + 1, :]
        holder = route_ref[8 + plane : 9 + plane, :]
        mixed = jnp.where(from_holder, holder, owner)
        mixed = jnp.where(from_low, owner - 1, jnp.where(from_high, owner + 1, mixed))
        for start in range(0, ROWS, 16):
            route = owner if start < MIXED else mixed if start == MIXED else holder
            route = jnp.broadcast_to(route, (16, LANES))
            value = pick(route, PLANE - 1, in_ref, slice(start, start + 16))
            out_ref[plane, start : start + 16] = value.astype(BF16)

    side_y, side_z = sides()
    tile, base, inner = geometry()
    right_ref[...] = right_in[...]
    left_ref[...] = left_in[...]
    corner = 8 * (6 * side_y + 2 * side_z)
    lanes = ids((1, LANES), 1)
    for ref, layer, a, row in ((right_ref, NX - 1, 2, 0), (left_ref, 0, 0, 6)):
        value = rolled(e_ref[layer : layer + 1, :], (base + inner - a) & 127)
        at = pl.ds(corner + row + tile, 1)
        ref[at, :] = ref[at, :] + jnp.where(lanes == base + inner, value, 0.0)


def finish_kernel(
    t_ref, e_ref, right_ref, left_ref, in_ref, route_ref, own_ref, line_ref, share_ref, ghost_ref,
    next_ref, update_ref,
    p_ref,
):
    side_y, side_z = sides()
    tile, base, inner = geometry()
    in_y, in_z = 2 * (1 - side_y), 2 * (1 - side_z)
    for i in range(Q):
        next_ref[SPAN * i : SPAN * (i + 1), :] = t_ref[PITCH * i + FIRST : PITCH * i + FIRST + SPAN, :]

    holder = jnp.broadcast_to(route_ref[17:18, :], (32, LANES)) >> 3
    p_ref[...] = pick(holder, PLANE - 1, in_ref, slice(MIXED, ROWS))
    swap = route_ref[18:19, :] == 1
    lines = line_ref[...]
    scaled = []
    for k in range(9):
        row = RECORDS - MIXED + k
        first, second = p_ref[row : row + 1, :], p_ref[row + 9 : row + 10, :]
        scaled.append(lines * jnp.where(swap, second, first))
        scaled.append(lines * jnp.where(swap, first, second))
    scaled = jnp.concatenate(scaled, 0)
    ghost = dot(jnp.concatenate(split_bf16(scaled), 1), ghost_ref[...])
    for k in range(9):
        index = 9 * (k // 3) + 3 * (k % 3) + in_z
        for h in range(2):
            rows = pl.ds(SPAN * index + h, NX, stride=2)
            part = ghost[NX * k : NX * (k + 1), LANES * (h + 1) : LANES * (h + 2)]
            next_ref[rows, :] = next_ref[rows, :] + part
    lanes = ids((NX, LANES), 1)
    outer = lanes >> 4 == 7 * side_y
    for k in range(9):
        index = 9 * (k // 3) + 3 * in_y + k % 3
        rows = pl.ds(SPAN * index + side_y, NX, stride=2)
        next_ref[rows, :] = jnp.where(outer, ghost[NX * k : NX * (k + 1), 0:LANES], next_ref[rows, :])
    for k in range(9):
        rows = pl.ds(SPAN * (18 + k), 8)
        next_ref[rows, :] = next_ref[rows, :] + right_ref[8 * k : 8 * k + 8, :]
        rows = pl.ds(SPAN * k + SPAN - 8, 8)
        next_ref[rows, :] = next_ref[rows, :] + left_ref[8 * k : 8 * k + 8, :]
    for a in range(3):
        index = 9 * a + 6 * side_y + 2 * side_z
        low, high = (0, NX - (a - 1)) if a >= 1 else (1, NX)
        value = rolled(e_ref[low:high, :], (base + inner - a) & 127)
        value = jnp.where(lanes[low:high] == base + inner, value, 0.0)
        rows = pl.ds(SPAN * index + 2 * (low + a - 1) + tile, high - low, stride=2)
        next_ref[rows, :] = next_ref[rows, :] + value

    owner = route_ref[16:17, :]
    main = pick(jnp.broadcast_to(owner, (64, LANES)) >> 3, PLANE - 1, in_ref, slice(0, 64))
    owner = jnp.broadcast_to(owner, (16, LANES))
    lower = pick((owner + BLOCKS - 1) >> 3, PLANE - 1, in_ref, slice(MIXED, 64))
    upper = pick((owner + 1) >> 3, PLANE - 1, in_ref, slice(MIXED, 64))
    share = share_ref[...]
    main = main[0:LOW] + main[CENTRE : CENTRE + 1] * share[0:LOW]
    shared = SHARED - 48
    lane_1 = ids((1, LANES), 1)
    low_centre = jnp.sum(jnp.where(lane_1 == 48, lower[shared : shared + 1], 0.0), axis=1, keepdims=True)
    high_centre = jnp.sum(jnp.where(lane_1 == 8, upper[shared : shared + 1], 0.0), axis=1, keepdims=True)
    lower = lower + low_centre * share[48:64]
    upper = upper + high_centre * share[48:64]
    rows, lane_a = ids((32, LANES), 0), ids((32, LANES), 1) >> 3 & 7
    from_low = jnp.where(
        rows == 26,
        jnp.where(lane_a == 7, lower[shared : shared + 1], 0.0),
        jnp.where(rows - 18 == lane_a, lower[LOW - 48 : LOW - 47], 0.0),
    )
    from_high = jnp.where(
        rows == 8,
        jnp.where(lane_a == 0, upper[shared : shared + 1], 0.0),
        jnp.where(rows == lane_a, upper[HIGH - 48 : HIGH - 47], 0.0),
    )
    lane_in, lane_out = ids((LANES, LANES), 0), ids((LANES, LANES), 1)
    alike = (lane_in >> 6 == lane_out >> 6) & (lane_in & 7 == lane_out & 7)
    alike = alike.astype(F32).astype(BF16)
    edges = jnp.zeros((2 * 32, LANES), F32)
    for part in split_bf16(jnp.concatenate([from_low, from_high], 0)):
        edges = edges + dot(part, alike)
    column_0 = main[0:Q] + jnp.where(lane_a == 0, edges[0:32], 0.0)[0:Q]
    column_1 = main[Q : 2 * Q] + jnp.where(lane_a == HALF - 1, edges[32:64], 0.0)[0:Q]
    crossed = jnp.broadcast_to(route_ref[19:20, :], (Q, LANES)) == 1
    for t in range(2):
        here, there = (column_0, column_1) if t == 0 else (column_1, column_0)
        value = jnp.where(crossed, there, here) + own_ref[32 * t : 32 * t + Q, :]
        for i in range(Q):
            update_ref[0, t : t + 1, LANES * i : LANES * (i + 1)] = value[i : i + 1]


VMEM = pl.BlockSpec(memory_space=pltpu.VMEM)
HBM = pl.BlockSpec(memory_space=pltpu.HBM)


def call(kernel, name, results, inputs, outputs=None, scratch=(), cost=None, aliases=None, limit=32):
    return pl.pallas_call(
        kernel,
        out_shape=tuple(jax.ShapeDtypeStruct(*result) for result in results),
        in_specs=inputs,
        out_specs=outputs or (VMEM,) * len(results),
        scratch_shapes=scratch,
        input_output_aliases=aliases or {},
        compiler_params=pltpu.CompilerParams(vmem_limit_bytes=limit * 1024 * 1024),
        cost_estimate=cost,
        name=name,
    )


def swapped(block, bits):
    return lax.ppermute(block, "group", [(i, i ^ bits) for i in range(4)])


def body(populations, solid_mask, relax_rates, coarse_pops, interface_pairs):
    collided, edge_y, edge_z = call(
        collide_kernel,
        "collide",
        [((Q, SPAN, LANES), F32), ((2, NX, LANES), F32), ((SPAN, LANES), F32)],
        [HBM] * 3,
        (HBM, VMEM, VMEM),
        [
            pltpu.VMEM((Q, SPAN, LANES), F32),
            pltpu.VMEM((Q, SPAN, LANES), F32),
            pltpu.VMEM((SPAN, LANES), jnp.int32),
            pltpu.SMEM((Q,), F32),
            pltpu.SemaphoreType.DMA((10,)),
        ],
        limit=60,
    )(populations.reshape(Q, SPAN, LANES), solid_mask.reshape(SPAN, LANES), relax_rates)

    edge_y = swapped(edge_y, 1)
    edge_z = swapped(edge_z, 2)
    streamed, edge_yz, pool, share, chosen, records = call(
        stream_kernel,
        "stream",
        [
            ((Q * PITCH, LANES), F32),
            ((NX, LANES), F32),
            ((256, LANES), BF16),
            ((64, LANES), F32),
            ((32, LANES), F32),
            ((64, LANES), F32),
        ],
        [VMEM] * 2,
        cost=pl.CostEstimate(flops=10_000_000, bytes_accessed=8_000_000, transcendentals=0),
    )(collided, coarse_pops)

    streamed, right, left, payload, edge_yz, records = call(
        halo_kernel,
        "halo",
        [
            ((Q * PITCH, LANES), F32),
            ((72, LANES), F32),
            ((72, LANES), F32),
            ((PLANE, ROWS, LANES), BF16),
            ((NX, LANES), F32),
            ((64, LANES), F32),
        ],
        [VMEM] * 8,
        aliases={0: 0},
    )(streamed, edge_y, edge_z, edge_yz, chosen, pool, share, records)
    edge_yz = swapped(edge_yz, 3)

    near = [[PLANE * i + j for j in range(PLANE)] for i in range(PLANE)]
    far = [[PLANE * j + i for j in range(PLANE)] for i in range(PLANE)]
    payload = lax.all_to_all(payload, "blocks", 0, 0, axis_index_groups=near, tiled=True)
    ghost, line, own, route = call(
        tables_kernel,
        "tables",
        [((256, 384), BF16), ((EDGE, LANES), F32), ((64, LANES), F32), ((24, LANES), jnp.int32)],
        [VMEM] * 2,
        cost=pl.CostEstimate(flops=1_000_000, bytes_accessed=4_000_000, transcendentals=0),
    )(records, interface_pairs)
    payload, right, left = call(
        route_kernel,
        "route",
        [((PLANE, ROWS, LANES), BF16), ((72, LANES), F32), ((72, LANES), F32)],
        [VMEM] * 5,
    )(route, payload, edge_yz, right, left)
    payload = lax.all_to_all(payload, "blocks", 0, 0, axis_index_groups=far, tiled=True)
    ring = [(i, (i + 1) % BLOCKS) for i in range(BLOCKS)]
    right = lax.ppermute(right, "blocks", ring)
    left = lax.ppermute(left, "blocks", [(b, a) for a, b in ring])

    result, update = call(
        finish_kernel,
        "finish",
        [((Q * SPAN, LANES), F32), ((1, 2, Q * LANES), F32)],
        [VMEM] * 10,
        scratch=[pltpu.VMEM((32, LANES), F32)],
    )(streamed, edge_yz, right, left, payload, route, own, line, share, ghost)
    return result.reshape(1, Q, SPAN * LANES), update


def solution(mesh):
    placed = (
        P("group", None, "blocks"),
        P("group", "blocks"),
        P(),
        P("group", "blocks", None),
        P("group", None),
    )
    return jax.shard_map(
        body,
        mesh=mesh,
        in_specs=placed,
        out_specs=(P("group", None, "blocks"), P("group", "blocks", None)),
        check_vma=False,
    )
```

```python
import jax
import jax.numpy as jnp
from jax import lax
from jax.experimental import pallas as pl
from jax.experimental.pallas import tpu as pltpu
from jax.sharding import PartitionSpec as P

Q = 27
EDGE = 16
HALF = 8
NX = 32
SPAN = 2 * NX
PITCH = SPAN + 16
FIRST = 8
LANES = 128
PLANE = 8
BLOCKS = PLANE * PLANE
LOW, HIGH, LAST_LOW, LAST_HIGH, CENTRE, RECORDS, ROWS = 54, 55, 56, 57, 58, 62, 80
TILE = 16
MIXED = 48
POOLED = 8 * (2 * Q + 4)
ENDS = 32
PAIRS = [(i // 9, i // 3 % 3, i % 3) for i in range(Q)]
F32 = jnp.float32
BF16 = jnp.bfloat16


def sides():
    position = lax.axis_index("group")
    return position & 1, position >> 1


def geometry():
    side_y, side_z = sides()
    return 1 - side_y, 112 * (1 - side_y), 15 * (1 - side_z)


def ids(shape, dim):
    return lax.broadcasted_iota(jnp.int32, shape, dim)


def rolled(value, shift):
    return pltpu.roll(value, shift, 1)


def split_bf16(value):
    high = value.astype(BF16)
    return high, (value - high.astype(F32)).astype(BF16)


def dot(left, right):
    return jnp.dot(left, right, preferred_element_type=F32)


def record_ids(shape, dim):
    value = ids(shape, dim) & 127
    return value >> 6, value >> 3 & 7, value & 7


def digits(index):
    third, ninth = index * 11 >> 5, index * 57 >> 9
    return ninth, third - 3 * ninth, index - 3 * third


def interp(fine, coarse):
    weight = 1.0 - jnp.abs(0.5 * fine.astype(F32) - 0.25 - coarse.astype(F32))
    end = (fine == 0) | (fine == EDGE - 1)
    return jnp.where(weight > 0.0, jnp.where(end, 1.0, weight), 0.0)


def pool_table():
    side_y, side_z = sides()
    shape = (256, LANES)
    cell = ids(shape, 0)
    pair_y, pair_z = cell >> 5, cell >> 1 & 7
    face, a, b = record_ids(shape, 1)
    on_y = (pair_y == 7 * side_y) & (pair_z == b)
    on_z = (pair_z == 7 * side_z) & (pair_y == b)
    return jnp.where(((face == 0) & on_y) | ((face == 1) & on_z), 0.125, 0.0).astype(BF16)


def share_table():
    side_y, side_z = sides()
    shape = (64, LANES)
    row = ids(shape, 0)
    face, a, b = record_ids(shape, 1)
    column = (row >= Q).astype(jnp.int32)
    index = jnp.where(row < LOW, row - Q * column, jnp.where(row == LOW, 18 + a, a))
    index = jnp.where(row == LAST_LOW, 26, jnp.where(row == LAST_HIGH, 8, index))
    by_x, by_y, by_z = digits(index)
    in_y, in_z = by_y == 2 * (1 - side_y), by_z == 2 * (1 - side_z)
    half_y = in_y & ((face == 0) | (b == 7 * side_y))
    half_z = in_z & ((face == 1) | (b == 7 * side_z))
    low = (by_x == 2) & (column == 0) & (a == 0)
    high = (by_x == 0) & (column == 1) & (a == HALF - 1)
    half_x = (row >= LOW) | low | high
    share = jnp.where(half_y, 0.5, 1.0) * jnp.where(half_z, 0.5, 1.0) * jnp.where(half_x, 0.5, 1.0)
    held = (row <= HIGH) | ((row == LAST_LOW) & (a == 7)) | ((row == LAST_HIGH) & (a == 0))
    return jnp.where(held, share, 0.0)


def chosen_table():
    shape = (64, POOLED)
    target, block = ids(shape, 0), ids(shape, 1) >> 3
    second = (target >= Q).astype(jnp.int32)
    wanted = jnp.where(target < LOW, 2 * (target - Q * second) + second, -1)
    wanted = jnp.where(target == LOW, 54, jnp.where(target == HIGH, 56, wanted))
    wanted = jnp.where(target == LAST_LOW, 55, jnp.where(target == LAST_HIGH, 57, wanted))
    return (wanted == block).astype(F32).astype(BF16)


def ghost_table():
    side_y, side_z = sides()
    shape = (LANES, LANES)
    face, a, b = record_ids(shape, 0)
    lanes = ids(shape, 1)
    y, z = lanes >> 4, lanes & 15
    parts = [jnp.where((face == 0) & (y == 7 * side_y), interp(z, b), 0.0)]
    for h in range(2):
        parts.append(jnp.where((face == 1) & (z == 15 * side_z), interp(y + HALF * h, b), 0.0))
    return jnp.concatenate(parts, 1).astype(BF16)


def part_table():
    side_y, side_z = sides()
    shape = (LANES, LANES)
    face, a, b = record_ids(shape, 0)
    to_face, to_a, to_b = record_ids(shape, 1)
    along_x = 0.125 * (interp(2 * to_a, a) + interp(2 * to_a + 1, a))
    across = along_x * (interp(2 * to_b, b) + interp(2 * to_b + 1, b))
    zero = jnp.zeros(shape, jnp.int32)
    out_y, out_z = zero + 15 * side_y, zero + 15 * side_z
    next_y, next_z = zero + 1 + 13 * side_y, zero + 1 + 13 * side_z
    edge_y, edge_z = to_b == 7 * side_y, to_b == 7 * side_z
    line_y = along_x * interp(out_y, b)
    both_y = line_y + along_x * interp(next_y, b)
    both_z = along_x * (interp(out_z, b) + interp(next_z, b))
    in_y = jnp.where(to_face == 0, across, jnp.where(edge_y, both_z, 0.0))
    in_z = jnp.where(to_face == 1, across, jnp.where(edge_z, both_y, 0.0))
    ends = ((to_face == 0) & edge_z) | ((to_face == 1) & edge_y)
    shared = jnp.where(ends, line_y, 0.0)
    parts = [jnp.where(face == 0, in_y, 0.0), jnp.where(face == 1, in_z, 0.0), jnp.where(face == 1, shared, 0.0)]
    return jnp.concatenate(parts, 1).astype(BF16)


def along(table, axis, line):
    out = {}
    for first in range(3):
        for second in range(3):
            keys = []
            for third in range(3):
                key = [first, second]
                key.insert(axis, third)
                keys.append(tuple(key))
            values = line(*[table[key] for key in keys])
            for key, value in zip(keys, values):
                out[key] = value
    return out


def line_moments(low, mid, high):
    both = low + high
    return both + 4.0 * mid, high - low, both


def line_inverse(zeroth, first, second):
    return second - first, zeroth - 0.5 * second, first + second


def collide_cells(current, rates):
    table = {PAIRS[i]: current[i] for i in range(Q)}
    moments = table
    for axis in range(3):
        moments = along(moments, axis, line_moments)
    density = moments[0, 0, 0]
    inverse = 1.0 / density
    flow = [moments[1, 0, 0], moments[0, 1, 0], moments[0, 0, 1]]
    speed = [part * inverse for part in flow]
    carried = [density * part for part in speed]
    square = [carried[axis] * speed[axis] for axis in range(3)]
    third = density * (1.0 / 3.0)
    relaxed = {}
    for index, key in enumerate(PAIRS):
        ones = [axis for axis in range(3) if key[axis] == 1]
        twos = [axis for axis in range(3) if key[axis] == 2]
        scale = (1.0 / 3.0) ** len(twos)
        if len(ones) == 0:
            if len(twos) == 0:
                balance = density
            elif len(twos) == 1:
                balance = third + square[twos[0]]
            elif len(twos) == 2:
                balance = (third + square[twos[0]] + square[twos[1]]) * (1.0 / 3.0)
            else:
                balance = (third + square[0] + square[1] + square[2]) * (1.0 / 9.0)
        elif len(ones) == 1:
            balance = carried[ones[0]] * scale if twos else carried[ones[0]]
        elif len(ones) == 2:
            balance = carried[ones[0]] * speed[ones[1]]
            balance = balance * scale if twos else balance
        else:
            balance = None
        rest = moments[key] if balance is None else moments[key] - balance
        relaxed[key] = rates[index] * rest
    change = relaxed
    for axis in range(3):
        change = along(change, axis, line_inverse)
    return [current[i] - change[PAIRS[i]] for i in range(Q)]


def collide_kernel(
    g_hbm, solid_hbm, rates_hbm, w_ref, y_ref, z_ref, g_ref, solid_ref, rates_ref, sems
):
    pieces = 4
    size = SPAN // pieces
    copies = [
        pltpu.make_async_copy(rates_hbm, rates_ref, sems.at[pieces]),
        pltpu.make_async_copy(solid_hbm, solid_ref, sems.at[pieces + 1]),
    ]
    for piece in range(pieces):
        rows = pl.ds(size * piece, size)
        copies.append(
            pltpu.make_async_copy(g_hbm.at[:, rows, :], g_ref.at[:, rows, :], sems.at[piece])
        )
    for copy in copies:
        copy.start()
    side_y, side_z = sides()
    copies[0].wait()
    rates = []
    for i in range(Q):
        scale = 1.0 / 216.0
        for part in PAIRS[i]:
            scale *= 1.5 if part == 0 else 3.0
        rates.append(rates_ref[i] * scale)
    copies[1].wait()

    def chunk(index, carry):
        row = pl.multiple_of(8 * index, 8)
        current = [g_ref[i, pl.ds(row, 8), :] for i in range(Q)]
        solid = solid_ref[pl.ds(row, 8), :] == 1
        collided = collide_cells(current, rates)
        for i in range(Q):
            w_ref[i, pl.ds(row, 8), :] = jnp.where(solid, current[Q - 1 - i], collided[i])
        return carry

    for piece in range(pieces):
        copies[2 + piece].wait()
        lax.fori_loop(size // 8 * piece, size // 8 * (piece + 1), chunk, 0)

    send_y, send_z = 2 * (1 - side_y), 2 * (1 - side_z)
    tile, base, inner = geometry()
    lanes = ids((NX, LANES), 1)
    packed = [jnp.zeros((NX, LANES), F32), jnp.zeros((NX, LANES), F32)]
    for k in range(9):
        index = 9 * (k // 3) + 3 * send_y + k % 3
        value = w_ref[index, pl.ds(tile, NX, stride=2), :]
        value = rolled(value, (16 * (k % 8) - base) & 127)
        packed[k // 8] = jnp.where(lanes >> 4 == k % 8, value, packed[k // 8])
    y_ref[0] = (packed[0] - 1.0).astype(BF16)
    y_ref[1] = (packed[1] - 1.0).astype(BF16)
    lanes = ids((SPAN, LANES), 1)
    packed_z = jnp.zeros((SPAN, LANES), F32)
    for k in range(9):
        index = 9 * (k // 3) + 3 * (k % 3) + send_z
        value = w_ref[index]
        packed_z = jnp.where(lanes & 15 == k, rolled(value, (k - inner) & 127), packed_z)
    z_ref[...] = (packed_z - 1.0).astype(BF16)


def moved(value, b, shift):
    value = rolled(value, shift)
    if b == 1:
        return value
    rows, lanes = ids(value.shape, 0), ids(value.shape, 1)
    if b == 2:
        other = pltpu.roll(value, 1, 0)
        return jnp.where(lanes >= 16, value, jnp.where(rows & 1 == 1, other, 0.0))
    other = pltpu.roll(value, value.shape[0] - 1, 0)
    return jnp.where(lanes < 112, value, jnp.where(rows & 1 == 0, other, 0.0))


def z_inside(lanes, c):
    return lanes & 15 <= 14 if c == 0 else lanes & 15 >= 1


def stream_kernel(
    w_ref, coarse_hbm, t_ref, e_ref, pool_ref, share_ref, rec_ref, p_ref, chosen_ref, coarse_ref, sem
):
    copy = pltpu.make_async_copy(coarse_hbm, coarse_ref, sem)
    copy.start()
    lanes = ids((8, LANES), 1)
    zeros = jnp.zeros((8, LANES), F32)
    for i, (a, b, c) in enumerate(PAIRS):
        for row in (0, 8, SPAN, SPAN + 8):
            t_ref[pl.ds(PITCH * i + row, 8), :] = zeros
        shift = (16 * (b - 1) + c - 1) % 128
        for row in range(0, SPAN, 8):
            value = w_ref[i, pl.ds(row, 8), :]
            if shift:
                value = moved(value, b, shift)
            if c != 1:
                value = jnp.where(z_inside(lanes, c), value, 0.0)
            t_ref[pl.ds(PITCH * i + FIRST + row + 2 * (a - 1), 8), :] = value

    side_y, side_z = sides()
    tile, base, inner = geometry()
    lanes = ids((NX, LANES), 1)
    packed = jnp.zeros((NX, LANES), F32)
    for a in range(3):
        index = 9 * a + 6 * (1 - side_y) + 2 * (1 - side_z)
        value = w_ref[index, pl.ds(tile, NX, stride=2), :]
        packed = jnp.where(lanes == a, rolled(value, (a - base - inner) & 127), packed)
    e_ref[...] = packed

    p_ref[...] = jnp.zeros((64, LANES), F32)
    copy.wait()
    records = coarse_ref[0].astype(F32)
    for t in range(2):
        for i in range(Q):
            p_ref[32 * t + i : 32 * t + i + 1, :] = records[t : t + 1, LANES * i : LANES * (i + 1)]
    in_y, in_z = 2 * (1 - side_y), 2 * (1 - side_z)
    first = ids((1, LANES), 1) < 64
    rec_ref[...] = jnp.zeros((32, LANES), F32)
    for t in range(2):
        for k in range(9):
            for_y = p_ref[pl.ds(32 * t + 9 * (k // 3) + 3 * in_y + k % 3, 1), :]
            for_z = p_ref[pl.ds(32 * t + 9 * (k // 3) + 3 * (k % 3) + in_z, 1), :]
            row = RECORDS - MIXED + 9 * t + k
            rec_ref[row : row + 1, :] = jnp.where(first, for_y, for_z)

    pool_ref[...] = pool_table()
    share_ref[...] = share_table()
    chosen_ref[...] = chosen_table()


def halo_kernel(
    t_ref, y_ref, z_ref, e_ref, rec_ref, pool_ref, share_ref, p_ref, chosen_ref,
    out_ref, right_ref, left_ref, pay_ref, kept_ref,
):
    del t_ref
    kept_ref[...] = p_ref[...]
    side_y, side_z = sides()
    halo_y, halo_z = 2 * side_y, 2 * side_z
    tile, base, inner = geometry()

    lanes = ids((NX, LANES), 1)
    row_mask = lanes >> 4 == base >> 4
    for k in range(9):
        a, c = k // 3, k % 3
        value = rolled(y_ref[k // 8].astype(F32) + 1.0, (base - 16 * (k % 8) + c - 1) & 127)
        mask = row_mask if c == 1 else row_mask & z_inside(lanes, c)
        index = 9 * a + 3 * halo_y + c
        rows = pl.ds(PITCH * index + FIRST + 2 * (a - 1) + tile, NX, stride=2)
        out_ref[rows, :] = out_ref[rows, :] + jnp.where(mask, value, 0.0)
    lanes = ids((TILE, LANES), 1)
    for k in range(9):
        a, b = k // 3, k % 3
        shift = (inner - k + 16 * (b - 1)) & 127
        index = 9 * a + 3 * b + halo_z
        for row in range(0, SPAN, TILE):
            value = moved(z_ref[row : row + TILE].astype(F32) + 1.0, b, shift)
            rows = pl.ds(PITCH * index + FIRST + row + 2 * (a - 1), TILE)
            out_ref[rows, :] = out_ref[rows, :] + jnp.where(lanes & 15 == inner, value, 0.0)

    for k in range(9):
        right_ref[2 * k : 2 * k + 2, :] = out_ref[pl.ds(PITCH * (18 + k) + FIRST + SPAN, 2), :]
        left_ref[2 * k : 2 * k + 2, :] = out_ref[pl.ds(PITCH * k + FIRST - 2, 2), :]
    right_ref[24:ENDS, :] = e_ref[NX - 8 : NX, :]
    left_ref[24:ENDS, :] = e_ref[0:8, :]

    row_8 = ids((8, LANES), 0)
    tiles = []
    for h in range(2):
        parts = []
        for i in range(Q):
            for s in range(2):
                row = PITCH * i + FIRST + NX * s + h
                parts.append(
                    out_ref[pl.ds(row, 8, stride=4), :] + out_ref[pl.ds(row + 2, 8, stride=4), :]
                )
        over, under = FIRST + SPAN + h, FIRST - 2 + h
        parts.append(out_ref[pl.ds(PITCH * 18 + over, 8, stride=PITCH), :])
        last = out_ref[pl.ds(PITCH * 19 + over, 8, stride=PITCH), :]
        parts.append(jnp.where(row_8 == 7, last, 0.0))
        parts.append(out_ref[pl.ds(under, 8, stride=PITCH), :])
        parts.append(out_ref[pl.ds(PITCH * 8 + under, 8, stride=PITCH), :])
        tiles.append(jnp.concatenate(parts, 0))
    pool = pool_ref[...]
    high, low = split_bf16(jnp.concatenate(tiles, 1))
    pooled = dot(high, pool) + dot(low, pool)
    pooled = jnp.where(ids((POOLED, LANES), 0) & 7 == ids((POOLED, LANES), 1) >> 3 & 7, pooled, 0.0)
    chosen = chosen_ref[...]
    high, low = split_bf16(pooled)
    routed = dot(chosen, high) + dot(chosen, low)

    share = share_ref[...]
    rows, lane_a = ids((64, LANES), 0), ids((64, LANES), 1) >> 3 & 7
    inside = rows < LOW
    held = jnp.sum(jnp.where(inside, routed, 0.0), axis=0, keepdims=True)
    held = jnp.sum(held, axis=1, keepdims=True)
    parts = jnp.sum(jnp.where(inside, share, 0.0), axis=0, keepdims=True)
    parts = jnp.sum(parts, axis=1, keepdims=True)
    centre = (held / parts).astype(BF16).astype(F32)
    routed = routed - centre * share
    is_centre = (rows == CENTRE) | ((rows == LAST_LOW) & (lane_a == 6)) | ((rows == LAST_HIGH) & (lane_a == 1))
    routed = jnp.where(is_centre, centre, routed)
    payload = jnp.where(rows[MIXED:64] >= RECORDS, rec_ref[0:16], routed[MIXED:64])
    payload = jnp.concatenate([routed[0:MIXED], payload, rec_ref[16:32]], 0).astype(BF16)
    for slot in range(PLANE):
        pay_ref[slot] = payload


def tables_kernel(p_ref, pairs_ref, ghost_ref, line_ref, own_ref, route_ref, last_ref, flag_ref):
    side_y, side_z = sides()
    ghost = ghost_table()
    ghost_ref[0:LANES] = ghost
    ghost_ref[LANES : 2 * LANES] = ghost
    shape = (EDGE, LANES)
    line_ref[...] = interp(ids(shape, 0), record_ids(shape, 1)[1])

    part = dot(p_ref[...].astype(BF16), part_table())
    _, by_y, by_z = digits(ids((32, LANES), 0))
    in_y, in_z = by_y == 2 * (1 - side_y), by_z == 2 * (1 - side_z)
    for t in range(2):
        rows = part[32 * t : 32 * t + 32]
        value = jnp.where(in_y, rows[:, 0:128], 0.0) + jnp.where(in_z, rows[:, 128:256], 0.0)
        own_ref[32 * t : 32 * t + 32] = value - jnp.where(in_y & in_z, rows[:, 256:384], 0.0)

    me = lax.axis_index("blocks")
    pairs = pairs_ref[...]
    rows, lanes = ids((LANES, LANES), 0), ids((LANES, LANES), 1)

    def total(mask, value):
        value = jnp.where(mask, value.astype(F32), 0.0)
        value = jnp.sum(value, axis=1, keepdims=True)
        return jnp.broadcast_to(value, mask.shape).astype(jnp.int32)

    def matrices(ref, owner, holder, source, rows, lanes):
        place = rows & (TILE - 1)
        low = (place == LOW - MIXED) | (place == LAST_LOW - MIXED)
        high = (place == HIGH - MIXED) | (place == LAST_HIGH - MIXED)
        mixed = jnp.where(low, owner - 1, jnp.where(high, owner + 1, owner))
        mixed = jnp.where(place >= RECORDS - MIXED, holder, mixed)
        for kind, route in enumerate((owner, mixed, holder)):
            chosen = (source(route) == lanes >> 4) & (place == lanes & (TILE - 1))
            ref[kind] = chosen.astype(F32).astype(BF16)

    device = PLANE * (rows >> 4) + (me & (PLANE - 1))
    pairs = jnp.broadcast_to(pairs, (LANES, LANES))
    owner = total(lanes == 2 * device, pairs >> 1)
    holder = total(pairs == 2 * device, lanes >> 1)
    matrices(route_ref, owner, holder, lambda route: route & (PLANE - 1), rows, lanes)
    rows, lanes, pairs = rows[0:TILE], lanes[0:TILE], pairs[0:TILE]
    serves = total(lanes == 2 * me, pairs)
    record = total(pairs == 2 * me, lanes)
    matrices(last_ref, serves >> 1, record >> 1, lambda route: (route & (BLOCKS - 1)) >> 3, rows, lanes)
    flag_ref[...] = jnp.where(rows[0:8] == 0, record[0:8] & 1, serves[0:8] & 1)


def passed_on(matrix_ref, in_ref):
    for start in range(0, ROWS, TILE):
        kind = 0 if start < MIXED else 1 if start == MIXED else 2
        tile = [in_ref[member, start : start + TILE] for member in range(PLANE)]
        yield start, dot(matrix_ref[kind], jnp.concatenate(tile, 0))


def route_kernel(route_ref, in_ref, e_ref, right_ref, left_ref, out_ref, edge_ref):
    for start, rows in passed_on(route_ref, in_ref):
        rows = rows.astype(BF16)
        for plane in range(PLANE):
            out_ref[plane, start : start + TILE] = rows[TILE * plane : TILE * (plane + 1)]
    edge_ref[0:NX, :] = e_ref[...]
    edge_ref[NX : NX + 8, :] = right_ref[24:ENDS, :]
    edge_ref[NX + 8 : NX + 16, :] = left_ref[24:ENDS, :]


def merge_kernel(t_ref, e_ref, right_ref, left_ref, next_ref):
    side_y, side_z = sides()
    tile, base, inner = geometry()
    for i in range(Q):
        next_ref[i] = t_ref[PITCH * i + FIRST : PITCH * i + FIRST + SPAN, :]
    for k in range(9):
        next_ref[18 + k, 0:2] = next_ref[18 + k, 0:2] + right_ref[2 * k : 2 * k + 2, :]
        next_ref[k, SPAN - 2 : SPAN] = next_ref[k, SPAN - 2 : SPAN] + left_ref[2 * k : 2 * k + 2, :]
    rows, lanes = ids((NX, LANES), 0), ids((NX, LANES), 1)
    corner = e_ref[0:NX, :]
    low = jnp.where(rows == 0, e_ref[NX + 7 : NX + 8, :], pltpu.roll(corner, 1, 0))
    high = jnp.where(rows == NX - 1, e_ref[NX + 8 : NX + 9, :], pltpu.roll(corner, NX - 1, 0))
    for a, value in ((0, high), (1, corner), (2, low)):
        index = 9 * a + 6 * side_y + 2 * side_z
        value = rolled(value, (base + inner - a) & 127)
        at = pl.ds(tile, NX, stride=2)
        next_ref[index, at, :] = next_ref[index, at, :] + jnp.where(lanes == base + inner, value, 0.0)


def finish_kernel(
    base_ref, in_ref, last_ref, flag_ref, own_ref, line_ref, share_ref, ghost_ref,
    value_ref, next_hbm, update_hbm,
    update_ref, sems,
):
    del base_ref
    side_y, side_z = sides()
    in_y, in_z = 2 * (1 - side_y), 2 * (1 - side_z)
    copies = []

    def send(source, target):
        copy = pltpu.make_async_copy(source, target, sems.at[len(copies)])
        copy.start()
        copies.append(copy)

    rows = jnp.concatenate([tile for _, tile in passed_on(last_ref, in_ref)], 0)
    swap = flag_ref[0:1, :] == 1
    lines = line_ref[...]
    scaled = []
    for k in range(9):
        row = RECORDS + k
        first, second = rows[row : row + 1], rows[row + 9 : row + 10]
        scaled.append(lines * jnp.where(swap, second, first))
        scaled.append(lines * jnp.where(swap, first, second))
    scaled = jnp.concatenate(scaled, 0)
    ghost = dot(jnp.concatenate(split_bf16(scaled), 1), ghost_ref[...])
    lanes = ids((NX, LANES), 1)
    outer = lanes >> 4 == 7 * side_y
    for a in range(3):
        for b in range(3):
            k = 3 * a + b
            for h in range(2):
                at = pl.ds(h, NX, stride=2)
                part = ghost[NX * k : NX * (k + 1), LANES * (h + 1) : LANES * (h + 2)]
                value_ref[9 * a + 3 * b + in_z, at, :] = value_ref[9 * a + 3 * b + in_z, at, :] + part
        for c in range(3):
            k = 3 * a + c
            at = pl.ds(side_y, NX, stride=2)
            part = ghost[NX * k : NX * (k + 1), 0:LANES]
            value = value_ref[9 * a + 3 * in_y + c, at, :]
            value_ref[9 * a + 3 * in_y + c, at, :] = jnp.where(outer, part, value)
        send(value_ref.at[pl.ds(9 * a, 9)], next_hbm.at[pl.ds(9 * a, 9)])

    share = share_ref[...]
    lane_1 = ids((1, LANES), 1)
    low_centre = jnp.sum(jnp.where(lane_1 == 48, rows[LAST_LOW : LAST_LOW + 1], 0.0), axis=1, keepdims=True)
    high_centre = jnp.sum(jnp.where(lane_1 == 8, rows[LAST_HIGH : LAST_HIGH + 1], 0.0), axis=1, keepdims=True)
    main = rows[0:LOW] + rows[CENTRE : CENTRE + 1] * share[0:LOW]
    low, high, last_low, last_high = (
        rows[row : row + 1] + centre * share[row : row + 1]
        for row, centre in (
            (LOW, low_centre), (HIGH, high_centre), (LAST_LOW, low_centre), (LAST_HIGH, high_centre)
        )
    )
    row, lane_a = ids((32, LANES), 0), ids((32, LANES), 1) >> 3 & 7
    from_low = jnp.where(row - 18 == lane_a, low, 0.0)
    from_low = jnp.where(row == 26, jnp.where(lane_a == 7, last_low, 0.0), from_low)
    from_high = jnp.where(row == lane_a, high, 0.0)
    from_high = jnp.where(row == 8, jnp.where(lane_a == 0, last_high, 0.0), from_high)
    lane_in, lane_out = ids((LANES, LANES), 0), ids((LANES, LANES), 1)
    alike = (lane_in >> 6 == lane_out >> 6) & (lane_in & 7 == lane_out & 7)
    alike = alike.astype(F32).astype(BF16)
    edges = jnp.zeros((2 * 32, LANES), F32)
    for part in split_bf16(jnp.concatenate([from_low, from_high], 0)):
        edges = edges + dot(part, alike)
    column_0 = main[0:Q] + jnp.where(lane_a == 0, edges[0:32], 0.0)[0:Q]
    column_1 = main[Q : 2 * Q] + jnp.where(lane_a == HALF - 1, edges[32:64], 0.0)[0:Q]
    crossed = jnp.broadcast_to(flag_ref[1:2, :], (Q, LANES)) == 1
    for t in range(2):
        here, there = (column_0, column_1) if t == 0 else (column_1, column_0)
        value = jnp.where(crossed, there, here) + own_ref[32 * t : 32 * t + Q, :]
        for i in range(Q):
            update_ref[0, t : t + 1, LANES * i : LANES * (i + 1)] = value[i : i + 1]
    send(update_ref, update_hbm)
    for copy in copies:
        copy.wait()


VMEM = pl.BlockSpec(memory_space=pltpu.VMEM)
HBM = pl.BlockSpec(memory_space=pltpu.HBM)


def call(kernel, name, results, inputs, outputs=None, scratch=(), cost=None, aliases=None, limit=32):
    return pl.pallas_call(
        kernel,
        out_shape=tuple(jax.ShapeDtypeStruct(*result) for result in results),
        in_specs=inputs,
        out_specs=outputs or (VMEM,) * len(results),
        scratch_shapes=scratch,
        input_output_aliases=aliases or {},
        compiler_params=pltpu.CompilerParams(vmem_limit_bytes=limit * 1024 * 1024),
        cost_estimate=cost,
        name=name,
    )


def in_hbm(value):
    return pltpu.with_memory_space_constraint(value, pltpu.HBM)


def swapped(block, bits):
    return lax.ppermute(block, "group", [(i, i ^ bits) for i in range(4)])


def body(populations, solid_mask, relax_rates, coarse_pops, interface_pairs):
    collided, edge_y, edge_z = call(
        collide_kernel,
        "collide",
        [((Q, SPAN, LANES), F32), ((2, NX, LANES), BF16), ((SPAN, LANES), BF16)],
        [HBM] * 3,
        scratch=[
            pltpu.VMEM((Q, SPAN, LANES), F32),
            pltpu.VMEM((SPAN, LANES), jnp.int32),
            pltpu.SMEM((Q,), F32),
            pltpu.SemaphoreType.DMA((6,)),
        ],
    )(
        in_hbm(populations.reshape(Q, SPAN, LANES)),
        in_hbm(solid_mask.reshape(SPAN, LANES)),
        in_hbm(relax_rates),
    )

    edge_z = swapped(edge_z, 2)
    edge_y = swapped(edge_y, 1)
    streamed, edge_yz, pool, share, halves, records, chosen = call(
        stream_kernel,
        "stream",
        [
            ((Q * PITCH, LANES), F32),
            ((NX, LANES), F32),
            ((256, LANES), BF16),
            ((64, LANES), F32),
            ((32, LANES), F32),
            ((64, LANES), F32),
            ((64, POOLED), BF16),
        ],
        [VMEM, HBM],
        scratch=[pltpu.VMEM((1, 2, Q * LANES), BF16), pltpu.SemaphoreType.DMA(())],
        cost=pl.CostEstimate(flops=10_000_000, bytes_accessed=8_000_000, transcendentals=0),
    )(collided, in_hbm(coarse_pops))

    streamed, right, left, payload, records = call(
        halo_kernel,
        "halo",
        [
            ((Q * PITCH, LANES), F32),
            ((ENDS, LANES), F32),
            ((ENDS, LANES), F32),
            ((PLANE, ROWS, LANES), BF16),
            ((64, LANES), F32),
        ],
        [VMEM] * 9,
        aliases={0: 0},
    )(streamed, edge_y, edge_z, edge_yz, halves, pool, share, records, chosen)

    near = [[PLANE * i + j for j in range(PLANE)] for i in range(PLANE)]
    far = [[PLANE * j + i for j in range(PLANE)] for i in range(PLANE)]
    payload = lax.all_to_all(payload, "blocks", 0, 0, axis_index_groups=near, tiled=True)
    ring = [(i, (i + 1) % BLOCKS) for i in range(BLOCKS)]
    right = lax.ppermute(right, "blocks", ring)
    left = lax.ppermute(left, "blocks", [(b, a) for a, b in ring])
    ghost, line, own, route, last, flags = call(
        tables_kernel,
        "tables",
        [
            ((256, 384), BF16),
            ((EDGE, LANES), F32),
            ((64, LANES), F32),
            ((3, LANES, LANES), BF16),
            ((3, TILE, LANES), BF16),
            ((8, LANES), jnp.int32),
        ],
        [VMEM] * 2,
        cost=pl.CostEstimate(flops=1_000_000, bytes_accessed=4_000_000, transcendentals=0),
    )(records, interface_pairs)
    payload, edge_yz = call(
        route_kernel,
        "route",
        [((PLANE, ROWS, LANES), BF16), ((NX + 16, LANES), F32)],
        [VMEM] * 5,
    )(route, payload, edge_yz, right, left)
    payload = lax.all_to_all(payload, "blocks", 0, 0, axis_index_groups=far, tiled=True)
    edge_yz = swapped(edge_yz, 3)
    merged = call(
        merge_kernel,
        "merge",
        [((Q, SPAN, LANES), F32)],
        [VMEM] * 4,
        cost=pl.CostEstimate(flops=1_000_000, bytes_accessed=4_000_000, transcendentals=0),
    )(streamed, edge_yz, right, left)[0]
    _, result, update = call(
        finish_kernel,
        "finish",
        [((Q, SPAN, LANES), F32), ((Q, SPAN, LANES), F32), ((1, 2, Q * LANES), F32)],
        [VMEM] * 8,
        (VMEM, HBM, HBM),
        [pltpu.VMEM((1, 2, Q * LANES), F32), pltpu.SemaphoreType.DMA((4,))],
        aliases={0: 0},
    )(merged, payload, last, flags, own, line, share, ghost)
    return result.reshape(1, Q, SPAN * LANES), update


def solution(mesh):
    placed = (
        P("group", None, "blocks"),
        P("group", "blocks"),
        P(),
        P("group", "blocks", None),
        P("group", None),
    )
    return jax.shard_map(
        body,
        mesh=mesh,
        in_specs=placed,
        out_specs=(P("group", None, "blocks"), P("group", "blocks", None)),
        check_vma=False,
    )
```

```python
import jax
import jax.numpy as jnp
from jax import lax
from jax.experimental import pallas as pl
from jax.experimental.pallas import tpu as pltpu
from jax.sharding import PartitionSpec as P

Q = 27
EDGE = 16
HALF = 8
NX = 32
SPAN = 2 * NX
PITCH = SPAN + 16
FIRST = 8
LANES = 128
PLANE = 8
BLOCKS = PLANE * PLANE
TURN = 5
LOW, HIGH, LAST_LOW, LAST_HIGH, CENTRE, RECORDS, ROWS = 54, 55, 56, 57, 58, 62, 80
TILE = 16
MIXED = 48
POOLED = 8 * (2 * Q + 4)
ENDS = 32
PAIRS = [(i // 9, i // 3 % 3, i % 3) for i in range(Q)]
F32 = jnp.float32
BF16 = jnp.bfloat16


def sides():
    position = lax.axis_index("group")
    return position & 1, position >> 1


def geometry():
    side_y, side_z = sides()
    return 1 - side_y, 112 * (1 - side_y), 15 * (1 - side_z)


def ids(shape, dim):
    return lax.broadcasted_iota(jnp.int32, shape, dim)


def rolled(value, shift):
    return pltpu.roll(value, shift, 1)


def split_bf16(value):
    high = value.astype(BF16)
    return high, (value - high.astype(F32)).astype(BF16)


def dot(left, right):
    return jnp.dot(left, right, preferred_element_type=F32)


def record_ids(shape, dim):
    value = ids(shape, dim) & 127
    return value >> 6, value >> 3 & 7, value & 7


def digits(index):
    third, ninth = index * 11 >> 5, index * 57 >> 9
    return ninth, third - 3 * ninth, index - 3 * third


def interp(fine, coarse):
    weight = 1.0 - jnp.abs(0.5 * fine.astype(F32) - 0.25 - coarse.astype(F32))
    end = (fine == 0) | (fine == EDGE - 1)
    return jnp.where(weight > 0.0, jnp.where(end, 1.0, weight), 0.0)


def pool_table():
    side_y, side_z = sides()
    shape = (256, LANES)
    cell = ids(shape, 0)
    pair_y, pair_z = cell >> 5, cell >> 1 & 7
    face, a, b = record_ids(shape, 1)
    on_y = (pair_y == 7 * side_y) & (pair_z == b)
    on_z = (pair_z == 7 * side_z) & (pair_y == b)
    return jnp.where(((face == 0) & on_y) | ((face == 1) & on_z), 0.125, 0.0).astype(BF16)


def share_table():
    side_y, side_z = sides()
    shape = (64, LANES)
    row = ids(shape, 0)
    face, a, b = record_ids(shape, 1)
    column = (row >= Q).astype(jnp.int32)
    index = jnp.where(row < LOW, row - Q * column, jnp.where(row == LOW, 18 + a, a))
    index = jnp.where(row == LAST_LOW, 26, jnp.where(row == LAST_HIGH, 8, index))
    by_x, by_y, by_z = digits(index)
    in_y, in_z = by_y == 2 * (1 - side_y), by_z == 2 * (1 - side_z)
    half_y = in_y & ((face == 0) | (b == 7 * side_y))
    half_z = in_z & ((face == 1) | (b == 7 * side_z))
    low = (by_x == 2) & (column == 0) & (a == 0)
    high = (by_x == 0) & (column == 1) & (a == HALF - 1)
    half_x = (row >= LOW) | low | high
    share = jnp.where(half_y, 0.5, 1.0) * jnp.where(half_z, 0.5, 1.0) * jnp.where(half_x, 0.5, 1.0)
    held = (row <= HIGH) | ((row == LAST_LOW) & (a == 7)) | ((row == LAST_HIGH) & (a == 0))
    return jnp.where(held, share, 0.0)


def chosen_table():
    shape = (64, POOLED)
    target, block = ids(shape, 0), ids(shape, 1) >> 3
    second = (target >= Q).astype(jnp.int32)
    wanted = jnp.where(target < LOW, 2 * (target - Q * second) + second, -1)
    wanted = jnp.where(target == LOW, 54, jnp.where(target == HIGH, 56, wanted))
    wanted = jnp.where(target == LAST_LOW, 55, jnp.where(target == LAST_HIGH, 57, wanted))
    return (wanted == block).astype(F32).astype(BF16)


def ghost_table():
    side_y, side_z = sides()
    shape = (LANES, LANES)
    face, a, b = record_ids(shape, 0)
    lanes = ids(shape, 1)
    y, z = lanes >> 4, lanes & 15
    parts = [jnp.where((face == 0) & (y == 7 * side_y), interp(z, b), 0.0)]
    for h in range(2):
        parts.append(jnp.where((face == 1) & (z == 15 * side_z), interp(y + HALF * h, b), 0.0))
    return jnp.concatenate(parts, 1).astype(BF16)


def part_table():
    side_y, side_z = sides()
    shape = (LANES, LANES)
    face, a, b = record_ids(shape, 0)
    to_face, to_a, to_b = record_ids(shape, 1)
    along_x = 0.125 * (interp(2 * to_a, a) + interp(2 * to_a + 1, a))
    across = along_x * (interp(2 * to_b, b) + interp(2 * to_b + 1, b))
    zero = jnp.zeros(shape, jnp.int32)
    out_y, out_z = zero + 15 * side_y, zero + 15 * side_z
    next_y, next_z = zero + 1 + 13 * side_y, zero + 1 + 13 * side_z
    edge_y, edge_z = to_b == 7 * side_y, to_b == 7 * side_z
    line_y = along_x * interp(out_y, b)
    both_y = line_y + along_x * interp(next_y, b)
    both_z = along_x * (interp(out_z, b) + interp(next_z, b))
    in_y = jnp.where(to_face == 0, across, jnp.where(edge_y, both_z, 0.0))
    in_z = jnp.where(to_face == 1, across, jnp.where(edge_z, both_y, 0.0))
    ends = ((to_face == 0) & edge_z) | ((to_face == 1) & edge_y)
    shared = jnp.where(ends, line_y, 0.0)
    parts = [jnp.where(face == 0, in_y, 0.0), jnp.where(face == 1, in_z, 0.0), jnp.where(face == 1, shared, 0.0)]
    return jnp.concatenate(parts, 1).astype(BF16)


def along(table, axis, line):
    out = {}
    for first in range(3):
        for second in range(3):
            keys = []
            for third in range(3):
                key = [first, second]
                key.insert(axis, third)
                keys.append(tuple(key))
            values = line(*[table[key] for key in keys])
            for key, value in zip(keys, values):
                out[key] = value
    return out


def line_moments(low, mid, high):
    both = low + high
    return both + 4.0 * mid, high - low, both


def line_inverse(zeroth, first, second):
    return second - first, zeroth - 0.5 * second, first + second


def collide_cells(current, rates):
    table = {PAIRS[i]: current[i] for i in range(Q)}
    moments = table
    for axis in range(3):
        moments = along(moments, axis, line_moments)
    density = moments[0, 0, 0]
    inverse = 1.0 / density
    flow = [moments[1, 0, 0], moments[0, 1, 0], moments[0, 0, 1]]
    speed = [part * inverse for part in flow]
    carried = [density * part for part in speed]
    square = [carried[axis] * speed[axis] for axis in range(3)]
    third = density * (1.0 / 3.0)
    relaxed = {}
    for index, key in enumerate(PAIRS):
        ones = [axis for axis in range(3) if key[axis] == 1]
        twos = [axis for axis in range(3) if key[axis] == 2]
        scale = (1.0 / 3.0) ** len(twos)
        if len(ones) == 0:
            if len(twos) == 0:
                balance = density
            elif len(twos) == 1:
                balance = third + square[twos[0]]
            elif len(twos) == 2:
                balance = (third + square[twos[0]] + square[twos[1]]) * (1.0 / 3.0)
            else:
                balance = (third + square[0] + square[1] + square[2]) * (1.0 / 9.0)
        elif len(ones) == 1:
            balance = carried[ones[0]] * scale if twos else carried[ones[0]]
        elif len(ones) == 2:
            balance = carried[ones[0]] * speed[ones[1]]
            balance = balance * scale if twos else balance
        else:
            balance = None
        rest = moments[key] if balance is None else moments[key] - balance
        relaxed[key] = rates[index] * rest
    change = relaxed
    for axis in range(3):
        change = along(change, axis, line_inverse)
    return [current[i] - change[PAIRS[i]] for i in range(Q)]


def collide_kernel(
    g_hbm, solid_hbm, rates_hbm, w_ref, y_ref, z_ref, g_ref, solid_ref, rates_ref, sems
):
    pieces = 4
    size = SPAN // pieces
    copies = [
        pltpu.make_async_copy(rates_hbm, rates_ref, sems.at[pieces]),
        pltpu.make_async_copy(solid_hbm, solid_ref, sems.at[pieces + 1]),
    ]
    for piece in range(pieces):
        rows = pl.ds(size * piece, size)
        copies.append(
            pltpu.make_async_copy(g_hbm.at[:, rows, :], g_ref.at[:, rows, :], sems.at[piece])
        )
    for copy in copies:
        copy.start()
    side_y, side_z = sides()
    copies[0].wait()
    rates = []
    for i in range(Q):
        scale = 1.0 / 216.0
        for part in PAIRS[i]:
            scale *= 1.5 if part == 0 else 3.0
        rates.append(rates_ref[i] * scale)
    copies[1].wait()

    def chunk(index, carry):
        row = pl.multiple_of(8 * index, 8)
        current = [g_ref[i, pl.ds(row, 8), :] for i in range(Q)]
        solid = solid_ref[pl.ds(row, 8), :] == 1
        collided = collide_cells(current, rates)
        for i in range(Q):
            w_ref[i, pl.ds(row, 8), :] = jnp.where(solid, current[Q - 1 - i], collided[i])
        return carry

    for piece in range(pieces):
        copies[2 + piece].wait()
        lax.fori_loop(size // 8 * piece, size // 8 * (piece + 1), chunk, 0)

    send_y, send_z = 2 * (1 - side_y), 2 * (1 - side_z)
    tile, base, inner = geometry()
    lanes = ids((NX, LANES), 1)
    packed = [jnp.zeros((NX, LANES), F32), jnp.zeros((NX, LANES), F32)]
    for k in range(9):
        index = 9 * (k // 3) + 3 * send_y + k % 3
        value = w_ref[index, pl.ds(tile, NX, stride=2), :]
        value = rolled(value, (16 * (k % 8) - base) & 127)
        packed[k // 8] = jnp.where(lanes >> 4 == k % 8, value, packed[k // 8])
    y_ref[0] = (packed[0] - 1.0).astype(BF16)
    y_ref[1] = (packed[1] - 1.0).astype(BF16)
    lanes = ids((SPAN, LANES), 1)
    packed_z = jnp.zeros((SPAN, LANES), F32)
    for k in range(9):
        index = 9 * (k // 3) + 3 * (k % 3) + send_z
        value = w_ref[index]
        packed_z = jnp.where(lanes & 15 == k, rolled(value, (k - inner) & 127), packed_z)
    z_ref[...] = (packed_z - 1.0).astype(BF16)


def moved(value, b, shift):
    value = rolled(value, shift)
    if b == 1:
        return value
    rows, lanes = ids(value.shape, 0), ids(value.shape, 1)
    if b == 2:
        other = pltpu.roll(value, 1, 0)
        return jnp.where(lanes >= 16, value, jnp.where(rows & 1 == 1, other, 0.0))
    other = pltpu.roll(value, value.shape[0] - 1, 0)
    return jnp.where(lanes < 112, value, jnp.where(rows & 1 == 0, other, 0.0))


def z_inside(lanes, c):
    return lanes & 15 <= 14 if c == 0 else lanes & 15 >= 1


def stream_kernel(
    w_ref, coarse_hbm, t_ref, e_ref, pool_ref, share_ref, rec_ref, p_ref, chosen_ref, coarse_ref, sem
):
    copy = pltpu.make_async_copy(coarse_hbm, coarse_ref, sem)
    copy.start()
    lanes = ids((8, LANES), 1)
    zeros = jnp.zeros((8, LANES), F32)
    for i, (a, b, c) in enumerate(PAIRS):
        for row in (0, 8, SPAN, SPAN + 8):
            t_ref[pl.ds(PITCH * i + row, 8), :] = zeros
        shift = (16 * (b - 1) + c - 1) % 128
        for row in range(0, SPAN, 8):
            value = w_ref[i, pl.ds(row, 8), :]
            if shift:
                value = moved(value, b, shift)
            if c != 1:
                value = jnp.where(z_inside(lanes, c), value, 0.0)
            t_ref[pl.ds(PITCH * i + FIRST + row + 2 * (a - 1), 8), :] = value

    side_y, side_z = sides()
    tile, base, inner = geometry()
    lanes = ids((NX, LANES), 1)
    packed = jnp.zeros((NX, LANES), F32)
    for a in range(3):
        index = 9 * a + 6 * (1 - side_y) + 2 * (1 - side_z)
        value = w_ref[index, pl.ds(tile, NX, stride=2), :]
        packed = jnp.where(lanes == a, rolled(value, (a - base - inner) & 127), packed)
    e_ref[...] = packed

    p_ref[...] = jnp.zeros((64, LANES), F32)
    copy.wait()
    records = coarse_ref[0].astype(F32)
    for t in range(2):
        for i in range(Q):
            p_ref[32 * t + i : 32 * t + i + 1, :] = records[t : t + 1, LANES * i : LANES * (i + 1)]
    in_y, in_z = 2 * (1 - side_y), 2 * (1 - side_z)
    first = ids((1, LANES), 1) < 64
    rec_ref[...] = jnp.zeros((32, LANES), F32)
    for t in range(2):
        for k in range(9):
            for_y = p_ref[pl.ds(32 * t + 9 * (k // 3) + 3 * in_y + k % 3, 1), :]
            for_z = p_ref[pl.ds(32 * t + 9 * (k // 3) + 3 * (k % 3) + in_z, 1), :]
            row = RECORDS - MIXED + 9 * t + k
            rec_ref[row : row + 1, :] = jnp.where(first, for_y, for_z)

    pool_ref[...] = pool_table()
    share_ref[...] = share_table()
    chosen_ref[...] = chosen_table()


def halo_kernel(
    t_ref, y_ref, z_ref, e_ref, rec_ref, pool_ref, share_ref, p_ref, chosen_ref,
    out_ref, right_ref, left_ref, pay_ref, kept_ref,
):
    del t_ref
    kept_ref[...] = p_ref[...]
    side_y, side_z = sides()
    halo_y, halo_z = 2 * side_y, 2 * side_z
    tile, base, inner = geometry()

    lanes = ids((NX, LANES), 1)
    row_mask = lanes >> 4 == base >> 4
    for k in range(9):
        a, c = k // 3, k % 3
        value = rolled(y_ref[k // 8].astype(F32) + 1.0, (base - 16 * (k % 8) + c - 1) & 127)
        mask = row_mask if c == 1 else row_mask & z_inside(lanes, c)
        index = 9 * a + 3 * halo_y + c
        rows = pl.ds(PITCH * index + FIRST + 2 * (a - 1) + tile, NX, stride=2)
        out_ref[rows, :] = out_ref[rows, :] + jnp.where(mask, value, 0.0)
    lanes = ids((TILE, LANES), 1)
    for k in range(9):
        a, b = k // 3, k % 3
        shift = (inner - k + 16 * (b - 1)) & 127
        index = 9 * a + 3 * b + halo_z
        for row in range(0, SPAN, TILE):
            value = moved(z_ref[row : row + TILE].astype(F32) + 1.0, b, shift)
            rows = pl.ds(PITCH * index + FIRST + row + 2 * (a - 1), TILE)
            out_ref[rows, :] = out_ref[rows, :] + jnp.where(lanes & 15 == inner, value, 0.0)

    for k in range(9):
        right_ref[2 * k : 2 * k + 2, :] = out_ref[pl.ds(PITCH * (18 + k) + FIRST + SPAN, 2), :]
        left_ref[2 * k : 2 * k + 2, :] = out_ref[pl.ds(PITCH * k + FIRST - 2, 2), :]
    right_ref[24:ENDS, :] = e_ref[NX - 8 : NX, :]
    left_ref[24:ENDS, :] = e_ref[0:8, :]

    row_8 = ids((8, LANES), 0)
    tiles = []
    for h in range(2):
        parts = []
        for i in range(Q):
            for s in range(2):
                row = PITCH * i + FIRST + NX * s + h
                parts.append(
                    out_ref[pl.ds(row, 8, stride=4), :] + out_ref[pl.ds(row + 2, 8, stride=4), :]
                )
        over, under = FIRST + SPAN + h, FIRST - 2 + h
        parts.append(out_ref[pl.ds(PITCH * 18 + over, 8, stride=PITCH), :])
        last = out_ref[pl.ds(PITCH * 19 + over, 8, stride=PITCH), :]
        parts.append(jnp.where(row_8 == 7, last, 0.0))
        parts.append(out_ref[pl.ds(under, 8, stride=PITCH), :])
        parts.append(out_ref[pl.ds(PITCH * 8 + under, 8, stride=PITCH), :])
        tiles.append(jnp.concatenate(parts, 0))
    pool = pool_ref[...]
    high, low = split_bf16(jnp.concatenate(tiles, 1))
    pooled = dot(high, pool) + dot(low, pool)
    pooled = jnp.where(ids((POOLED, LANES), 0) & 7 == ids((POOLED, LANES), 1) >> 3 & 7, pooled, 0.0)
    chosen = chosen_ref[...]
    high, low = split_bf16(pooled)
    routed = dot(chosen, high) + dot(chosen, low)

    share = share_ref[...]
    rows, lane_a = ids((64, LANES), 0), ids((64, LANES), 1) >> 3 & 7
    inside = rows < LOW
    held = jnp.sum(jnp.where(inside, routed, 0.0), axis=0, keepdims=True)
    held = jnp.sum(held, axis=1, keepdims=True)
    parts = jnp.sum(jnp.where(inside, share, 0.0), axis=0, keepdims=True)
    parts = jnp.sum(parts, axis=1, keepdims=True)
    centre = (held / parts).astype(BF16).astype(F32)
    routed = routed - centre * share
    is_centre = (rows == CENTRE) | ((rows == LAST_LOW) & (lane_a == 6)) | ((rows == LAST_HIGH) & (lane_a == 1))
    routed = jnp.where(is_centre, centre, routed)
    payload = jnp.where(rows[MIXED:64] >= RECORDS, rec_ref[0:16], routed[MIXED:64])
    payload = jnp.concatenate([routed[0:MIXED], payload, rec_ref[16:32]], 0).astype(BF16)
    for slot in range(PLANE):
        pay_ref[slot] = payload


def tables_kernel(p_ref, pairs_ref, ghost_ref, line_ref, own_ref, route_ref, last_ref, flag_ref):
    side_y, side_z = sides()
    ghost = ghost_table()
    ghost_ref[0:LANES] = ghost
    ghost_ref[LANES : 2 * LANES] = ghost
    shape = (EDGE, LANES)
    line_ref[...] = interp(ids(shape, 0), record_ids(shape, 1)[1])

    part = dot(p_ref[...].astype(BF16), part_table())
    _, by_y, by_z = digits(ids((32, LANES), 0))
    in_y, in_z = by_y == 2 * (1 - side_y), by_z == 2 * (1 - side_z)
    for t in range(2):
        rows = part[32 * t : 32 * t + 32]
        value = jnp.where(in_y, rows[:, 0:128], 0.0) + jnp.where(in_z, rows[:, 128:256], 0.0)
        own_ref[32 * t : 32 * t + 32] = value - jnp.where(in_y & in_z, rows[:, 256:384], 0.0)

    me = lax.axis_index("blocks")
    pairs = pairs_ref[...]
    rows, lanes = ids((LANES, LANES), 0), ids((LANES, LANES), 1)

    def total(mask, value):
        value = jnp.where(mask, value.astype(F32), 0.0)
        value = jnp.sum(value, axis=1, keepdims=True)
        return jnp.broadcast_to(value, mask.shape).astype(jnp.int32)

    def matrices(ref, owner, holder, source, rows, lanes):
        place = rows & (TILE - 1)
        low = (place == LOW - MIXED) | (place == LAST_LOW - MIXED)
        high = (place == HIGH - MIXED) | (place == LAST_HIGH - MIXED)
        mixed = jnp.where(low, owner - 1, jnp.where(high, owner + 1, owner))
        mixed = jnp.where(place >= RECORDS - MIXED, holder, mixed)
        for kind, route in enumerate((owner, mixed, holder)):
            chosen = (source(route) == lanes >> 4) & (place == lanes & (TILE - 1))
            ref[kind] = chosen.astype(F32).astype(BF16)

    device = PLANE * ((rows >> 4) + TURN & (PLANE - 1)) + (me & (PLANE - 1))
    pairs = jnp.broadcast_to(pairs, (LANES, LANES))
    owner = total(lanes == 2 * device, pairs >> 1)
    holder = total(pairs == 2 * device, lanes >> 1)
    matrices(route_ref, owner, holder, lambda route: route & (PLANE - 1), rows, lanes)
    rows, lanes, pairs = rows[0:TILE], lanes[0:TILE], pairs[0:TILE]
    serves = total(lanes == 2 * me, pairs)
    record = total(pairs == 2 * me, lanes)
    matrices(last_ref, serves >> 1, record >> 1, lambda route: (route >> 3) - TURN & (PLANE - 1), rows, lanes)
    flag_ref[...] = jnp.where(rows[0:8] == 0, record[0:8] & 1, serves[0:8] & 1)


def passed_on(matrix_ref, in_ref):
    for start in range(0, ROWS, TILE):
        kind = 0 if start < MIXED else 1 if start == MIXED else 2
        tile = [in_ref[member, start : start + TILE] for member in range(PLANE)]
        yield start, dot(matrix_ref[kind], jnp.concatenate(tile, 0))


def route_kernel(route_ref, in_ref, e_ref, right_ref, left_ref, out_ref, edge_ref):
    for start, rows in passed_on(route_ref, in_ref):
        rows = rows.astype(BF16)
        for plane in range(PLANE):
            out_ref[plane, start : start + TILE] = rows[TILE * plane : TILE * (plane + 1)]
    edge_ref[0:NX, :] = e_ref[...]
    edge_ref[NX : NX + 8, :] = right_ref[24:ENDS, :]
    edge_ref[NX + 8 : NX + 16, :] = left_ref[24:ENDS, :]


def merge_kernel(t_ref, e_ref, right_ref, left_ref, next_ref):
    side_y, side_z = sides()
    tile, base, inner = geometry()
    for i in range(Q):
        next_ref[i] = t_ref[PITCH * i + FIRST : PITCH * i + FIRST + SPAN, :]
    for k in range(9):
        next_ref[18 + k, 0:2] = next_ref[18 + k, 0:2] + right_ref[2 * k : 2 * k + 2, :]
        next_ref[k, SPAN - 2 : SPAN] = next_ref[k, SPAN - 2 : SPAN] + left_ref[2 * k : 2 * k + 2, :]
    rows, lanes = ids((NX, LANES), 0), ids((NX, LANES), 1)
    corner = e_ref[0:NX, :]
    low = jnp.where(rows == 0, e_ref[NX + 7 : NX + 8, :], pltpu.roll(corner, 1, 0))
    high = jnp.where(rows == NX - 1, e_ref[NX + 8 : NX + 9, :], pltpu.roll(corner, NX - 1, 0))
    for a, value in ((0, high), (1, corner), (2, low)):
        index = 9 * a + 6 * side_y + 2 * side_z
        value = rolled(value, (base + inner - a) & 127)
        at = pl.ds(tile, NX, stride=2)
        next_ref[index, at, :] = next_ref[index, at, :] + jnp.where(lanes == base + inner, value, 0.0)


def finish_kernel(
    base_ref, in_ref, last_ref, flag_ref, own_ref, line_ref, share_ref, ghost_ref,
    value_ref, next_hbm, update_hbm,
    update_ref, sems,
):
    del base_ref
    side_y, side_z = sides()
    in_y, in_z = 2 * (1 - side_y), 2 * (1 - side_z)
    copies = []

    def send(source, target):
        copy = pltpu.make_async_copy(source, target, sems.at[len(copies)])
        copy.start()
        copies.append(copy)

    rows = jnp.concatenate([tile for _, tile in passed_on(last_ref, in_ref)], 0)
    swap = flag_ref[0:1, :] == 1
    lines = line_ref[...]
    scaled = []
    for k in range(9):
        row = RECORDS + k
        first, second = rows[row : row + 1], rows[row + 9 : row + 10]
        scaled.append(lines * jnp.where(swap, second, first))
        scaled.append(lines * jnp.where(swap, first, second))
    scaled = jnp.concatenate(scaled, 0)
    ghost = dot(jnp.concatenate(split_bf16(scaled), 1), ghost_ref[...])
    lanes = ids((NX, LANES), 1)
    outer = lanes >> 4 == 7 * side_y
    for a in range(3):
        for b in range(3):
            k = 3 * a + b
            for h in range(2):
                at = pl.ds(h, NX, stride=2)
                part = ghost[NX * k : NX * (k + 1), LANES * (h + 1) : LANES * (h + 2)]
                value_ref[9 * a + 3 * b + in_z, at, :] = value_ref[9 * a + 3 * b + in_z, at, :] + part
        for c in range(3):
            k = 3 * a + c
            at = pl.ds(side_y, NX, stride=2)
            part = ghost[NX * k : NX * (k + 1), 0:LANES]
            value = value_ref[9 * a + 3 * in_y + c, at, :]
            value_ref[9 * a + 3 * in_y + c, at, :] = jnp.where(outer, part, value)
        send(value_ref.at[pl.ds(9 * a, 9)], next_hbm.at[pl.ds(9 * a, 9)])

    share = share_ref[...]
    lane_1 = ids((1, LANES), 1)
    low_centre = jnp.sum(jnp.where(lane_1 == 48, rows[LAST_LOW : LAST_LOW + 1], 0.0), axis=1, keepdims=True)
    high_centre = jnp.sum(jnp.where(lane_1 == 8, rows[LAST_HIGH : LAST_HIGH + 1], 0.0), axis=1, keepdims=True)
    main = rows[0:LOW] + rows[CENTRE : CENTRE + 1] * share[0:LOW]
    low, high, last_low, last_high = (
        rows[row : row + 1] + centre * share[row : row + 1]
        for row, centre in (
            (LOW, low_centre), (HIGH, high_centre), (LAST_LOW, low_centre), (LAST_HIGH, high_centre)
        )
    )
    row, lane_a = ids((32, LANES), 0), ids((32, LANES), 1) >> 3 & 7
    from_low = jnp.where(row - 18 == lane_a, low, 0.0)
    from_low = jnp.where(row == 26, jnp.where(lane_a == 7, last_low, 0.0), from_low)
    from_high = jnp.where(row == lane_a, high, 0.0)
    from_high = jnp.where(row == 8, jnp.where(lane_a == 0, last_high, 0.0), from_high)
    lane_in, lane_out = ids((LANES, LANES), 0), ids((LANES, LANES), 1)
    alike = (lane_in >> 6 == lane_out >> 6) & (lane_in & 7 == lane_out & 7)
    alike = alike.astype(F32).astype(BF16)
    edges = jnp.zeros((2 * 32, LANES), F32)
    for part in split_bf16(jnp.concatenate([from_low, from_high], 0)):
        edges = edges + dot(part, alike)
    column_0 = main[0:Q] + jnp.where(lane_a == 0, edges[0:32], 0.0)[0:Q]
    column_1 = main[Q : 2 * Q] + jnp.where(lane_a == HALF - 1, edges[32:64], 0.0)[0:Q]
    crossed = jnp.broadcast_to(flag_ref[1:2, :], (Q, LANES)) == 1
    for t in range(2):
        here, there = (column_0, column_1) if t == 0 else (column_1, column_0)
        value = jnp.where(crossed, there, here) + own_ref[32 * t : 32 * t + Q, :]
        for i in range(Q):
            update_ref[0, t : t + 1, LANES * i : LANES * (i + 1)] = value[i : i + 1]
    send(update_ref, update_hbm)
    for copy in copies:
        copy.wait()


VMEM = pl.BlockSpec(memory_space=pltpu.VMEM)
HBM = pl.BlockSpec(memory_space=pltpu.HBM)


def call(kernel, name, results, inputs, outputs=None, scratch=(), cost=None, aliases=None, limit=32):
    return pl.pallas_call(
        kernel,
        out_shape=tuple(jax.ShapeDtypeStruct(*result) for result in results),
        in_specs=inputs,
        out_specs=outputs or (VMEM,) * len(results),
        scratch_shapes=scratch,
        input_output_aliases=aliases or {},
        compiler_params=pltpu.CompilerParams(vmem_limit_bytes=limit * 1024 * 1024),
        cost_estimate=cost,
        name=name,
    )


def in_hbm(value):
    return pltpu.with_memory_space_constraint(value, pltpu.HBM)


def swapped(block, bits):
    return lax.ppermute(block, "group", [(i, i ^ bits) for i in range(4)])


def body(populations, solid_mask, relax_rates, coarse_pops, interface_pairs):
    collided, edge_y, edge_z = call(
        collide_kernel,
        "collide",
        [((Q, SPAN, LANES), F32), ((2, NX, LANES), BF16), ((SPAN, LANES), BF16)],
        [HBM] * 3,
        scratch=[
            pltpu.VMEM((Q, SPAN, LANES), F32),
            pltpu.VMEM((SPAN, LANES), jnp.int32),
            pltpu.SMEM((Q,), F32),
            pltpu.SemaphoreType.DMA((6,)),
        ],
    )(
        in_hbm(populations.reshape(Q, SPAN, LANES)),
        in_hbm(solid_mask.reshape(SPAN, LANES)),
        in_hbm(relax_rates),
    )

    edge_z = swapped(edge_z, 2)
    edge_y = swapped(edge_y, 1)
    streamed, edge_yz, pool, share, halves, records, chosen = call(
        stream_kernel,
        "stream",
        [
            ((Q * PITCH, LANES), F32),
            ((NX, LANES), F32),
            ((256, LANES), BF16),
            ((64, LANES), F32),
            ((32, LANES), F32),
            ((64, LANES), F32),
            ((64, POOLED), BF16),
        ],
        [VMEM, HBM],
        scratch=[pltpu.VMEM((1, 2, Q * LANES), BF16), pltpu.SemaphoreType.DMA(())],
        cost=pl.CostEstimate(flops=10_000_000, bytes_accessed=8_000_000, transcendentals=0),
    )(collided, in_hbm(coarse_pops))

    streamed, right, left, payload, records = call(
        halo_kernel,
        "halo",
        [
            ((Q * PITCH, LANES), F32),
            ((ENDS, LANES), F32),
            ((ENDS, LANES), F32),
            ((PLANE, ROWS, LANES), BF16),
            ((64, LANES), F32),
        ],
        [VMEM] * 9,
        aliases={0: 0},
    )(streamed, edge_y, edge_z, edge_yz, halves, pool, share, records, chosen)

    near = [[PLANE * i + j for j in range(PLANE)] for i in range(PLANE)]
    far = [[PLANE * ((j + TURN) % PLANE) + i for j in range(PLANE)] for i in range(PLANE)]
    payload = lax.all_to_all(payload, "blocks", 0, 0, axis_index_groups=near, tiled=True)
    ring = [(i, (i + 1) % BLOCKS) for i in range(BLOCKS)]
    right = lax.ppermute(right, "blocks", ring)
    left = lax.ppermute(left, "blocks", [(b, a) for a, b in ring])
    ghost, line, own, route, last, flags = call(
        tables_kernel,
        "tables",
        [
            ((256, 384), BF16),
            ((EDGE, LANES), F32),
            ((64, LANES), F32),
            ((3, LANES, LANES), BF16),
            ((3, TILE, LANES), BF16),
            ((8, LANES), jnp.int32),
        ],
        [VMEM] * 2,
        cost=pl.CostEstimate(flops=1_000_000, bytes_accessed=4_000_000, transcendentals=0),
    )(records, interface_pairs)
    payload, edge_yz = call(
        route_kernel,
        "route",
        [((PLANE, ROWS, LANES), BF16), ((NX + 16, LANES), F32)],
        [VMEM] * 5,
    )(route, payload, edge_yz, right, left)
    payload = lax.all_to_all(payload, "blocks", 0, 0, axis_index_groups=far, tiled=True)
    edge_yz = swapped(edge_yz, 3)
    merged = call(
        merge_kernel,
        "merge",
        [((Q, SPAN, LANES), F32)],
        [VMEM] * 4,
        cost=pl.CostEstimate(flops=1_000_000, bytes_accessed=4_000_000, transcendentals=0),
    )(streamed, edge_yz, right, left)[0]
    _, result, update = call(
        finish_kernel,
        "finish",
        [((Q, SPAN, LANES), F32), ((Q, SPAN, LANES), F32), ((1, 2, Q * LANES), F32)],
        [VMEM] * 8,
        (VMEM, HBM, HBM),
        [pltpu.VMEM((1, 2, Q * LANES), F32), pltpu.SemaphoreType.DMA((4,))],
        aliases={0: 0},
    )(merged, payload, last, flags, own, line, share, ghost)
    return result.reshape(1, Q, SPAN * LANES), update


def solution(mesh):
    placed = (
        P("group", None, "blocks"),
        P("group", "blocks"),
        P(),
        P("group", "blocks", None),
        P("group", None),
    )
    return jax.shard_map(
        body,
        mesh=mesh,
        in_specs=placed,
        out_specs=(P("group", None, "blocks"), P("group", "blocks", None)),
        check_vma=False,
    )
```

```python
import jax
import jax.numpy as jnp
from jax import lax
from jax.experimental import pallas as pl
from jax.experimental.pallas import tpu as pltpu
from jax.sharding import PartitionSpec as P

Q = 27
EDGE = 16
HALF = 8
NX = 32
SPAN = 2 * NX
PITCH = SPAN + 16
FIRST = 8
LANES = 128
PLANE = 8
BLOCKS = PLANE * PLANE
TURN = 5
LOW, HIGH, LAST_LOW, LAST_HIGH, CENTRE, RECORDS, ROWS = 54, 55, 56, 57, 58, 62, 80
TILE = 16
MIXED = 48
POOLED = 8 * (2 * Q + 4)
ENDS = 32
PAIRS = [(i // 9, i // 3 % 3, i % 3) for i in range(Q)]
F32 = jnp.float32
BF16 = jnp.bfloat16


def sides():
    position = lax.axis_index("group")
    return position & 1, position >> 1


def geometry():
    side_y, side_z = sides()
    return 1 - side_y, 112 * (1 - side_y), 15 * (1 - side_z)


def ids(shape, dim):
    return lax.broadcasted_iota(jnp.int32, shape, dim)


def rolled(value, shift):
    return pltpu.roll(value, shift, 1)


def split_bf16(value):
    high = value.astype(BF16)
    return high, (value - high.astype(F32)).astype(BF16)


def dot(left, right):
    return jnp.dot(left, right, preferred_element_type=F32)


def record_ids(shape, dim):
    value = ids(shape, dim) & 127
    return value >> 6, value >> 3 & 7, value & 7


def digits(index):
    third, ninth = index * 11 >> 5, index * 57 >> 9
    return ninth, third - 3 * ninth, index - 3 * third


def interp(fine, coarse):
    weight = 1.0 - jnp.abs(0.5 * fine.astype(F32) - 0.25 - coarse.astype(F32))
    end = (fine == 0) | (fine == EDGE - 1)
    return jnp.where(weight > 0.0, jnp.where(end, 1.0, weight), 0.0)


def pool_table():
    side_y, side_z = sides()
    shape = (256, LANES)
    cell = ids(shape, 0)
    pair_y, pair_z = cell >> 5, cell >> 1 & 7
    face, a, b = record_ids(shape, 1)
    on_y = (pair_y == 7 * side_y) & (pair_z == b)
    on_z = (pair_z == 7 * side_z) & (pair_y == b)
    return jnp.where(((face == 0) & on_y) | ((face == 1) & on_z), 0.125, 0.0).astype(BF16)


def share_table():
    side_y, side_z = sides()
    shape = (64, LANES)
    row = ids(shape, 0)
    face, a, b = record_ids(shape, 1)
    column = (row >= Q).astype(jnp.int32)
    index = jnp.where(row < LOW, row - Q * column, jnp.where(row == LOW, 18 + a, a))
    index = jnp.where(row == LAST_LOW, 26, jnp.where(row == LAST_HIGH, 8, index))
    by_x, by_y, by_z = digits(index)
    in_y, in_z = by_y == 2 * (1 - side_y), by_z == 2 * (1 - side_z)
    half_y = in_y & ((face == 0) | (b == 7 * side_y))
    half_z = in_z & ((face == 1) | (b == 7 * side_z))
    low = (by_x == 2) & (column == 0) & (a == 0)
    high = (by_x == 0) & (column == 1) & (a == HALF - 1)
    half_x = (row >= LOW) | low | high
    share = jnp.where(half_y, 0.5, 1.0) * jnp.where(half_z, 0.5, 1.0) * jnp.where(half_x, 0.5, 1.0)
    held = (row <= HIGH) | ((row == LAST_LOW) & (a == 7)) | ((row == LAST_HIGH) & (a == 0))
    return jnp.where(held, share, 0.0)


def chosen_table():
    shape = (64, POOLED)
    target, block = ids(shape, 0), ids(shape, 1) >> 3
    second = (target >= Q).astype(jnp.int32)
    wanted = jnp.where(target < LOW, 2 * (target - Q * second) + second, -1)
    wanted = jnp.where(target == LOW, 54, jnp.where(target == HIGH, 56, wanted))
    wanted = jnp.where(target == LAST_LOW, 55, jnp.where(target == LAST_HIGH, 57, wanted))
    return (wanted == block).astype(F32).astype(BF16)


def ghost_table():
    side_y, side_z = sides()
    shape = (LANES, LANES)
    face, a, b = record_ids(shape, 0)
    lanes = ids(shape, 1)
    y, z = lanes >> 4, lanes & 15
    parts = [jnp.where((face == 0) & (y == 7 * side_y), interp(z, b), 0.0)]
    for h in range(2):
        parts.append(jnp.where((face == 1) & (z == 15 * side_z), interp(y + HALF * h, b), 0.0))
    return jnp.concatenate(parts, 1).astype(BF16)


def part_table():
    side_y, side_z = sides()
    shape = (LANES, LANES)
    face, a, b = record_ids(shape, 0)
    to_face, to_a, to_b = record_ids(shape, 1)
    along_x = 0.125 * (interp(2 * to_a, a) + interp(2 * to_a + 1, a))
    across = along_x * (interp(2 * to_b, b) + interp(2 * to_b + 1, b))
    zero = jnp.zeros(shape, jnp.int32)
    out_y, out_z = zero + 15 * side_y, zero + 15 * side_z
    next_y, next_z = zero + 1 + 13 * side_y, zero + 1 + 13 * side_z
    edge_y, edge_z = to_b == 7 * side_y, to_b == 7 * side_z
    line_y = along_x * interp(out_y, b)
    both_y = line_y + along_x * interp(next_y, b)
    both_z = along_x * (interp(out_z, b) + interp(next_z, b))
    in_y = jnp.where(to_face == 0, across, jnp.where(edge_y, both_z, 0.0))
    in_z = jnp.where(to_face == 1, across, jnp.where(edge_z, both_y, 0.0))
    ends = ((to_face == 0) & edge_z) | ((to_face == 1) & edge_y)
    shared = jnp.where(ends, line_y, 0.0)
    parts = [jnp.where(face == 0, in_y, 0.0), jnp.where(face == 1, in_z, 0.0), jnp.where(face == 1, shared, 0.0)]
    return jnp.concatenate(parts, 1).astype(BF16)


def along(table, axis, line):
    out = {}
    for first in range(3):
        for second in range(3):
            keys = []
            for third in range(3):
                key = [first, second]
                key.insert(axis, third)
                keys.append(tuple(key))
            values = line(*[table[key] for key in keys])
            for key, value in zip(keys, values):
                out[key] = value
    return out


def line_moments(low, mid, high):
    both = low + high
    return both + 4.0 * mid, high - low, both


def line_inverse(zeroth, first, second):
    return second - first, zeroth - 0.5 * second, first + second


def collide_cells(current, rates):
    table = {PAIRS[i]: current[i] for i in range(Q)}
    moments = table
    for axis in range(3):
        moments = along(moments, axis, line_moments)
    density = moments[0, 0, 0]
    inverse = 1.0 / density
    flow = [moments[1, 0, 0], moments[0, 1, 0], moments[0, 0, 1]]
    speed = [part * inverse for part in flow]
    carried = [density * part for part in speed]
    square = [carried[axis] * speed[axis] for axis in range(3)]
    third = density * (1.0 / 3.0)
    relaxed = {}
    for index, key in enumerate(PAIRS):
        ones = [axis for axis in range(3) if key[axis] == 1]
        twos = [axis for axis in range(3) if key[axis] == 2]
        scale = (1.0 / 3.0) ** len(twos)
        if len(ones) == 0:
            if len(twos) == 0:
                balance = density
            elif len(twos) == 1:
                balance = third + square[twos[0]]
            elif len(twos) == 2:
                balance = (third + square[twos[0]] + square[twos[1]]) * (1.0 / 3.0)
            else:
                balance = (third + square[0] + square[1] + square[2]) * (1.0 / 9.0)
        elif len(ones) == 1:
            balance = carried[ones[0]] * scale if twos else carried[ones[0]]
        elif len(ones) == 2:
            balance = carried[ones[0]] * speed[ones[1]]
            balance = balance * scale if twos else balance
        else:
            balance = None
        rest = moments[key] if balance is None else moments[key] - balance
        relaxed[key] = rates[index] * rest
    change = relaxed
    for axis in range(3):
        change = along(change, axis, line_inverse)
    return [current[i] - change[PAIRS[i]] for i in range(Q)]


def collide_kernel(
    g_hbm, solid_hbm, rates_hbm, w_ref, y_ref, z_ref, g_ref, solid_ref, rates_ref, sems
):
    pieces = 4
    size = SPAN // pieces
    copies = [
        pltpu.make_async_copy(rates_hbm, rates_ref, sems.at[pieces]),
        pltpu.make_async_copy(solid_hbm, solid_ref, sems.at[pieces + 1]),
    ]
    for piece in range(pieces):
        rows = pl.ds(size * piece, size)
        copies.append(
            pltpu.make_async_copy(g_hbm.at[:, rows, :], g_ref.at[:, rows, :], sems.at[piece])
        )
    for copy in copies:
        copy.start()
    side_y, side_z = sides()
    copies[0].wait()
    rates = []
    for i in range(Q):
        scale = 1.0 / 216.0
        for part in PAIRS[i]:
            scale *= 1.5 if part == 0 else 3.0
        rates.append(rates_ref[i] * scale)
    copies[1].wait()

    def chunk(index, carry):
        row = pl.multiple_of(8 * index, 8)
        current = [g_ref[i, pl.ds(row, 8), :] for i in range(Q)]
        solid = solid_ref[pl.ds(row, 8), :] == 1
        collided = collide_cells(current, rates)
        for i in range(Q):
            w_ref[i, pl.ds(row, 8), :] = jnp.where(solid, current[Q - 1 - i], collided[i])
        return carry

    for piece in range(pieces):
        copies[2 + piece].wait()
        lax.fori_loop(size // 8 * piece, size // 8 * (piece + 1), chunk, 0)

    send_y, send_z = 2 * (1 - side_y), 2 * (1 - side_z)
    tile, base, inner = geometry()
    lanes = ids((NX, LANES), 1)
    packed = [jnp.zeros((NX, LANES), F32), jnp.zeros((NX, LANES), F32)]
    for k in range(9):
        index = 9 * (k // 3) + 3 * send_y + k % 3
        value = w_ref[index, pl.ds(tile, NX, stride=2), :]
        value = rolled(value, (16 * (k % 8) - base) & 127)
        packed[k // 8] = jnp.where(lanes >> 4 == k % 8, value, packed[k // 8])
    y_ref[0] = (packed[0] - 1.0).astype(BF16)
    y_ref[1] = (packed[1] - 1.0).astype(BF16)
    lanes = ids((SPAN, LANES), 1)
    packed_z = jnp.zeros((SPAN, LANES), F32)
    for k in range(9):
        index = 9 * (k // 3) + 3 * (k % 3) + send_z
        value = w_ref[index]
        packed_z = jnp.where(lanes & 15 == k, rolled(value, (k - inner) & 127), packed_z)
    z_ref[...] = (packed_z - 1.0).astype(BF16)


def moved(value, b, shift):
    value = rolled(value, shift)
    if b == 1:
        return value
    rows, lanes = ids(value.shape, 0), ids(value.shape, 1)
    if b == 2:
        other = pltpu.roll(value, 1, 0)
        return jnp.where(lanes >= 16, value, jnp.where(rows & 1 == 1, other, 0.0))
    other = pltpu.roll(value, value.shape[0] - 1, 0)
    return jnp.where(lanes < 112, value, jnp.where(rows & 1 == 0, other, 0.0))


def z_inside(lanes, c):
    return lanes & 15 <= 14 if c == 0 else lanes & 15 >= 1


def stream_kernel(
    w_ref, coarse_hbm, t_ref, e_ref, pool_ref, share_ref, rec_ref, p_ref, chosen_ref, centre_ref, coarse_ref, sem
):
    copy = pltpu.make_async_copy(coarse_hbm, coarse_ref, sem)
    copy.start()
    lanes = ids((8, LANES), 1)
    zeros = jnp.zeros((8, LANES), F32)
    held = zeros
    for i, (a, b, c) in enumerate(PAIRS):
        for row in (0, 8, SPAN, SPAN + 8):
            t_ref[pl.ds(PITCH * i + row, 8), :] = zeros
        shift = (16 * (b - 1) + c - 1) % 128
        for row in range(0, SPAN, 8):
            value = w_ref[i, pl.ds(row, 8), :]
            held = held + value
            if shift:
                value = moved(value, b, shift)
            if c != 1:
                value = jnp.where(z_inside(lanes, c), value, 0.0)
            t_ref[pl.ds(PITCH * i + FIRST + row + 2 * (a - 1), 8), :] = value

    side_y, side_z = sides()
    tile, base, inner = geometry()
    lanes = ids((NX, LANES), 1)
    packed = jnp.zeros((NX, LANES), F32)
    for a in range(3):
        index = 9 * a + 6 * (1 - side_y) + 2 * (1 - side_z)
        value = w_ref[index, pl.ds(tile, NX, stride=2), :]
        packed = jnp.where(lanes == a, rolled(value, (a - base - inner) & 127), packed)
    e_ref[...] = packed

    p_ref[...] = jnp.zeros((64, LANES), F32)
    copy.wait()
    records = coarse_ref[0].astype(F32)
    for t in range(2):
        for i in range(Q):
            p_ref[32 * t + i : 32 * t + i + 1, :] = records[t : t + 1, LANES * i : LANES * (i + 1)]
    in_y, in_z = 2 * (1 - side_y), 2 * (1 - side_z)
    first = ids((1, LANES), 1) < 64
    rec_ref[...] = jnp.zeros((32, LANES), F32)
    for t in range(2):
        for k in range(9):
            for_y = p_ref[pl.ds(32 * t + 9 * (k // 3) + 3 * in_y + k % 3, 1), :]
            for_z = p_ref[pl.ds(32 * t + 9 * (k // 3) + 3 * (k % 3) + in_z, 1), :]
            row = RECORDS - MIXED + 9 * t + k
            rec_ref[row : row + 1, :] = jnp.where(first, for_y, for_z)

    pool_ref[...] = pool_table()
    share_ref[...] = share_table()
    chosen_ref[...] = chosen_table()
    held = jnp.sum(jnp.sum(held, axis=0, keepdims=True), axis=1, keepdims=True)
    centre = (held * (1.0 / (Q * SPAN * LANES))).astype(BF16).astype(F32)
    centre_ref[...] = jnp.broadcast_to(centre, (8, LANES))


def halo_kernel(
    t_ref, z_ref, y_ref, e_ref, rec_ref, pool_ref, share_ref, p_ref, chosen_ref, centre_ref,
    out_ref, right_ref, left_ref, pay_ref, kept_ref,
):
    del t_ref
    kept_ref[...] = p_ref[...]
    side_y, side_z = sides()
    halo_y, halo_z = 2 * side_y, 2 * side_z
    tile, base, inner = geometry()

    lanes = ids((NX, LANES), 1)
    row_mask = lanes >> 4 == base >> 4
    for k in range(9):
        a, c = k // 3, k % 3
        value = rolled(y_ref[k // 8].astype(F32) + 1.0, (base - 16 * (k % 8) + c - 1) & 127)
        mask = row_mask if c == 1 else row_mask & z_inside(lanes, c)
        index = 9 * a + 3 * halo_y + c
        rows = pl.ds(PITCH * index + FIRST + 2 * (a - 1) + tile, NX, stride=2)
        out_ref[rows, :] = out_ref[rows, :] + jnp.where(mask, value, 0.0)
    lanes = ids((TILE, LANES), 1)
    for k in range(9):
        a, b = k // 3, k % 3
        shift = (inner - k + 16 * (b - 1)) & 127
        index = 9 * a + 3 * b + halo_z
        for row in range(0, SPAN, TILE):
            value = moved(z_ref[row : row + TILE].astype(F32) + 1.0, b, shift)
            rows = pl.ds(PITCH * index + FIRST + row + 2 * (a - 1), TILE)
            out_ref[rows, :] = out_ref[rows, :] + jnp.where(lanes & 15 == inner, value, 0.0)

    for k in range(9):
        right_ref[2 * k : 2 * k + 2, :] = out_ref[pl.ds(PITCH * (18 + k) + FIRST + SPAN, 2), :]
        left_ref[2 * k : 2 * k + 2, :] = out_ref[pl.ds(PITCH * k + FIRST - 2, 2), :]
    right_ref[24:ENDS, :] = e_ref[NX - 8 : NX, :]
    left_ref[24:ENDS, :] = e_ref[0:8, :]

    row_8 = ids((8, LANES), 0)
    tiles = []
    for h in range(2):
        parts = []
        for i in range(Q):
            for s in range(2):
                row = PITCH * i + FIRST + NX * s + h
                parts.append(
                    out_ref[pl.ds(row, 8, stride=4), :] + out_ref[pl.ds(row + 2, 8, stride=4), :]
                )
        over, under = FIRST + SPAN + h, FIRST - 2 + h
        parts.append(out_ref[pl.ds(PITCH * 18 + over, 8, stride=PITCH), :])
        last = out_ref[pl.ds(PITCH * 19 + over, 8, stride=PITCH), :]
        parts.append(jnp.where(row_8 == 7, last, 0.0))
        parts.append(out_ref[pl.ds(under, 8, stride=PITCH), :])
        parts.append(out_ref[pl.ds(PITCH * 8 + under, 8, stride=PITCH), :])
        tiles.append(jnp.concatenate(parts, 0))
    pool = pool_ref[...]
    high, low = split_bf16(jnp.concatenate(tiles, 1))
    pooled = dot(high, pool) + dot(low, pool)
    pooled = jnp.where(ids((POOLED, LANES), 0) & 7 == ids((POOLED, LANES), 1) >> 3 & 7, pooled, 0.0)
    chosen = chosen_ref[...]
    high, low = split_bf16(pooled)
    routed = dot(chosen, high) + dot(chosen, low)

    share = share_ref[...]
    rows, lane_a = ids((64, LANES), 0), ids((64, LANES), 1) >> 3 & 7
    centre = centre_ref[0:1, :]
    routed = routed - centre * share
    is_centre = (rows == CENTRE) | ((rows == LAST_LOW) & (lane_a == 6)) | ((rows == LAST_HIGH) & (lane_a == 1))
    routed = jnp.where(is_centre, centre, routed)
    payload = jnp.where(rows[MIXED:64] >= RECORDS, rec_ref[0:16], routed[MIXED:64])
    payload = jnp.concatenate([routed[0:MIXED], payload, rec_ref[16:32]], 0).astype(BF16)
    for slot in range(PLANE):
        pay_ref[slot] = payload


def tables_kernel(p_ref, pairs_ref, ghost_ref, line_ref, own_ref, route_ref, last_ref, flag_ref):
    side_y, side_z = sides()
    ghost = ghost_table()
    ghost_ref[0:LANES] = ghost
    ghost_ref[LANES : 2 * LANES] = ghost
    shape = (EDGE, LANES)
    line_ref[...] = interp(ids(shape, 0), record_ids(shape, 1)[1])

    part = dot(p_ref[...].astype(BF16), part_table())
    _, by_y, by_z = digits(ids((32, LANES), 0))
    in_y, in_z = by_y == 2 * (1 - side_y), by_z == 2 * (1 - side_z)
    for t in range(2):
        rows = part[32 * t : 32 * t + 32]
        value = jnp.where(in_y, rows[:, 0:128], 0.0) + jnp.where(in_z, rows[:, 128:256], 0.0)
        own_ref[32 * t : 32 * t + 32] = value - jnp.where(in_y & in_z, rows[:, 256:384], 0.0)

    me = lax.axis_index("blocks")
    pairs = pairs_ref[...]
    rows, lanes = ids((LANES, LANES), 0), ids((LANES, LANES), 1)

    def total(mask, value):
        value = jnp.where(mask, value.astype(F32), 0.0)
        value = jnp.sum(value, axis=1, keepdims=True)
        return jnp.broadcast_to(value, mask.shape).astype(jnp.int32)

    def matrices(ref, owner, holder, source, rows, lanes):
        place = rows & (TILE - 1)
        low = (place == LOW - MIXED) | (place == LAST_LOW - MIXED)
        high = (place == HIGH - MIXED) | (place == LAST_HIGH - MIXED)
        mixed = jnp.where(low, owner - 1, jnp.where(high, owner + 1, owner))
        mixed = jnp.where(place >= RECORDS - MIXED, holder, mixed)
        for kind, route in enumerate((owner, mixed, holder)):
            chosen = (source(route) == lanes >> 4) & (place == lanes & (TILE - 1))
            ref[kind] = chosen.astype(F32).astype(BF16)

    device = PLANE * ((rows >> 4) + TURN & (PLANE - 1)) + (me & (PLANE - 1))
    pairs = jnp.broadcast_to(pairs, (LANES, LANES))
    owner = total(lanes == 2 * device, pairs >> 1)
    holder = total(pairs == 2 * device, lanes >> 1)
    matrices(route_ref, owner, holder, lambda route: route & (PLANE - 1), rows, lanes)
    rows, lanes, pairs = rows[0:TILE], lanes[0:TILE], pairs[0:TILE]
    serves = total(lanes == 2 * me, pairs)
    record = total(pairs == 2 * me, lanes)
    matrices(last_ref, serves >> 1, record >> 1, lambda route: (route >> 3) - TURN & (PLANE - 1), rows, lanes)
    flag_ref[...] = jnp.where(rows[0:8] == 0, record[0:8] & 1, serves[0:8] & 1)


def passed_on(matrix_ref, in_ref):
    for start in range(0, ROWS, TILE):
        kind = 0 if start < MIXED else 1 if start == MIXED else 2
        tile = [in_ref[member, start : start + TILE] for member in range(PLANE)]
        yield start, dot(matrix_ref[kind], jnp.concatenate(tile, 0))


def route_kernel(route_ref, in_ref, e_ref, right_ref, left_ref, out_ref, edge_ref):
    for start, rows in passed_on(route_ref, in_ref):
        rows = rows.astype(BF16)
        for plane in range(PLANE):
            out_ref[plane, start : start + TILE] = rows[TILE * plane : TILE * (plane + 1)]
    edge_ref[0:NX, :] = e_ref[...]
    edge_ref[NX : NX + 8, :] = right_ref[24:ENDS, :]
    edge_ref[NX + 8 : NX + 16, :] = left_ref[24:ENDS, :]


def merge_kernel(t_ref, e_ref, right_ref, left_ref, next_ref):
    side_y, side_z = sides()
    tile, base, inner = geometry()
    for i in range(Q):
        next_ref[i] = t_ref[PITCH * i + FIRST : PITCH * i + FIRST + SPAN, :]
    for k in range(9):
        next_ref[18 + k, 0:2] = next_ref[18 + k, 0:2] + right_ref[2 * k : 2 * k + 2, :]
        next_ref[k, SPAN - 2 : SPAN] = next_ref[k, SPAN - 2 : SPAN] + left_ref[2 * k : 2 * k + 2, :]
    rows, lanes = ids((NX, LANES), 0), ids((NX, LANES), 1)
    corner = e_ref[0:NX, :]
    low = jnp.where(rows == 0, e_ref[NX + 7 : NX + 8, :], pltpu.roll(corner, 1, 0))
    high = jnp.where(rows == NX - 1, e_ref[NX + 8 : NX + 9, :], pltpu.roll(corner, NX - 1, 0))
    for a, value in ((0, high), (1, corner), (2, low)):
        index = 9 * a + 6 * side_y + 2 * side_z
        value = rolled(value, (base + inner - a) & 127)
        at = pl.ds(tile, NX, stride=2)
        next_ref[index, at, :] = next_ref[index, at, :] + jnp.where(lanes == base + inner, value, 0.0)


def finish_kernel(
    base_ref, in_ref, last_ref, flag_ref, own_ref, line_ref, share_ref, ghost_ref,
    value_ref, next_hbm, update_hbm,
    update_ref, sems,
):
    del base_ref
    side_y, side_z = sides()
    in_y, in_z = 2 * (1 - side_y), 2 * (1 - side_z)
    copies = []

    def send(source, target):
        copy = pltpu.make_async_copy(source, target, sems.at[len(copies)])
        copy.start()
        copies.append(copy)

    rows = jnp.concatenate([tile for _, tile in passed_on(last_ref, in_ref)], 0)
    swap = flag_ref[0:1, :] == 1
    lines = line_ref[...]
    scaled = []
    for k in range(9):
        row = RECORDS + k
        first, second = rows[row : row + 1], rows[row + 9 : row + 10]
        scaled.append(lines * jnp.where(swap, second, first))
        scaled.append(lines * jnp.where(swap, first, second))
    scaled = jnp.concatenate(scaled, 0)
    ghost = dot(jnp.concatenate(split_bf16(scaled), 1), ghost_ref[...])
    lanes = ids((NX, LANES), 1)
    outer = lanes >> 4 == 7 * side_y
    for a in range(3):
        for b in range(3):
            k = 3 * a + b
            for h in range(2):
                at = pl.ds(h, NX, stride=2)
                part = ghost[NX * k : NX * (k + 1), LANES * (h + 1) : LANES * (h + 2)]
                value_ref[9 * a + 3 * b + in_z, at, :] = value_ref[9 * a + 3 * b + in_z, at, :] + part
        for c in range(3):
            k = 3 * a + c
            at = pl.ds(side_y, NX, stride=2)
            part = ghost[NX * k : NX * (k + 1), 0:LANES]
            value = value_ref[9 * a + 3 * in_y + c, at, :]
            value_ref[9 * a + 3 * in_y + c, at, :] = jnp.where(outer, part, value)
        send(value_ref.at[pl.ds(9 * a, 9)], next_hbm.at[pl.ds(9 * a, 9)])

    share = share_ref[...]
    lane_1 = ids((1, LANES), 1)
    low_centre = jnp.sum(jnp.where(lane_1 == 48, rows[LAST_LOW : LAST_LOW + 1], 0.0), axis=1, keepdims=True)
    high_centre = jnp.sum(jnp.where(lane_1 == 8, rows[LAST_HIGH : LAST_HIGH + 1], 0.0), axis=1, keepdims=True)
    main = rows[0:LOW] + rows[CENTRE : CENTRE + 1] * share[0:LOW]
    low, high, last_low, last_high = (
        rows[row : row + 1] + centre * share[row : row + 1]
        for row, centre in (
            (LOW, low_centre), (HIGH, high_centre), (LAST_LOW, low_centre), (LAST_HIGH, high_centre)
        )
    )
    row, lane_a = ids((32, LANES), 0), ids((32, LANES), 1) >> 3 & 7
    from_low = jnp.where(row - 18 == lane_a, low, 0.0)
    from_low = jnp.where(row == 26, jnp.where(lane_a == 7, last_low, 0.0), from_low)
    from_high = jnp.where(row == lane_a, high, 0.0)
    from_high = jnp.where(row == 8, jnp.where(lane_a == 0, last_high, 0.0), from_high)
    lane_in, lane_out = ids((LANES, LANES), 0), ids((LANES, LANES), 1)
    alike = (lane_in >> 6 == lane_out >> 6) & (lane_in & 7 == lane_out & 7)
    alike = alike.astype(F32).astype(BF16)
    edges = jnp.zeros((2 * 32, LANES), F32)
    for part in split_bf16(jnp.concatenate([from_low, from_high], 0)):
        edges = edges + dot(part, alike)
    column_0 = main[0:Q] + jnp.where(lane_a == 0, edges[0:32], 0.0)[0:Q]
    column_1 = main[Q : 2 * Q] + jnp.where(lane_a == HALF - 1, edges[32:64], 0.0)[0:Q]
    crossed = jnp.broadcast_to(flag_ref[1:2, :], (Q, LANES)) == 1
    for t in range(2):
        here, there = (column_0, column_1) if t == 0 else (column_1, column_0)
        value = jnp.where(crossed, there, here) + own_ref[32 * t : 32 * t + Q, :]
        for i in range(Q):
            update_ref[0, t : t + 1, LANES * i : LANES * (i + 1)] = value[i : i + 1]
    send(update_ref, update_hbm)
    for copy in copies:
        copy.wait()


VMEM = pl.BlockSpec(memory_space=pltpu.VMEM)
HBM = pl.BlockSpec(memory_space=pltpu.HBM)


def call(kernel, name, results, inputs, outputs=None, scratch=(), cost=None, aliases=None, limit=32):
    return pl.pallas_call(
        kernel,
        out_shape=tuple(jax.ShapeDtypeStruct(*result) for result in results),
        in_specs=inputs,
        out_specs=outputs or (VMEM,) * len(results),
        scratch_shapes=scratch,
        input_output_aliases=aliases or {},
        compiler_params=pltpu.CompilerParams(vmem_limit_bytes=limit * 1024 * 1024),
        cost_estimate=cost,
        name=name,
    )


def in_hbm(value):
    return pltpu.with_memory_space_constraint(value, pltpu.HBM)


def swapped(block, bits):
    return lax.ppermute(block, "group", [(i, i ^ bits) for i in range(4)])


def body(populations, solid_mask, relax_rates, coarse_pops, interface_pairs):
    collided, edge_y, edge_z = call(
        collide_kernel,
        "collide",
        [((Q, SPAN, LANES), F32), ((2, NX, LANES), BF16), ((SPAN, LANES), BF16)],
        [HBM] * 3,
        scratch=[
            pltpu.VMEM((Q, SPAN, LANES), F32),
            pltpu.VMEM((SPAN, LANES), jnp.int32),
            pltpu.SMEM((Q,), F32),
            pltpu.SemaphoreType.DMA((6,)),
        ],
    )(
        in_hbm(populations.reshape(Q, SPAN, LANES)),
        in_hbm(solid_mask.reshape(SPAN, LANES)),
        in_hbm(relax_rates),
    )

    edge_z = swapped(edge_z, 2)
    edge_y = swapped(edge_y, 1)
    streamed, edge_yz, pool, share, halves, records, chosen, centre = call(
        stream_kernel,
        "stream",
        [
            ((Q * PITCH, LANES), F32),
            ((NX, LANES), F32),
            ((256, LANES), BF16),
            ((64, LANES), F32),
            ((32, LANES), F32),
            ((64, LANES), F32),
            ((64, POOLED), BF16),
            ((8, LANES), F32),
        ],
        [VMEM, HBM],
        scratch=[pltpu.VMEM((1, 2, Q * LANES), BF16), pltpu.SemaphoreType.DMA(())],
        cost=pl.CostEstimate(flops=10_000_000, bytes_accessed=8_000_000, transcendentals=0),
    )(collided, in_hbm(coarse_pops))

    streamed, right, left, payload, records = call(
        halo_kernel,
        "halo",
        [
            ((Q * PITCH, LANES), F32),
            ((ENDS, LANES), F32),
            ((ENDS, LANES), F32),
            ((PLANE, ROWS, LANES), BF16),
            ((64, LANES), F32),
        ],
        [VMEM] * 10,
        aliases={0: 0},
    )(streamed, edge_z, edge_y, edge_yz, halves, pool, share, records, chosen, centre)

    near = [[PLANE * i + j for j in range(PLANE)] for i in range(PLANE)]
    far = [[PLANE * ((j + TURN) % PLANE) + i for j in range(PLANE)] for i in range(PLANE)]
    payload = lax.all_to_all(payload, "blocks", 0, 0, axis_index_groups=near, tiled=True)
    ring = [(i, (i + 1) % BLOCKS) for i in range(BLOCKS)]
    right = lax.ppermute(right, "blocks", ring)
    left = lax.ppermute(left, "blocks", [(b, a) for a, b in ring])
    ghost, line, own, route, last, flags = call(
        tables_kernel,
        "tables",
        [
            ((256, 384), BF16),
            ((EDGE, LANES), F32),
            ((64, LANES), F32),
            ((3, LANES, LANES), BF16),
            ((3, TILE, LANES), BF16),
            ((8, LANES), jnp.int32),
        ],
        [VMEM] * 2,
        cost=pl.CostEstimate(flops=1_000_000, bytes_accessed=4_000_000, transcendentals=0),
    )(records, interface_pairs)
    payload, edge_yz = call(
        route_kernel,
        "route",
        [((PLANE, ROWS, LANES), BF16), ((NX + 16, LANES), F32)],
        [VMEM] * 5,
    )(route, payload, edge_yz, right, left)
    payload = lax.all_to_all(payload, "blocks", 0, 0, axis_index_groups=far, tiled=True)
    edge_yz = swapped(edge_yz, 3)
    merged = call(
        merge_kernel,
        "merge",
        [((Q, SPAN, LANES), F32)],
        [VMEM] * 4,
        cost=pl.CostEstimate(flops=1_000_000, bytes_accessed=4_000_000, transcendentals=0),
    )(streamed, edge_yz, right, left)[0]
    _, result, update = call(
        finish_kernel,
        "finish",
        [((Q, SPAN, LANES), F32), ((Q, SPAN, LANES), F32), ((1, 2, Q * LANES), F32)],
        [VMEM] * 8,
        (VMEM, HBM, HBM),
        [pltpu.VMEM((1, 2, Q * LANES), F32), pltpu.SemaphoreType.DMA((4,))],
        aliases={0: 0},
    )(merged, payload, last, flags, own, line, share, ghost)
    return result.reshape(1, Q, SPAN * LANES), update


def solution(mesh):
    placed = (
        P("group", None, "blocks"),
        P("group", "blocks"),
        P(),
        P("group", "blocks", None),
        P("group", None),
    )
    return jax.shard_map(
        body,
        mesh=mesh,
        in_specs=placed,
        out_specs=(P("group", None, "blocks"), P("group", "blocks", None)),
        check_vma=False,
    )
```

```python
import jax
import jax.numpy as jnp
from jax import lax
from jax.experimental import pallas as pl
from jax.experimental.pallas import tpu as pltpu
from jax.sharding import PartitionSpec as P

Q = 27
EDGE = 16
HALF = 8
NX = 32
SPAN = 2 * NX
PITCH = SPAN + 16
FIRST = 8
LANES = 128
PLANE = 8
BLOCKS = PLANE * PLANE
TURN = 5
LOW, HIGH, LAST_LOW, LAST_HIGH, CENTRE, RECORDS, ROWS = 54, 55, 56, 57, 58, 62, 80
TILE = 16
MIXED = 48
POOLED = 8 * (2 * Q + 4)
ENDS = 32
PAIRS = [(i // 9, i // 3 % 3, i % 3) for i in range(Q)]
F32 = jnp.float32
BF16 = jnp.bfloat16


def sides():
    position = lax.axis_index("group")
    return position & 1, position >> 1


def geometry():
    side_y, side_z = sides()
    return 1 - side_y, 112 * (1 - side_y), 15 * (1 - side_z)


def ids(shape, dim):
    return lax.broadcasted_iota(jnp.int32, shape, dim)


def rolled(value, shift):
    return pltpu.roll(value, shift, 1)


def split_bf16(value):
    high = value.astype(BF16)
    return high, (value - high.astype(F32)).astype(BF16)


def dot(left, right):
    return jnp.dot(left, right, preferred_element_type=F32)


def record_ids(shape, dim):
    value = ids(shape, dim) & 127
    return value >> 6, value >> 3 & 7, value & 7


def digits(index):
    third, ninth = index * 11 >> 5, index * 57 >> 9
    return ninth, third - 3 * ninth, index - 3 * third


def interp(fine, coarse):
    weight = 1.0 - jnp.abs(0.5 * fine.astype(F32) - 0.25 - coarse.astype(F32))
    end = (fine == 0) | (fine == EDGE - 1)
    return jnp.where(weight > 0.0, jnp.where(end, 1.0, weight), 0.0)


def pool_table():
    side_y, side_z = sides()
    shape = (256, LANES)
    cell = ids(shape, 0)
    pair_y, pair_z = cell >> 5, cell >> 1 & 7
    face, a, b = record_ids(shape, 1)
    on_y = (pair_y == 7 * side_y) & (pair_z == b)
    on_z = (pair_z == 7 * side_z) & (pair_y == b)
    return jnp.where(((face == 0) & on_y) | ((face == 1) & on_z), 0.125, 0.0).astype(BF16)


def share_table():
    side_y, side_z = sides()
    shape = (64, LANES)
    row = ids(shape, 0)
    face, a, b = record_ids(shape, 1)
    column = (row >= Q).astype(jnp.int32)
    index = jnp.where(row < LOW, row - Q * column, jnp.where(row == LOW, 18 + a, a))
    index = jnp.where(row == LAST_LOW, 26, jnp.where(row == LAST_HIGH, 8, index))
    by_x, by_y, by_z = digits(index)
    in_y, in_z = by_y == 2 * (1 - side_y), by_z == 2 * (1 - side_z)
    half_y = in_y & ((face == 0) | (b == 7 * side_y))
    half_z = in_z & ((face == 1) | (b == 7 * side_z))
    low = (by_x == 2) & (column == 0) & (a == 0)
    high = (by_x == 0) & (column == 1) & (a == HALF - 1)
    half_x = (row >= LOW) | low | high
    share = jnp.where(half_y, 0.5, 1.0) * jnp.where(half_z, 0.5, 1.0) * jnp.where(half_x, 0.5, 1.0)
    held = (row <= HIGH) | ((row == LAST_LOW) & (a == 7)) | ((row == LAST_HIGH) & (a == 0))
    return jnp.where(held, share, 0.0)


def pooled_share_table():
    side_y, side_z = sides()
    shape = (POOLED, LANES)
    row = ids(shape, 0)
    block, place = row >> 3, row & 7
    face, a, b = record_ids(shape, 1)
    column, index = block & 1, block >> 1
    index = jnp.where(block == 54, 18 + place, jnp.where(block == 55, 26, index))
    index = jnp.where(block == 56, place, jnp.where(block == 57, 8, index))
    by_x, by_y, by_z = digits(index)
    in_y, in_z = by_y == 2 * (1 - side_y), by_z == 2 * (1 - side_z)
    half_y = in_y & ((face == 0) | (b == 7 * side_y))
    half_z = in_z & ((face == 1) | (b == 7 * side_z))
    low = (by_x == 2) & (column == 0) & (a == 0)
    high = (by_x == 0) & (column == 1) & (a == HALF - 1)
    half_x = (block >= 54) | low | high
    share = jnp.where(half_y, 0.5, 1.0) * jnp.where(half_z, 0.5, 1.0) * jnp.where(half_x, 0.5, 1.0)
    held = (place == a) & ((block != 55) | (place == 7)) & ((block != 57) | (place == 0))
    return jnp.where(held, share, 0.0)


def chosen_table():
    shape = (64, POOLED)
    target, block = ids(shape, 0), ids(shape, 1) >> 3
    second = (target >= Q).astype(jnp.int32)
    wanted = jnp.where(target < LOW, 2 * (target - Q * second) + second, -1)
    wanted = jnp.where(target == LOW, 54, jnp.where(target == HIGH, 56, wanted))
    wanted = jnp.where(target == LAST_LOW, 55, jnp.where(target == LAST_HIGH, 57, wanted))
    return (wanted == block).astype(F32).astype(BF16)


def ghost_table():
    side_y, side_z = sides()
    shape = (LANES, LANES)
    face, a, b = record_ids(shape, 0)
    lanes = ids(shape, 1)
    y, z = lanes >> 4, lanes & 15
    parts = [jnp.where((face == 0) & (y == 7 * side_y), interp(z, b), 0.0)]
    for h in range(2):
        parts.append(jnp.where((face == 1) & (z == 15 * side_z), interp(y + HALF * h, b), 0.0))
    return jnp.concatenate(parts, 1).astype(BF16)


def part_table():
    side_y, side_z = sides()
    shape = (LANES, LANES)
    face, a, b = record_ids(shape, 0)
    to_face, to_a, to_b = record_ids(shape, 1)
    along_x = 0.125 * (interp(2 * to_a, a) + interp(2 * to_a + 1, a))
    across = along_x * (interp(2 * to_b, b) + interp(2 * to_b + 1, b))
    zero = jnp.zeros(shape, jnp.int32)
    out_y, out_z = zero + 15 * side_y, zero + 15 * side_z
    next_y, next_z = zero + 1 + 13 * side_y, zero + 1 + 13 * side_z
    edge_y, edge_z = to_b == 7 * side_y, to_b == 7 * side_z
    line_y = along_x * interp(out_y, b)
    both_y = line_y + along_x * interp(next_y, b)
    both_z = along_x * (interp(out_z, b) + interp(next_z, b))
    in_y = jnp.where(to_face == 0, across, jnp.where(edge_y, both_z, 0.0))
    in_z = jnp.where(to_face == 1, across, jnp.where(edge_z, both_y, 0.0))
    ends = ((to_face == 0) & edge_z) | ((to_face == 1) & edge_y)
    shared = jnp.where(ends, line_y, 0.0)
    parts = [jnp.where(face == 0, in_y, 0.0), jnp.where(face == 1, in_z, 0.0), jnp.where(face == 1, shared, 0.0)]
    return jnp.concatenate(parts, 1).astype(BF16)


def along(table, axis, line):
    out = {}
    for first in range(3):
        for second in range(3):
            keys = []
            for third in range(3):
                key = [first, second]
                key.insert(axis, third)
                keys.append(tuple(key))
            values = line(*[table[key] for key in keys])
            for key, value in zip(keys, values):
                out[key] = value
    return out


def line_moments(low, mid, high):
    both = low + high
    return both + 4.0 * mid, high - low, both


def line_inverse(zeroth, first, second):
    return second - first, zeroth - 0.5 * second, first + second


def collide_cells(current, rates):
    table = {PAIRS[i]: current[i] for i in range(Q)}
    moments = table
    for axis in range(3):
        moments = along(moments, axis, line_moments)
    density = moments[0, 0, 0]
    inverse = 1.0 / density
    flow = [moments[1, 0, 0], moments[0, 1, 0], moments[0, 0, 1]]
    speed = [part * inverse for part in flow]
    carried = [density * part for part in speed]
    square = [carried[axis] * speed[axis] for axis in range(3)]
    third = density * (1.0 / 3.0)
    relaxed = {}
    for index, key in enumerate(PAIRS):
        ones = [axis for axis in range(3) if key[axis] == 1]
        twos = [axis for axis in range(3) if key[axis] == 2]
        scale = (1.0 / 3.0) ** len(twos)
        if len(ones) == 0:
            if len(twos) == 0:
                balance = density
            elif len(twos) == 1:
                balance = third + square[twos[0]]
            elif len(twos) == 2:
                balance = (third + square[twos[0]] + square[twos[1]]) * (1.0 / 3.0)
            else:
                balance = (third + square[0] + square[1] + square[2]) * (1.0 / 9.0)
        elif len(ones) == 1:
            balance = carried[ones[0]] * scale if twos else carried[ones[0]]
        elif len(ones) == 2:
            balance = carried[ones[0]] * speed[ones[1]]
            balance = balance * scale if twos else balance
        else:
            balance = None
        rest = moments[key] if balance is None else moments[key] - balance
        relaxed[key] = rates[index] * rest
    change = relaxed
    for axis in range(3):
        change = along(change, axis, line_inverse)
    return [current[i] - change[PAIRS[i]] for i in range(Q)]


def collide_kernel(
    g_hbm, solid_hbm, rates_hbm, w_ref, y_ref, z_ref, g_ref, solid_ref, rates_ref, sems
):
    pieces = 4
    size = SPAN // pieces
    copies = [
        pltpu.make_async_copy(rates_hbm, rates_ref, sems.at[pieces]),
        pltpu.make_async_copy(solid_hbm, solid_ref, sems.at[pieces + 1]),
    ]
    for piece in range(pieces):
        rows = pl.ds(size * piece, size)
        copies.append(
            pltpu.make_async_copy(g_hbm.at[:, rows, :], g_ref.at[:, rows, :], sems.at[piece])
        )
    for copy in copies:
        copy.start()
    side_y, side_z = sides()
    copies[0].wait()
    rates = []
    for i in range(Q):
        scale = 1.0 / 216.0
        for part in PAIRS[i]:
            scale *= 1.5 if part == 0 else 3.0
        rates.append(rates_ref[i] * scale)
    copies[1].wait()

    def chunk(index, carry):
        row = pl.multiple_of(8 * index, 8)
        current = [g_ref[i, pl.ds(row, 8), :] for i in range(Q)]
        solid = solid_ref[pl.ds(row, 8), :] == 1
        collided = collide_cells(current, rates)
        for i in range(Q):
            w_ref[i, pl.ds(row, 8), :] = jnp.where(solid, current[Q - 1 - i], collided[i])
        return carry

    for piece in range(pieces):
        copies[2 + piece].wait()
        lax.fori_loop(size // 8 * piece, size // 8 * (piece + 1), chunk, 0)

    send_y, send_z = 2 * (1 - side_y), 2 * (1 - side_z)
    tile, base, inner = geometry()
    lanes = ids((NX, LANES), 1)
    packed = [jnp.zeros((NX, LANES), F32), jnp.zeros((NX, LANES), F32)]
    for k in range(9):
        index = 9 * (k // 3) + 3 * send_y + k % 3
        value = w_ref[index, pl.ds(tile, NX, stride=2), :]
        value = rolled(value, (16 * (k % 8) - base) & 127)
        packed[k // 8] = jnp.where(lanes >> 4 == k % 8, value, packed[k // 8])
    y_ref[0] = (packed[0] - 1.0).astype(BF16)
    y_ref[1] = (packed[1] - 1.0).astype(BF16)
    lanes = ids((SPAN, LANES), 1)
    packed_z = jnp.zeros((SPAN, LANES), F32)
    for k in range(9):
        index = 9 * (k // 3) + 3 * (k % 3) + send_z
        value = w_ref[index]
        packed_z = jnp.where(lanes & 15 == k, rolled(value, (k - inner) & 127), packed_z)
    z_ref[...] = (packed_z - 1.0).astype(BF16)


def moved(value, b, shift):
    value = rolled(value, shift)
    if b == 1:
        return value
    rows, lanes = ids(value.shape, 0), ids(value.shape, 1)
    if b == 2:
        other = pltpu.roll(value, 1, 0)
        return jnp.where(lanes >= 16, value, jnp.where(rows & 1 == 1, other, 0.0))
    other = pltpu.roll(value, value.shape[0] - 1, 0)
    return jnp.where(lanes < 112, value, jnp.where(rows & 1 == 0, other, 0.0))


def z_inside(lanes, c):
    return lanes & 15 <= 14 if c == 0 else lanes & 15 >= 1


def stream_kernel(
    w_ref, coarse_hbm, t_ref, e_ref, pool_ref, share_ref, rec_ref, p_ref, chosen_ref, centre_ref, pooled_share_ref,
    coarse_ref, sem
):
    copy = pltpu.make_async_copy(coarse_hbm, coarse_ref, sem)
    copy.start()
    lanes = ids((8, LANES), 1)
    zeros = jnp.zeros((8, LANES), F32)
    held = zeros
    for i, (a, b, c) in enumerate(PAIRS):
        for row in (0, 8, SPAN, SPAN + 8):
            t_ref[pl.ds(PITCH * i + row, 8), :] = zeros
        shift = (16 * (b - 1) + c - 1) % 128
        for row in range(0, SPAN, 8):
            value = w_ref[i, pl.ds(row, 8), :]
            held = held + value
            if shift:
                value = moved(value, b, shift)
            if c != 1:
                value = jnp.where(z_inside(lanes, c), value, 0.0)
            t_ref[pl.ds(PITCH * i + FIRST + row + 2 * (a - 1), 8), :] = value

    side_y, side_z = sides()
    tile, base, inner = geometry()
    lanes = ids((NX, LANES), 1)
    packed = jnp.zeros((NX, LANES), F32)
    for a in range(3):
        index = 9 * a + 6 * (1 - side_y) + 2 * (1 - side_z)
        value = w_ref[index, pl.ds(tile, NX, stride=2), :]
        packed = jnp.where(lanes == a, rolled(value, (a - base - inner) & 127), packed)
    e_ref[...] = packed

    p_ref[...] = jnp.zeros((64, LANES), F32)
    copy.wait()
    records = coarse_ref[0].astype(F32)
    for t in range(2):
        for i in range(Q):
            p_ref[32 * t + i : 32 * t + i + 1, :] = records[t : t + 1, LANES * i : LANES * (i + 1)]
    in_y, in_z = 2 * (1 - side_y), 2 * (1 - side_z)
    first = ids((1, LANES), 1) < 64
    rec_ref[...] = jnp.zeros((32, LANES), F32)
    for t in range(2):
        for k in range(9):
            for_y = p_ref[pl.ds(32 * t + 9 * (k // 3) + 3 * in_y + k % 3, 1), :]
            for_z = p_ref[pl.ds(32 * t + 9 * (k // 3) + 3 * (k % 3) + in_z, 1), :]
            row = RECORDS - MIXED + 9 * t + k
            rec_ref[row : row + 1, :] = jnp.where(first, for_y, for_z)

    pool_ref[...] = pool_table()
    share_ref[...] = share_table()
    chosen_ref[...] = chosen_table()
    pooled_share_ref[...] = pooled_share_table()
    held = jnp.sum(jnp.sum(held, axis=0, keepdims=True), axis=1, keepdims=True)
    centre = (held * (1.0 / (Q * SPAN * LANES))).astype(BF16).astype(F32)
    centre_ref[...] = jnp.broadcast_to(centre, (8, LANES))


def halo_kernel(
    t_ref, z_ref, y_ref, e_ref, rec_ref, pool_ref, pooled_share_ref, p_ref, chosen_ref, centre_ref,
    out_ref, right_ref, left_ref, pay_ref, kept_ref,
):
    del t_ref
    kept_ref[...] = p_ref[...]
    side_y, side_z = sides()
    halo_y, halo_z = 2 * side_y, 2 * side_z
    tile, base, inner = geometry()

    lanes = ids((NX, LANES), 1)
    row_mask = lanes >> 4 == base >> 4
    for k in range(9):
        a, c = k // 3, k % 3
        value = rolled(y_ref[k // 8].astype(F32) + 1.0, (base - 16 * (k % 8) + c - 1) & 127)
        mask = row_mask if c == 1 else row_mask & z_inside(lanes, c)
        index = 9 * a + 3 * halo_y + c
        rows = pl.ds(PITCH * index + FIRST + 2 * (a - 1) + tile, NX, stride=2)
        out_ref[rows, :] = out_ref[rows, :] + jnp.where(mask, value, 0.0)
    lanes = ids((TILE, LANES), 1)
    for k in range(9):
        a, b = k // 3, k % 3
        shift = (inner - k + 16 * (b - 1)) & 127
        index = 9 * a + 3 * b + halo_z
        for row in range(0, SPAN, TILE):
            value = moved(z_ref[row : row + TILE].astype(F32) + 1.0, b, shift)
            rows = pl.ds(PITCH * index + FIRST + row + 2 * (a - 1), TILE)
            out_ref[rows, :] = out_ref[rows, :] + jnp.where(lanes & 15 == inner, value, 0.0)

    for k in range(9):
        right_ref[2 * k : 2 * k + 2, :] = out_ref[pl.ds(PITCH * (18 + k) + FIRST + SPAN, 2), :]
        left_ref[2 * k : 2 * k + 2, :] = out_ref[pl.ds(PITCH * k + FIRST - 2, 2), :]
    right_ref[24:ENDS, :] = e_ref[NX - 8 : NX, :]
    left_ref[24:ENDS, :] = e_ref[0:8, :]

    row_8 = ids((8, LANES), 0)
    tiles = []
    for h in range(2):
        parts = []
        for i in range(Q):
            for s in range(2):
                row = PITCH * i + FIRST + NX * s + h
                parts.append(
                    out_ref[pl.ds(row, 8, stride=4), :] + out_ref[pl.ds(row + 2, 8, stride=4), :]
                )
        over, under = FIRST + SPAN + h, FIRST - 2 + h
        parts.append(out_ref[pl.ds(PITCH * 18 + over, 8, stride=PITCH), :])
        last = out_ref[pl.ds(PITCH * 19 + over, 8, stride=PITCH), :]
        parts.append(jnp.where(row_8 == 7, last, 0.0))
        parts.append(out_ref[pl.ds(under, 8, stride=PITCH), :])
        parts.append(out_ref[pl.ds(PITCH * 8 + under, 8, stride=PITCH), :])
        tiles.append(jnp.concatenate(parts, 0))
    pool = pool_ref[...]
    high, low = split_bf16(jnp.concatenate(tiles, 1))
    pooled = dot(high, pool) + dot(low, pool)
    pooled = jnp.where(ids((POOLED, LANES), 0) & 7 == ids((POOLED, LANES), 1) >> 3 & 7, pooled, 0.0)
    centre = centre_ref[0:1, :]
    pooled = pooled - centre * pooled_share_ref[...]
    routed = dot(chosen_ref[...], pooled.astype(BF16))
    rows, lane_a = ids((64, LANES), 0), ids((64, LANES), 1) >> 3 & 7
    is_centre = (rows == CENTRE) | ((rows == LAST_LOW) & (lane_a == 6)) | ((rows == LAST_HIGH) & (lane_a == 1))
    routed = jnp.where(is_centre, centre, routed)
    payload = jnp.where(rows[MIXED:64] >= RECORDS, rec_ref[0:16], routed[MIXED:64])
    payload = jnp.concatenate([routed[0:MIXED], payload, rec_ref[16:32]], 0).astype(BF16)
    for slot in range(PLANE):
        pay_ref[slot] = payload


def tables_kernel(p_ref, pairs_ref, ghost_ref, line_ref, own_ref, route_ref, last_ref, flag_ref):
    side_y, side_z = sides()
    ghost = ghost_table()
    ghost_ref[0:LANES] = ghost
    ghost_ref[LANES : 2 * LANES] = ghost
    shape = (EDGE, LANES)
    line_ref[...] = interp(ids(shape, 0), record_ids(shape, 1)[1])

    part = dot(p_ref[...].astype(BF16), part_table())
    _, by_y, by_z = digits(ids((32, LANES), 0))
    in_y, in_z = by_y == 2 * (1 - side_y), by_z == 2 * (1 - side_z)
    for t in range(2):
        rows = part[32 * t : 32 * t + 32]
        value = jnp.where(in_y, rows[:, 0:128], 0.0) + jnp.where(in_z, rows[:, 128:256], 0.0)
        own_ref[32 * t : 32 * t + 32] = value - jnp.where(in_y & in_z, rows[:, 256:384], 0.0)

    me = lax.axis_index("blocks")
    pairs = pairs_ref[...]
    rows, lanes = ids((LANES, LANES), 0), ids((LANES, LANES), 1)

    def total(mask, value):
        value = jnp.where(mask, value.astype(F32), 0.0)
        value = jnp.sum(value, axis=1, keepdims=True)
        return jnp.broadcast_to(value, mask.shape).astype(jnp.int32)

    def matrices(ref, owner, holder, source, rows, lanes):
        place = rows & (TILE - 1)
        low = (place == LOW - MIXED) | (place == LAST_LOW - MIXED)
        high = (place == HIGH - MIXED) | (place == LAST_HIGH - MIXED)
        mixed = jnp.where(low, owner - 1, jnp.where(high, owner + 1, owner))
        mixed = jnp.where(place >= RECORDS - MIXED, holder, mixed)
        for kind, route in enumerate((owner, mixed, holder)):
            chosen = (source(route) == lanes >> 4) & (place == lanes & (TILE - 1))
            ref[kind] = chosen.astype(F32).astype(BF16)

    device = PLANE * ((rows >> 4) + TURN & (PLANE - 1)) + (me & (PLANE - 1))
    pairs = jnp.broadcast_to(pairs, (LANES, LANES))
    owner = total(lanes == 2 * device, pairs >> 1)
    holder = total(pairs == 2 * device, lanes >> 1)
    matrices(route_ref, owner, holder, lambda route: route & (PLANE - 1), rows, lanes)
    rows, lanes, pairs = rows[0:TILE], lanes[0:TILE], pairs[0:TILE]
    serves = total(lanes == 2 * me, pairs)
    record = total(pairs == 2 * me, lanes)
    matrices(last_ref, serves >> 1, record >> 1, lambda route: (route >> 3) - TURN & (PLANE - 1), rows, lanes)
    flag_ref[...] = jnp.where(rows[0:8] == 0, record[0:8] & 1, serves[0:8] & 1)


def passed_on(matrix_ref, in_ref):
    for start in range(0, ROWS, TILE):
        kind = 0 if start < MIXED else 1 if start == MIXED else 2
        tile = [in_ref[member, start : start + TILE] for member in range(PLANE)]
        yield start, dot(matrix_ref[kind], jnp.concatenate(tile, 0))


def route_kernel(route_ref, in_ref, e_ref, right_ref, left_ref, out_ref, edge_ref):
    for start, rows in passed_on(route_ref, in_ref):
        rows = rows.astype(BF16)
        for plane in range(PLANE):
            out_ref[plane, start : start + TILE] = rows[TILE * plane : TILE * (plane + 1)]
    edge_ref[0:NX, :] = e_ref[...]
    edge_ref[NX : NX + 8, :] = right_ref[24:ENDS, :]
    edge_ref[NX + 8 : NX + 16, :] = left_ref[24:ENDS, :]


def merge_kernel(t_ref, e_ref, right_ref, left_ref, next_ref):
    side_y, side_z = sides()
    tile, base, inner = geometry()
    for i in range(Q):
        next_ref[i] = t_ref[PITCH * i + FIRST : PITCH * i + FIRST + SPAN, :]
    for k in range(9):
        next_ref[18 + k, 0:2] = next_ref[18 + k, 0:2] + right_ref[2 * k : 2 * k + 2, :]
        next_ref[k, SPAN - 2 : SPAN] = next_ref[k, SPAN - 2 : SPAN] + left_ref[2 * k : 2 * k + 2, :]
    rows, lanes = ids((NX, LANES), 0), ids((NX, LANES), 1)
    corner = e_ref[0:NX, :]
    low = jnp.where(rows == 0, e_ref[NX + 7 : NX + 8, :], pltpu.roll(corner, 1, 0))
    high = jnp.where(rows == NX - 1, e_ref[NX + 8 : NX + 9, :], pltpu.roll(corner, NX - 1, 0))
    for a, value in ((0, high), (1, corner), (2, low)):
        index = 9 * a + 6 * side_y + 2 * side_z
        value = rolled(value, (base + inner - a) & 127)
        at = pl.ds(tile, NX, stride=2)
        next_ref[index, at, :] = next_ref[index, at, :] + jnp.where(lanes == base + inner, value, 0.0)


def finish_kernel(
    base_ref, in_ref, last_ref, flag_ref, own_ref, line_ref, share_ref, ghost_ref,
    value_ref, next_hbm, update_hbm,
    update_ref, sems,
):
    del base_ref
    side_y, side_z = sides()
    in_y, in_z = 2 * (1 - side_y), 2 * (1 - side_z)
    copies = []

    def send(source, target):
        copy = pltpu.make_async_copy(source, target, sems.at[len(copies)])
        copy.start()
        copies.append(copy)

    rows = jnp.concatenate([tile for _, tile in passed_on(last_ref, in_ref)], 0)
    swap = flag_ref[0:1, :] == 1
    lines = line_ref[...]
    scaled = []
    for k in range(9):
        row = RECORDS + k
        first, second = rows[row : row + 1], rows[row + 9 : row + 10]
        scaled.append(lines * jnp.where(swap, second, first))
        scaled.append(lines * jnp.where(swap, first, second))
    scaled = jnp.concatenate(scaled, 0)
    ghost = dot(jnp.concatenate(split_bf16(scaled), 1), ghost_ref[...])
    lanes = ids((NX, LANES), 1)
    outer = lanes >> 4 == 7 * side_y
    for a in range(3):
        for b in range(3):
            k = 3 * a + b
            for h in range(2):
                at = pl.ds(h, NX, stride=2)
                part = ghost[NX * k : NX * (k + 1), LANES * (h + 1) : LANES * (h + 2)]
                value_ref[9 * a + 3 * b + in_z, at, :] = value_ref[9 * a + 3 * b + in_z, at, :] + part
        for c in range(3):
            k = 3 * a + c
            at = pl.ds(side_y, NX, stride=2)
            part = ghost[NX * k : NX * (k + 1), 0:LANES]
            value = value_ref[9 * a + 3 * in_y + c, at, :]
            value_ref[9 * a + 3 * in_y + c, at, :] = jnp.where(outer, part, value)
        send(value_ref.at[pl.ds(9 * a, 9)], next_hbm.at[pl.ds(9 * a, 9)])

    share = share_ref[...]
    lane_1 = ids((1, LANES), 1)
    low_centre = jnp.sum(jnp.where(lane_1 == 48, rows[LAST_LOW : LAST_LOW + 1], 0.0), axis=1, keepdims=True)
    high_centre = jnp.sum(jnp.where(lane_1 == 8, rows[LAST_HIGH : LAST_HIGH + 1], 0.0), axis=1, keepdims=True)
    main = rows[0:LOW] + rows[CENTRE : CENTRE + 1] * share[0:LOW]
    low, high, last_low, last_high = (
        rows[row : row + 1] + centre * share[row : row + 1]
        for row, centre in (
            (LOW, low_centre), (HIGH, high_centre), (LAST_LOW, low_centre), (LAST_HIGH, high_centre)
        )
    )
    row, lane_a = ids((32, LANES), 0), ids((32, LANES), 1) >> 3 & 7
    from_low = jnp.where(row - 18 == lane_a, low, 0.0)
    from_low = jnp.where(row == 26, jnp.where(lane_a == 7, last_low, 0.0), from_low)
    from_high = jnp.where(row == lane_a, high, 0.0)
    from_high = jnp.where(row == 8, jnp.where(lane_a == 0, last_high, 0.0), from_high)
    lane_in, lane_out = ids((LANES, LANES), 0), ids((LANES, LANES), 1)
    alike = (lane_in >> 6 == lane_out >> 6) & (lane_in & 7 == lane_out & 7)
    alike = alike.astype(F32).astype(BF16)
    edges = jnp.zeros((2 * 32, LANES), F32)
    for part in split_bf16(jnp.concatenate([from_low, from_high], 0)):
        edges = edges + dot(part, alike)
    column_0 = main[0:Q] + jnp.where(lane_a == 0, edges[0:32], 0.0)[0:Q]
    column_1 = main[Q : 2 * Q] + jnp.where(lane_a == HALF - 1, edges[32:64], 0.0)[0:Q]
    crossed = jnp.broadcast_to(flag_ref[1:2, :], (Q, LANES)) == 1
    for t in range(2):
        here, there = (column_0, column_1) if t == 0 else (column_1, column_0)
        value = jnp.where(crossed, there, here) + own_ref[32 * t : 32 * t + Q, :]
        for i in range(Q):
            update_ref[0, t : t + 1, LANES * i : LANES * (i + 1)] = value[i : i + 1]
    send(update_ref, update_hbm)
    for copy in copies:
        copy.wait()


VMEM = pl.BlockSpec(memory_space=pltpu.VMEM)
HBM = pl.BlockSpec(memory_space=pltpu.HBM)


def call(kernel, name, results, inputs, outputs=None, scratch=(), cost=None, aliases=None, limit=32):
    return pl.pallas_call(
        kernel,
        out_shape=tuple(jax.ShapeDtypeStruct(*result) for result in results),
        in_specs=inputs,
        out_specs=outputs or (VMEM,) * len(results),
        scratch_shapes=scratch,
        input_output_aliases=aliases or {},
        compiler_params=pltpu.CompilerParams(vmem_limit_bytes=limit * 1024 * 1024),
        cost_estimate=cost,
        name=name,
    )


def in_hbm(value):
    return pltpu.with_memory_space_constraint(value, pltpu.HBM)


def swapped(block, bits):
    return lax.ppermute(block, "group", [(i, i ^ bits) for i in range(4)])


def body(populations, solid_mask, relax_rates, coarse_pops, interface_pairs):
    collided, edge_y, edge_z = call(
        collide_kernel,
        "collide",
        [((Q, SPAN, LANES), F32), ((2, NX, LANES), BF16), ((SPAN, LANES), BF16)],
        [HBM] * 3,
        scratch=[
            pltpu.VMEM((Q, SPAN, LANES), F32),
            pltpu.VMEM((SPAN, LANES), jnp.int32),
            pltpu.SMEM((Q,), F32),
            pltpu.SemaphoreType.DMA((6,)),
        ],
    )(
        in_hbm(populations.reshape(Q, SPAN, LANES)),
        in_hbm(solid_mask.reshape(SPAN, LANES)),
        in_hbm(relax_rates),
    )

    edge_z = swapped(edge_z, 2)
    edge_y = swapped(edge_y, 1)
    streamed, edge_yz, pool, share, halves, records, chosen, centre, pooled_share = call(
        stream_kernel,
        "stream",
        [
            ((Q * PITCH, LANES), F32),
            ((NX, LANES), F32),
            ((256, LANES), BF16),
            ((64, LANES), F32),
            ((32, LANES), F32),
            ((64, LANES), F32),
            ((64, POOLED), BF16),
            ((8, LANES), F32),
            ((POOLED, LANES), F32),
        ],
        [VMEM, HBM],
        scratch=[pltpu.VMEM((1, 2, Q * LANES), BF16), pltpu.SemaphoreType.DMA(())],
        cost=pl.CostEstimate(flops=10_000_000, bytes_accessed=8_000_000, transcendentals=0),
    )(collided, in_hbm(coarse_pops))

    streamed, right, left, payload, records = call(
        halo_kernel,
        "halo",
        [
            ((Q * PITCH, LANES), F32),
            ((ENDS, LANES), F32),
            ((ENDS, LANES), F32),
            ((PLANE, ROWS, LANES), BF16),
            ((64, LANES), F32),
        ],
        [VMEM] * 10,
        aliases={0: 0},
    )(streamed, edge_z, edge_y, edge_yz, halves, pool, pooled_share, records, chosen, centre)

    near = [[PLANE * i + j for j in range(PLANE)] for i in range(PLANE)]
    far = [[PLANE * ((j + TURN) % PLANE) + i for j in range(PLANE)] for i in range(PLANE)]
    payload = lax.all_to_all(payload, "blocks", 0, 0, axis_index_groups=near, tiled=True)
    ring = [(i, (i + 1) % BLOCKS) for i in range(BLOCKS)]
    right = lax.ppermute(right, "blocks", ring)
    left = lax.ppermute(left, "blocks", [(b, a) for a, b in ring])
    ghost, line, own, route, last, flags = call(
        tables_kernel,
        "tables",
        [
            ((256, 384), BF16),
            ((EDGE, LANES), F32),
            ((64, LANES), F32),
            ((3, LANES, LANES), BF16),
            ((3, TILE, LANES), BF16),
            ((8, LANES), jnp.int32),
        ],
        [VMEM] * 2,
        cost=pl.CostEstimate(flops=1_000_000, bytes_accessed=4_000_000, transcendentals=0),
    )(records, interface_pairs)
    payload, edge_yz = call(
        route_kernel,
        "route",
        [((PLANE, ROWS, LANES), BF16), ((NX + 16, LANES), F32)],
        [VMEM] * 5,
    )(route, payload, edge_yz, right, left)
    payload = lax.all_to_all(payload, "blocks", 0, 0, axis_index_groups=far, tiled=True)
    edge_yz = swapped(edge_yz, 3)
    merged = call(
        merge_kernel,
        "merge",
        [((Q, SPAN, LANES), F32)],
        [VMEM] * 4,
        cost=pl.CostEstimate(flops=1_000_000, bytes_accessed=4_000_000, transcendentals=0),
    )(streamed, edge_yz, right, left)[0]
    _, result, update = call(
        finish_kernel,
        "finish",
        [((Q, SPAN, LANES), F32), ((Q, SPAN, LANES), F32), ((1, 2, Q * LANES), F32)],
        [VMEM] * 8,
        (VMEM, HBM, HBM),
        [pltpu.VMEM((1, 2, Q * LANES), F32), pltpu.SemaphoreType.DMA((4,))],
        aliases={0: 0},
    )(merged, payload, last, flags, own, line, share, ghost)
    return result.reshape(1, Q, SPAN * LANES), update


def solution(mesh):
    placed = (
        P("group", None, "blocks"),
        P("group", "blocks"),
        P(),
        P("group", "blocks", None),
        P("group", None),
    )
    return jax.shard_map(
        body,
        mesh=mesh,
        in_specs=placed,
        out_specs=(P("group", None, "blocks"), P("group", "blocks", None)),
        check_vma=False,
    )
```

```python
import jax
import jax.numpy as jnp
from jax import lax
from jax.experimental import pallas as pl
from jax.experimental.pallas import tpu as pltpu
from jax.sharding import PartitionSpec as P

Q = 27
EDGE = 16
HALF = 8
NX = 32
SPAN = 2 * NX
PITCH = SPAN + 16
FIRST = 8
LANES = 128
PLANE = 8
BLOCKS = PLANE * PLANE
TURN = 5
LOW, HIGH, LAST_LOW, LAST_HIGH, CENTRE, RECORDS, ROWS = 54, 55, 56, 57, 58, 62, 80
TILE = 16
MIXED = 48
POOLED = 8 * (2 * Q + 4)
ENDS = 32
PAIRS = [(i // 9, i // 3 % 3, i % 3) for i in range(Q)]
F32 = jnp.float32
BF16 = jnp.bfloat16


def sides():
    position = lax.axis_index("group")
    return position & 1, position >> 1


def geometry():
    side_y, side_z = sides()
    return 1 - side_y, 112 * (1 - side_y), 15 * (1 - side_z)


def ids(shape, dim):
    return lax.broadcasted_iota(jnp.int32, shape, dim)


def rolled(value, shift):
    return pltpu.roll(value, shift, 1)


def split_bf16(value):
    high = value.astype(BF16)
    return high, (value - high.astype(F32)).astype(BF16)


def dot(left, right):
    return jnp.dot(left, right, preferred_element_type=F32)


def record_ids(shape, dim):
    value = ids(shape, dim) & 127
    return value >> 6, value >> 3 & 7, value & 7


def digits(index):
    third, ninth = index * 11 >> 5, index * 57 >> 9
    return ninth, third - 3 * ninth, index - 3 * third


def interp(fine, coarse):
    weight = 1.0 - jnp.abs(0.5 * fine.astype(F32) - 0.25 - coarse.astype(F32))
    end = (fine == 0) | (fine == EDGE - 1)
    return jnp.where(weight > 0.0, jnp.where(end, 1.0, weight), 0.0)


def pool_table():
    side_y, side_z = sides()
    shape = (256, LANES)
    cell = ids(shape, 0)
    pair_y, pair_z = cell >> 5, cell >> 1 & 7
    face, a, b = record_ids(shape, 1)
    on_y = (pair_y == 7 * side_y) & (pair_z == b)
    on_z = (pair_z == 7 * side_z) & (pair_y == b)
    return jnp.where(((face == 0) & on_y) | ((face == 1) & on_z), 0.125, 0.0).astype(BF16)


def share_table():
    side_y, side_z = sides()
    shape = (64, LANES)
    row = ids(shape, 0)
    face, a, b = record_ids(shape, 1)
    column = (row >= Q).astype(jnp.int32)
    index = jnp.where(row < LOW, row - Q * column, jnp.where(row == LOW, 18 + a, a))
    index = jnp.where(row == LAST_LOW, 26, jnp.where(row == LAST_HIGH, 8, index))
    by_x, by_y, by_z = digits(index)
    in_y, in_z = by_y == 2 * (1 - side_y), by_z == 2 * (1 - side_z)
    half_y = in_y & ((face == 0) | (b == 7 * side_y))
    half_z = in_z & ((face == 1) | (b == 7 * side_z))
    low = (by_x == 2) & (column == 0) & (a == 0)
    high = (by_x == 0) & (column == 1) & (a == HALF - 1)
    half_x = (row >= LOW) | low | high
    share = jnp.where(half_y, 0.5, 1.0) * jnp.where(half_z, 0.5, 1.0) * jnp.where(half_x, 0.5, 1.0)
    held = (row <= HIGH) | ((row == LAST_LOW) & (a == 7)) | ((row == LAST_HIGH) & (a == 0))
    return jnp.where(held, share, 0.0)


def chosen_table():
    shape = (64, POOLED)
    target, block = ids(shape, 0), ids(shape, 1) >> 3
    second = (target >= Q).astype(jnp.int32)
    wanted = jnp.where(target < LOW, 2 * (target - Q * second) + second, -1)
    wanted = jnp.where(target == LOW, 54, jnp.where(target == HIGH, 56, wanted))
    wanted = jnp.where(target == LAST_LOW, 55, jnp.where(target == LAST_HIGH, 57, wanted))
    return (wanted == block).astype(F32).astype(BF16)


def ghost_table():
    side_y, side_z = sides()
    shape = (LANES, LANES)
    face, a, b = record_ids(shape, 0)
    lanes = ids(shape, 1)
    y, z = lanes >> 4, lanes & 15
    parts = [jnp.where((face == 0) & (y == 7 * side_y), interp(z, b), 0.0)]
    for h in range(2):
        parts.append(jnp.where((face == 1) & (z == 15 * side_z), interp(y + HALF * h, b), 0.0))
    return jnp.concatenate(parts, 1).astype(BF16)


def part_table():
    side_y, side_z = sides()
    shape = (LANES, LANES)
    face, a, b = record_ids(shape, 0)
    to_face, to_a, to_b = record_ids(shape, 1)
    along_x = 0.125 * (interp(2 * to_a, a) + interp(2 * to_a + 1, a))
    across = along_x * (interp(2 * to_b, b) + interp(2 * to_b + 1, b))
    zero = jnp.zeros(shape, jnp.int32)
    out_y, out_z = zero + 15 * side_y, zero + 15 * side_z
    next_y, next_z = zero + 1 + 13 * side_y, zero + 1 + 13 * side_z
    edge_y, edge_z = to_b == 7 * side_y, to_b == 7 * side_z
    line_y = along_x * interp(out_y, b)
    both_y = line_y + along_x * interp(next_y, b)
    both_z = along_x * (interp(out_z, b) + interp(next_z, b))
    in_y = jnp.where(to_face == 0, across, jnp.where(edge_y, both_z, 0.0))
    in_z = jnp.where(to_face == 1, across, jnp.where(edge_z, both_y, 0.0))
    ends = ((to_face == 0) & edge_z) | ((to_face == 1) & edge_y)
    shared = jnp.where(ends, line_y, 0.0)
    parts = [jnp.where(face == 0, in_y, 0.0), jnp.where(face == 1, in_z, 0.0), jnp.where(face == 1, shared, 0.0)]
    return jnp.concatenate(parts, 1).astype(BF16)


def along(table, axis, line):
    out = {}
    for first in range(3):
        for second in range(3):
            keys = []
            for third in range(3):
                key = [first, second]
                key.insert(axis, third)
                keys.append(tuple(key))
            values = line(*[table[key] for key in keys])
            for key, value in zip(keys, values):
                out[key] = value
    return out


def line_moments(low, mid, high):
    both = low + high
    return both + 4.0 * mid, high - low, both


def line_inverse(zeroth, first, second):
    return second - first, zeroth - 0.5 * second, first + second


def collide_cells(current, rates):
    table = {PAIRS[i]: current[i] for i in range(Q)}
    moments = table
    for axis in range(3):
        moments = along(moments, axis, line_moments)
    density = moments[0, 0, 0]
    inverse = 1.0 / density
    flow = [moments[1, 0, 0], moments[0, 1, 0], moments[0, 0, 1]]
    speed = [part * inverse for part in flow]
    carried = [density * part for part in speed]
    square = [carried[axis] * speed[axis] for axis in range(3)]
    third = density * (1.0 / 3.0)
    relaxed = {}
    for index, key in enumerate(PAIRS):
        ones = [axis for axis in range(3) if key[axis] == 1]
        twos = [axis for axis in range(3) if key[axis] == 2]
        scale = (1.0 / 3.0) ** len(twos)
        if len(ones) == 0:
            if len(twos) == 0:
                balance = density
            elif len(twos) == 1:
                balance = third + square[twos[0]]
            elif len(twos) == 2:
                balance = (third + square[twos[0]] + square[twos[1]]) * (1.0 / 3.0)
            else:
                balance = (third + square[0] + square[1] + square[2]) * (1.0 / 9.0)
        elif len(ones) == 1:
            balance = carried[ones[0]] * scale if twos else carried[ones[0]]
        elif len(ones) == 2:
            balance = carried[ones[0]] * speed[ones[1]]
            balance = balance * scale if twos else balance
        else:
            balance = None
        rest = moments[key] if balance is None else moments[key] - balance
        relaxed[key] = rates[index] * rest
    change = relaxed
    for axis in range(3):
        change = along(change, axis, line_inverse)
    return [current[i] - change[PAIRS[i]] for i in range(Q)]


def collide_kernel(
    g_hbm, solid_hbm, rates_hbm, w_ref, y_ref, z_ref, g_ref, solid_ref, rates_ref, sems
):
    pieces = 4
    size = SPAN // pieces
    copies = [
        pltpu.make_async_copy(rates_hbm, rates_ref, sems.at[pieces]),
        pltpu.make_async_copy(solid_hbm, solid_ref, sems.at[pieces + 1]),
    ]
    for piece in range(pieces):
        rows = pl.ds(size * piece, size)
        copies.append(
            pltpu.make_async_copy(g_hbm.at[:, rows, :], g_ref.at[:, rows, :], sems.at[piece])
        )
    for copy in copies:
        copy.start()
    side_y, side_z = sides()
    copies[0].wait()
    rates = []
    for i in range(Q):
        scale = 1.0 / 216.0
        for part in PAIRS[i]:
            scale *= 1.5 if part == 0 else 3.0
        rates.append(rates_ref[i] * scale)
    copies[1].wait()

    def chunk(index, carry):
        row = pl.multiple_of(8 * index, 8)
        current = [g_ref[i, pl.ds(row, 8), :] for i in range(Q)]
        solid = solid_ref[pl.ds(row, 8), :] == 1
        collided = collide_cells(current, rates)
        for i in range(Q):
            w_ref[i, pl.ds(row, 8), :] = jnp.where(solid, current[Q - 1 - i], collided[i])
        return carry

    for piece in range(pieces):
        copies[2 + piece].wait()
        lax.fori_loop(size // 8 * piece, size // 8 * (piece + 1), chunk, 0)

    send_y, send_z = 2 * (1 - side_y), 2 * (1 - side_z)
    tile, base, inner = geometry()
    lanes = ids((NX, LANES), 1)
    packed = [jnp.zeros((NX, LANES), F32), jnp.zeros((NX, LANES), F32)]
    for k in range(9):
        index = 9 * (k // 3) + 3 * send_y + k % 3
        value = w_ref[index, pl.ds(tile, NX, stride=2), :]
        value = rolled(value, (16 * (k % 8) - base) & 127)
        packed[k // 8] = jnp.where(lanes >> 4 == k % 8, value, packed[k // 8])
    y_ref[0] = (packed[0] - 1.0).astype(BF16)
    y_ref[1] = (packed[1] - 1.0).astype(BF16)
    lanes = ids((SPAN, LANES), 1)
    packed_z = jnp.zeros((SPAN, LANES), F32)
    for k in range(9):
        index = 9 * (k // 3) + 3 * (k % 3) + send_z
        value = w_ref[index]
        packed_z = jnp.where(lanes & 15 == k, rolled(value, (k - inner) & 127), packed_z)
    z_ref[...] = (packed_z - 1.0).astype(BF16)


def moved(value, b, shift):
    value = rolled(value, shift)
    if b == 1:
        return value
    rows, lanes = ids(value.shape, 0), ids(value.shape, 1)
    if b == 2:
        other = pltpu.roll(value, 1, 0)
        return jnp.where(lanes >= 16, value, jnp.where(rows & 1 == 1, other, 0.0))
    other = pltpu.roll(value, value.shape[0] - 1, 0)
    return jnp.where(lanes < 112, value, jnp.where(rows & 1 == 0, other, 0.0))


def z_inside(lanes, c):
    return lanes & 15 <= 14 if c == 0 else lanes & 15 >= 1


def stream_kernel(
    w_ref, coarse_hbm, t_ref, e_ref, pool_ref, share_ref, rec_ref, p_ref, chosen_ref, centre_ref, coarse_ref, sem
):
    copy = pltpu.make_async_copy(coarse_hbm, coarse_ref, sem)
    copy.start()
    lanes = ids((8, LANES), 1)
    zeros = jnp.zeros((8, LANES), F32)
    held = zeros
    for i, (a, b, c) in enumerate(PAIRS):
        for row in (0, 8, SPAN, SPAN + 8):
            t_ref[pl.ds(PITCH * i + row, 8), :] = zeros
        shift = (16 * (b - 1) + c - 1) % 128
        for row in range(0, SPAN, 8):
            value = w_ref[i, pl.ds(row, 8), :]
            held = held + value
            if shift:
                value = moved(value, b, shift)
            if c != 1:
                value = jnp.where(z_inside(lanes, c), value, 0.0)
            t_ref[pl.ds(PITCH * i + FIRST + row + 2 * (a - 1), 8), :] = value

    side_y, side_z = sides()
    tile, base, inner = geometry()
    lanes = ids((NX, LANES), 1)
    packed = jnp.zeros((NX, LANES), F32)
    for a in range(3):
        index = 9 * a + 6 * (1 - side_y) + 2 * (1 - side_z)
        value = w_ref[index, pl.ds(tile, NX, stride=2), :]
        packed = jnp.where(lanes == a, rolled(value, (a - base - inner) & 127), packed)
    e_ref[...] = packed

    p_ref[...] = jnp.zeros((64, LANES), F32)
    copy.wait()
    records = coarse_ref[0].astype(F32)
    for t in range(2):
        for i in range(Q):
            p_ref[32 * t + i : 32 * t + i + 1, :] = records[t : t + 1, LANES * i : LANES * (i + 1)]
    in_y, in_z = 2 * (1 - side_y), 2 * (1 - side_z)
    first = ids((1, LANES), 1) < 64
    rec_ref[...] = jnp.zeros((32, LANES), F32)
    for t in range(2):
        for k in range(9):
            for_y = p_ref[pl.ds(32 * t + 9 * (k // 3) + 3 * in_y + k % 3, 1), :]
            for_z = p_ref[pl.ds(32 * t + 9 * (k // 3) + 3 * (k % 3) + in_z, 1), :]
            row = RECORDS - MIXED + 9 * t + k
            rec_ref[row : row + 1, :] = jnp.where(first, for_y, for_z)

    pool_ref[...] = pool_table()
    share_ref[...] = share_table()
    chosen_ref[...] = chosen_table()
    held = jnp.sum(jnp.sum(held, axis=0, keepdims=True), axis=1, keepdims=True)
    centre = (held * (1.0 / (Q * SPAN * LANES))).astype(BF16).astype(F32)
    centre_ref[...] = jnp.broadcast_to(centre, (8, LANES))


def halo_kernel(
    t_ref, z_ref, y_ref, e_ref, rec_ref, pool_ref, share_ref, p_ref, chosen_ref, centre_ref,
    out_ref, right_ref, left_ref, pay_ref, kept_ref,
):
    del t_ref
    kept_ref[...] = p_ref[...]
    side_y, side_z = sides()
    halo_y, halo_z = 2 * side_y, 2 * side_z
    tile, base, inner = geometry()

    lanes = ids((NX, LANES), 1)
    row_mask = lanes >> 4 == base >> 4
    for k in range(9):
        a, c = k // 3, k % 3
        value = rolled(y_ref[k // 8].astype(F32) + 1.0, (base - 16 * (k % 8) + c - 1) & 127)
        mask = row_mask if c == 1 else row_mask & z_inside(lanes, c)
        index = 9 * a + 3 * halo_y + c
        rows = pl.ds(PITCH * index + FIRST + 2 * (a - 1) + tile, NX, stride=2)
        out_ref[rows, :] = out_ref[rows, :] + jnp.where(mask, value, 0.0)
    lanes = ids((TILE, LANES), 1)
    for k in range(9):
        a, b = k // 3, k % 3
        shift = (inner - k + 16 * (b - 1)) & 127
        index = 9 * a + 3 * b + halo_z
        for row in range(0, SPAN, TILE):
            value = moved(z_ref[row : row + TILE].astype(F32) + 1.0, b, shift)
            rows = pl.ds(PITCH * index + FIRST + row + 2 * (a - 1), TILE)
            out_ref[rows, :] = out_ref[rows, :] + jnp.where(lanes & 15 == inner, value, 0.0)

    for k in range(9):
        right_ref[2 * k : 2 * k + 2, :] = out_ref[pl.ds(PITCH * (18 + k) + FIRST + SPAN, 2), :]
        left_ref[2 * k : 2 * k + 2, :] = out_ref[pl.ds(PITCH * k + FIRST - 2, 2), :]
    right_ref[24:ENDS, :] = e_ref[NX - 8 : NX, :]
    left_ref[24:ENDS, :] = e_ref[0:8, :]

    row_8 = ids((8, LANES), 0)
    tiles = []
    for h in range(2):
        parts = []
        for i in range(Q):
            for s in range(2):
                row = PITCH * i + FIRST + NX * s + h
                parts.append(
                    out_ref[pl.ds(row, 8, stride=4), :] + out_ref[pl.ds(row + 2, 8, stride=4), :]
                )
        over, under = FIRST + SPAN + h, FIRST - 2 + h
        parts.append(out_ref[pl.ds(PITCH * 18 + over, 8, stride=PITCH), :])
        last = out_ref[pl.ds(PITCH * 19 + over, 8, stride=PITCH), :]
        parts.append(jnp.where(row_8 == 7, last, 0.0))
        parts.append(out_ref[pl.ds(under, 8, stride=PITCH), :])
        parts.append(out_ref[pl.ds(PITCH * 8 + under, 8, stride=PITCH), :])
        tiles.append(jnp.concatenate(parts, 0))
    pool = pool_ref[...]
    high, low = split_bf16(jnp.concatenate(tiles, 1))
    pooled = dot(high, pool) + dot(low, pool)
    pooled = jnp.where(ids((POOLED, LANES), 0) & 7 == ids((POOLED, LANES), 1) >> 3 & 7, pooled, 0.0)
    chosen = chosen_ref[...]
    high, low = split_bf16(pooled)
    routed = dot(chosen, high) + dot(chosen, low)

    share = share_ref[...]
    rows, lane_a = ids((64, LANES), 0), ids((64, LANES), 1) >> 3 & 7
    centre = centre_ref[0:1, :]
    routed = routed - centre * share
    is_centre = (rows == CENTRE) | ((rows == LAST_LOW) & (lane_a == 6)) | ((rows == LAST_HIGH) & (lane_a == 1))
    routed = jnp.where(is_centre, centre, routed)
    payload = jnp.where(rows[MIXED:64] >= RECORDS, rec_ref[0:16], routed[MIXED:64])
    payload = jnp.concatenate([routed[0:MIXED], payload, rec_ref[16:32]], 0).astype(BF16)
    for slot in range(PLANE):
        pay_ref[slot] = payload


def tables_kernel(p_ref, pairs_ref, ghost_ref, line_ref, own_ref, route_ref, last_ref, flag_ref):
    side_y, side_z = sides()
    ghost = ghost_table()
    ghost_ref[0:LANES] = ghost
    ghost_ref[LANES : 2 * LANES] = ghost
    shape = (EDGE, LANES)
    line_ref[...] = interp(ids(shape, 0), record_ids(shape, 1)[1])

    part = dot(p_ref[...].astype(BF16), part_table())
    _, by_y, by_z = digits(ids((32, LANES), 0))
    in_y, in_z = by_y == 2 * (1 - side_y), by_z == 2 * (1 - side_z)
    for t in range(2):
        rows = part[32 * t : 32 * t + 32]
        value = jnp.where(in_y, rows[:, 0:128], 0.0) + jnp.where(in_z, rows[:, 128:256], 0.0)
        own_ref[32 * t : 32 * t + 32] = value - jnp.where(in_y & in_z, rows[:, 256:384], 0.0)

    me = lax.axis_index("blocks")
    pairs = pairs_ref[...]
    rows, lanes = ids((LANES, LANES), 0), ids((LANES, LANES), 1)

    def total(mask, value):
        value = jnp.where(mask, value.astype(F32), 0.0)
        value = jnp.sum(value, axis=1, keepdims=True)
        return jnp.broadcast_to(value, mask.shape).astype(jnp.int32)

    def matrices(ref, owner, holder, source, rows, lanes):
        place = rows & (TILE - 1)
        low = (place == LOW - MIXED) | (place == LAST_LOW - MIXED)
        high = (place == HIGH - MIXED) | (place == LAST_HIGH - MIXED)
        mixed = jnp.where(low, owner - 1, jnp.where(high, owner + 1, owner))
        mixed = jnp.where(place >= RECORDS - MIXED, holder, mixed)
        for kind, route in enumerate((owner, mixed, holder)):
            chosen = (source(route) == lanes >> 4) & (place == lanes & (TILE - 1))
            ref[kind] = chosen.astype(F32).astype(BF16)

    device = PLANE * ((rows >> 4) + TURN & (PLANE - 1)) + (me & (PLANE - 1))
    pairs = jnp.broadcast_to(pairs, (LANES, LANES))
    owner = total(lanes == 2 * device, pairs >> 1)
    holder = total(pairs == 2 * device, lanes >> 1)
    matrices(route_ref, owner, holder, lambda route: route & (PLANE - 1), rows, lanes)
    rows, lanes, pairs = rows[0:TILE], lanes[0:TILE], pairs[0:TILE]
    serves = total(lanes == 2 * me, pairs)
    record = total(pairs == 2 * me, lanes)
    matrices(last_ref, serves >> 1, record >> 1, lambda route: (route >> 3) - TURN & (PLANE - 1), rows, lanes)
    flag_ref[...] = jnp.where(rows[0:8] == 0, record[0:8] & 1, serves[0:8] & 1)


def passed_on(matrix_ref, in_ref):
    for start in range(0, ROWS, TILE):
        kind = 0 if start < MIXED else 1 if start == MIXED else 2
        tile = [in_ref[member, start : start + TILE] for member in range(PLANE)]
        yield start, dot(matrix_ref[kind], jnp.concatenate(tile, 0))


def route_kernel(route_ref, in_ref, e_ref, right_ref, left_ref, out_ref, edge_ref):
    for start, rows in passed_on(route_ref, in_ref):
        rows = rows.astype(BF16)
        for plane in range(PLANE):
            out_ref[plane, start : start + TILE] = rows[TILE * plane : TILE * (plane + 1)]
    edge_ref[0:NX, :] = e_ref[...]
    edge_ref[NX : NX + 8, :] = right_ref[24:ENDS, :]
    edge_ref[NX + 8 : NX + 16, :] = left_ref[24:ENDS, :]


def merge_kernel(t_ref, e_ref, right_ref, left_ref, next_ref):
    side_y, side_z = sides()
    tile, base, inner = geometry()
    for i in range(Q):
        next_ref[i] = t_ref[PITCH * i + FIRST : PITCH * i + FIRST + SPAN, :]
    for k in range(9):
        next_ref[18 + k, 0:2] = next_ref[18 + k, 0:2] + right_ref[2 * k : 2 * k + 2, :]
        next_ref[k, SPAN - 2 : SPAN] = next_ref[k, SPAN - 2 : SPAN] + left_ref[2 * k : 2 * k + 2, :]
    rows, lanes = ids((NX, LANES), 0), ids((NX, LANES), 1)
    corner = e_ref[0:NX, :]
    low = jnp.where(rows == 0, e_ref[NX + 7 : NX + 8, :], pltpu.roll(corner, 1, 0))
    high = jnp.where(rows == NX - 1, e_ref[NX + 8 : NX + 9, :], pltpu.roll(corner, NX - 1, 0))
    for a, value in ((0, high), (1, corner), (2, low)):
        index = 9 * a + 6 * side_y + 2 * side_z
        value = rolled(value, (base + inner - a) & 127)
        at = pl.ds(tile, NX, stride=2)
        next_ref[index, at, :] = next_ref[index, at, :] + jnp.where(lanes == base + inner, value, 0.0)


def finish_kernel(
    base_ref, in_ref, last_ref, flag_ref, own_ref, line_ref, share_ref, ghost_ref,
    value_ref, next_hbm, update_hbm,
    update_ref, sems,
):
    del base_ref
    side_y, side_z = sides()
    in_y, in_z = 2 * (1 - side_y), 2 * (1 - side_z)
    copies = []

    def send(source, target):
        copy = pltpu.make_async_copy(source, target, sems.at[len(copies)])
        copy.start()
        copies.append(copy)

    rows = jnp.concatenate([tile for _, tile in passed_on(last_ref, in_ref)], 0)
    share = share_ref[...]
    lane_1 = ids((1, LANES), 1)
    low_centre = jnp.sum(jnp.where(lane_1 == 48, rows[LAST_LOW : LAST_LOW + 1], 0.0), axis=1, keepdims=True)
    high_centre = jnp.sum(jnp.where(lane_1 == 8, rows[LAST_HIGH : LAST_HIGH + 1], 0.0), axis=1, keepdims=True)
    main = rows[0:LOW] + rows[CENTRE : CENTRE + 1] * share[0:LOW]
    low, high, last_low, last_high = (
        rows[row : row + 1] + centre * share[row : row + 1]
        for row, centre in (
            (LOW, low_centre), (HIGH, high_centre), (LAST_LOW, low_centre), (LAST_HIGH, high_centre)
        )
    )
    row, lane_a = ids((32, LANES), 0), ids((32, LANES), 1) >> 3 & 7
    from_low = jnp.where(row - 18 == lane_a, low, 0.0)
    from_low = jnp.where(row == 26, jnp.where(lane_a == 7, last_low, 0.0), from_low)
    from_high = jnp.where(row == lane_a, high, 0.0)
    from_high = jnp.where(row == 8, jnp.where(lane_a == 0, last_high, 0.0), from_high)
    lane_in, lane_out = ids((LANES, LANES), 0), ids((LANES, LANES), 1)
    alike = (lane_in >> 6 == lane_out >> 6) & (lane_in & 7 == lane_out & 7)
    alike = alike.astype(F32).astype(BF16)
    edges = jnp.zeros((2 * 32, LANES), F32)
    for part in split_bf16(jnp.concatenate([from_low, from_high], 0)):
        edges = edges + dot(part, alike)
    column_0 = main[0:Q] + jnp.where(lane_a == 0, edges[0:32], 0.0)[0:Q]
    column_1 = main[Q : 2 * Q] + jnp.where(lane_a == HALF - 1, edges[32:64], 0.0)[0:Q]
    crossed = jnp.broadcast_to(flag_ref[1:2, :], (Q, LANES)) == 1
    for t in range(2):
        here, there = (column_0, column_1) if t == 0 else (column_1, column_0)
        value = jnp.where(crossed, there, here) + own_ref[32 * t : 32 * t + Q, :]
        for i in range(Q):
            update_ref[0, t : t + 1, LANES * i : LANES * (i + 1)] = value[i : i + 1]
    send(update_ref, update_hbm)

    swap = flag_ref[0:1, :] == 1
    lines = line_ref[...]
    scaled = []
    for k in range(9):
        row = RECORDS + k
        first, second = rows[row : row + 1], rows[row + 9 : row + 10]
        scaled.append(lines * jnp.where(swap, second, first))
        scaled.append(lines * jnp.where(swap, first, second))
    scaled = jnp.concatenate(scaled, 0)
    ghost = dot(jnp.concatenate(split_bf16(scaled), 1), ghost_ref[...])
    lanes = ids((NX, LANES), 1)
    outer = lanes >> 4 == 7 * side_y
    for a in range(3):
        for b in range(3):
            k = 3 * a + b
            for h in range(2):
                at = pl.ds(h, NX, stride=2)
                part = ghost[NX * k : NX * (k + 1), LANES * (h + 1) : LANES * (h + 2)]
                value_ref[9 * a + 3 * b + in_z, at, :] = value_ref[9 * a + 3 * b + in_z, at, :] + part
        for c in range(3):
            k = 3 * a + c
            at = pl.ds(side_y, NX, stride=2)
            part = ghost[NX * k : NX * (k + 1), 0:LANES]
            value = value_ref[9 * a + 3 * in_y + c, at, :]
            value_ref[9 * a + 3 * in_y + c, at, :] = jnp.where(outer, part, value)
        send(value_ref.at[pl.ds(9 * a, 9)], next_hbm.at[pl.ds(9 * a, 9)])
    for copy in copies:
        copy.wait()


VMEM = pl.BlockSpec(memory_space=pltpu.VMEM)
HBM = pl.BlockSpec(memory_space=pltpu.HBM)


def call(kernel, name, results, inputs, outputs=None, scratch=(), cost=None, aliases=None, limit=32):
    return pl.pallas_call(
        kernel,
        out_shape=tuple(jax.ShapeDtypeStruct(*result) for result in results),
        in_specs=inputs,
        out_specs=outputs or (VMEM,) * len(results),
        scratch_shapes=scratch,
        input_output_aliases=aliases or {},
        compiler_params=pltpu.CompilerParams(vmem_limit_bytes=limit * 1024 * 1024),
        cost_estimate=cost,
        name=name,
    )


def in_hbm(value):
    return pltpu.with_memory_space_constraint(value, pltpu.HBM)


def swapped(block, bits):
    return lax.ppermute(block, "group", [(i, i ^ bits) for i in range(4)])


def body(populations, solid_mask, relax_rates, coarse_pops, interface_pairs):
    collided, edge_y, edge_z = call(
        collide_kernel,
        "collide",
        [((Q, SPAN, LANES), F32), ((2, NX, LANES), BF16), ((SPAN, LANES), BF16)],
        [HBM] * 3,
        scratch=[
            pltpu.VMEM((Q, SPAN, LANES), F32),
            pltpu.VMEM((SPAN, LANES), jnp.int32),
            pltpu.SMEM((Q,), F32),
            pltpu.SemaphoreType.DMA((6,)),
        ],
    )(
        in_hbm(populations.reshape(Q, SPAN, LANES)),
        in_hbm(solid_mask.reshape(SPAN, LANES)),
        in_hbm(relax_rates),
    )

    edge_z = swapped(edge_z, 2)
    edge_y = swapped(edge_y, 1)
    streamed, edge_yz, pool, share, halves, records, chosen, centre = call(
        stream_kernel,
        "stream",
        [
            ((Q * PITCH, LANES), F32),
            ((NX, LANES), F32),
            ((256, LANES), BF16),
            ((64, LANES), F32),
            ((32, LANES), F32),
            ((64, LANES), F32),
            ((64, POOLED), BF16),
            ((8, LANES), F32),
        ],
        [VMEM, HBM],
        scratch=[pltpu.VMEM((1, 2, Q * LANES), BF16), pltpu.SemaphoreType.DMA(())],
        cost=pl.CostEstimate(flops=10_000_000, bytes_accessed=8_000_000, transcendentals=0),
    )(collided, in_hbm(coarse_pops))

    streamed, right, left, payload, records = call(
        halo_kernel,
        "halo",
        [
            ((Q * PITCH, LANES), F32),
            ((ENDS, LANES), F32),
            ((ENDS, LANES), F32),
            ((PLANE, ROWS, LANES), BF16),
            ((64, LANES), F32),
        ],
        [VMEM] * 10,
        aliases={0: 0},
    )(streamed, edge_z, edge_y, edge_yz, halves, pool, share, records, chosen, centre)

    near = [[PLANE * i + j for j in range(PLANE)] for i in range(PLANE)]
    far = [[PLANE * ((j + TURN) % PLANE) + i for j in range(PLANE)] for i in range(PLANE)]
    payload = lax.all_to_all(payload, "blocks", 0, 0, axis_index_groups=near, tiled=True)
    ring = [(i, (i + 1) % BLOCKS) for i in range(BLOCKS)]
    right = lax.ppermute(right, "blocks", ring)
    left = lax.ppermute(left, "blocks", [(b, a) for a, b in ring])
    ghost, line, own, route, last, flags = call(
        tables_kernel,
        "tables",
        [
            ((256, 384), BF16),
            ((EDGE, LANES), F32),
            ((64, LANES), F32),
            ((3, LANES, LANES), BF16),
            ((3, TILE, LANES), BF16),
            ((8, LANES), jnp.int32),
        ],
        [VMEM] * 2,
        cost=pl.CostEstimate(flops=1_000_000, bytes_accessed=4_000_000, transcendentals=0),
    )(records, interface_pairs)
    payload, edge_yz = call(
        route_kernel,
        "route",
        [((PLANE, ROWS, LANES), BF16), ((NX + 16, LANES), F32)],
        [VMEM] * 5,
    )(route, payload, edge_yz, right, left)
    payload = lax.all_to_all(payload, "blocks", 0, 0, axis_index_groups=far, tiled=True)
    edge_yz = swapped(edge_yz, 3)
    merged = call(
        merge_kernel,
        "merge",
        [((Q, SPAN, LANES), F32)],
        [VMEM] * 4,
        cost=pl.CostEstimate(flops=1_000_000, bytes_accessed=4_000_000, transcendentals=0),
    )(streamed, edge_yz, right, left)[0]
    _, result, update = call(
        finish_kernel,
        "finish",
        [((Q, SPAN, LANES), F32), ((Q, SPAN, LANES), F32), ((1, 2, Q * LANES), F32)],
        [VMEM] * 8,
        (VMEM, HBM, HBM),
        [pltpu.VMEM((1, 2, Q * LANES), F32), pltpu.SemaphoreType.DMA((4,))],
        aliases={0: 0},
    )(merged, payload, last, flags, own, line, share, ghost)
    return result.reshape(1, Q, SPAN * LANES), update


def solution(mesh):
    placed = (
        P("group", None, "blocks"),
        P("group", "blocks"),
        P(),
        P("group", "blocks", None),
        P("group", None),
    )
    return jax.shard_map(
        body,
        mesh=mesh,
        in_specs=placed,
        out_specs=(P("group", None, "blocks"), P("group", "blocks", None)),
        check_vma=False,
    )
```
